256 devices in a mesh: seq: 32 (over x, z), head: 8 (over y, core).
Axes of the slice: x: 4, y: 4, z: 8, core: 2. Of those that a mesh axis runs over, the one named last changes fastest.
Arguments:
- queries: bfloat16 [16384, 4096], P('seq', 'head'), may hold values from -6 to 6
- key_inputs: bfloat16 [16384, 4096], P('seq', 'head'), may hold values from -6 to 6
- value_inputs: bfloat16 [16384, 4096], P('seq', 'head'), may hold values from -6 to 6
- head_scale: float32 [32], P('head'), may hold values from 0.25 to 4
- out_gain: float32 [4096], P('head'), may hold values from 0.5 to 1.5
Outputs:
- layer_out: bfloat16 [16384, 4096], P('seq', 'head')
The draws below stay inside these ranges and needn't reach their ends.
All inputs are finite; a program needn't handle non-finite values.
Results may differ from the reference program's by a relative error of at most 0.008.
Values may be sent and summed in bfloat16 or wider, within the bound.
A program may use at most 64 MiB of HBM per device.

```python
import math
import jax
import jax.numpy as jnp
from jax import lax

HEADS = 32
HEAD_SIZE = 128
BLOCK = 128
LEVELS = 7
TOKENS = 16384
D = 4096


def block_scale(key, extent, shards, smallest, largest):
    loudness, own = 1.0, jax.random.fold_in(key, 6)
    for dim, parts in shards:
        steps = jnp.exp(jax.random.uniform(jax.random.fold_in(own, dim), (parts,), jnp.float32, smallest / len(shards), largest / len(shards)))
        loudness = loudness * jnp.repeat(steps, extent[dim] // parts).reshape([-1 if axis == dim else 1 for axis in range(len(extent))])
    return loudness


def centred(rng, dims, scale, most, shards=(), dtype=jnp.bfloat16):
    entries = scale * jax.random.normal(rng, dims, jnp.float32)
    if shards:
        entries = entries * block_scale(rng, dims, shards, -0.22, 0.18)
    return jnp.clip(entries, -most, most).astype(dtype)


def setup_inputs(seed: int = 0) -> dict:
    keys = jax.random.split(jax.random.key(seed), 6)
    queries = centred(keys[0], (TOKENS, D), 1.0, 6.0, ((0, 32), (1, 8)))
    key_inputs = centred(keys[1], (TOKENS, D), 1.0, 6.0, ((0, 32), (1, 8)))
    value_inputs = centred(keys[2], (TOKENS, D), 1.0, 6.0, ((0, 32), (1, 8)))
    head_scale = jnp.clip(jnp.exp(math.log(4.0) - 2.7725887 * jax.random.uniform(keys[3], (HEADS,), jnp.float32) ** block_scale(keys[3], (HEADS,), ((0, 8),), -0.2, 0.2)), 0.25, 4.0)
    out_gain = jnp.clip(1.0 + 0.1 * jax.random.normal(keys[4], (D,), jnp.float32), 0.5, 1.5)
    return dict(queries=queries, key_inputs=key_inputs, value_inputs=value_inputs, head_scale=head_scale, out_gain=out_gain)


EPSILON = 1e-06

def unit_heads(matrix):
    tensor = matrix.reshape(matrix.shape[0], HEADS, HEAD_SIZE).astype(jnp.float32)
    inverse = lax.rsqrt(lax.optimization_barrier(jnp.mean(tensor * tensor, axis=-1, keepdims=True)) + EPSILON)
    return (tensor * inverse).astype(jnp.bfloat16)

def pooled(column, repeat_factor):
    pair_count = column.shape[0] // repeat_factor
    grouped = column.reshape(pair_count, repeat_factor, HEAD_SIZE).astype(jnp.float32)
    return lax.optimization_barrier(jnp.mean(grouped, axis=1)).astype(jnp.bfloat16)

def level_terms(query_col, key_col, value_col, level_index):
    repeat_factor = 2 ** level_index
    coarse_q = pooled(query_col, repeat_factor)
    coarse_k = pooled(key_col, repeat_factor)
    coarse_v = pooled(value_col, repeat_factor)
    coarse_rows = coarse_q.shape[0]
    block_count = coarse_rows // BLOCK
    edge_pad = ((1, 1), (0, 0), (0, 0))
    query_tiles = coarse_q.reshape(block_count, BLOCK, HEAD_SIZE).astype(jnp.float32)
    key_blocks = jnp.pad(coarse_k.reshape(block_count, BLOCK, HEAD_SIZE), edge_pad)
    value_blocks = jnp.pad(coarse_v.reshape(block_count, BLOCK, HEAD_SIZE), edge_pad)
    numbers = jnp.arange(block_count)
    before_ok = (numbers >= 1)[:, None, None]
    after_ok = (numbers <= block_count - 2)[:, None, None]
    square = (block_count, BLOCK, BLOCK)
    if level_index == 0:
        key_span_rows = jnp.concatenate([key_blocks[:-2], key_blocks[1:-1], key_blocks[2:]], axis=1)
        value_span_rows = jnp.concatenate([value_blocks[:-2], value_blocks[1:-1], value_blocks[2:]], axis=1)
        allowed = jnp.concatenate([jnp.broadcast_to(before_ok, square), jnp.ones(square, jnp.bool_), jnp.broadcast_to(after_ok, square)], axis=2)
    else:
        key_span_rows = jnp.concatenate([key_blocks[:-2], key_blocks[2:]], axis=1)
        value_span_rows = jnp.concatenate([value_blocks[:-2], value_blocks[2:]], axis=1)
        half_rows = BLOCK // 2
        query_half = jnp.arange(BLOCK) // half_rows
        before = query_half[:, None] >= query_half[None, :]
        after = query_half[None, :] >= query_half[:, None]
        allowed = jnp.concatenate([before_ok & before[None], after_ok & after[None]], axis=2)
    attention_logits = jnp.einsum('hzr,hnr->hzn', query_tiles, key_span_rows.astype(jnp.float32)) * HEAD_SIZE ** (-0.5)
    weights = jnp.where(allowed, jnp.exp(attention_logits), 0.0)
    totals = repeat_factor * lax.optimization_barrier(jnp.sum(weights, axis=-1))
    rounded_length = lax.optimization_barrier(weights.astype(jnp.bfloat16))
    mixed_output = repeat_factor * jnp.einsum('gul,glz->guz', rounded_length.astype(jnp.float32), value_span_rows.astype(jnp.float32))
    mixed_output = jnp.repeat(mixed_output.reshape(coarse_rows, HEAD_SIZE), repeat_factor, axis=0)
    totals = jnp.repeat(totals.reshape(coarse_rows), repeat_factor, axis=0)
    return (mixed_output, totals)

def head_attention(columns):
    query_col, key_col, value_col = columns
    numerator = jnp.zeros((query_col.shape[0], HEAD_SIZE), jnp.float32)
    denominator = jnp.zeros((query_col.shape[0],), jnp.float32)
    for level_index in range(LEVELS):
        mixed_output, totals = level_terms(query_col, key_col, value_col, level_index)
        numerator = numerator + mixed_output
        denominator = denominator + totals
    return numerator / denominator[:, None]

def reference(queries, key_inputs, value_inputs, head_scale, out_gain):
    query_unit = unit_heads(queries).transpose(1, 0, 2)
    key_unit = unit_heads(key_inputs).transpose(1, 0, 2)
    value_heads = value_inputs.reshape(TOKENS, HEADS, HEAD_SIZE).transpose(1, 0, 2)
    attended = lax.map(head_attention, (query_unit, key_unit, value_heads))
    scaled = attended * head_scale[:, None, None]
    power = lax.optimization_barrier(jnp.sum(scaled * scaled, axis=(0, 2)))
    factor = lax.rsqrt(power / D + EPSILON)
    normed = (scaled * factor[None, :, None]).transpose(1, 0, 2).reshape(TOKENS, D) * out_gain[None, :]
    return normed.astype(jnp.bfloat16)
```

```python
import jax
import jax.numpy as jnp
from jax import lax
from jax.experimental import pallas as pl
from jax.experimental.pallas import tpu as pltpu
from jax.sharding import PartitionSpec as P

MESH = pl.DeviceIdType.MESH
BF = jnp.bfloat16
F32 = jnp.float32
EPSILON = 1e-06
E = 128
ROWS = 512
HD = 4
WIDTH = HD * E
SCALE = E ** (-0.5)
NX, NZ, NSEQ, NHEAD = 4, 8, 32, 8


def iota(shape, dim):
    return lax.broadcasted_iota(jnp.int32, shape, dim)


def pool_matrix(parts, columns):
    out = []
    for rows, shift, offset, repeat in parts:
        group = iota((rows, columns), 0) // repeat + offset
        inside = (iota((rows, columns), 1) >> shift) == group
        out.append(jnp.where(inside, 0.5**shift, 0.0))
    return jnp.concatenate(out, axis=0).astype(BF)


def dot(a, b):
    return jnp.dot(a, b, preferred_element_type=F32)


def attn(q, k, v, mask=None):
    logits = lax.dot_general(q, k, (((1,), (1,)), ((), ())), preferred_element_type=F32)
    p = jnp.exp(logits * SCALE)
    if mask is not None:
        p = p * mask
    va = jnp.concatenate([v, jnp.ones(v.shape, BF)], axis=1)
    return dot(p.astype(BF), va)


def half_mask(rows, before_on, after_on):
    qh = iota((rows, 256), 0) // 64
    col = iota((rows, 256), 1)
    kh = (col % 128) // 64
    before = jnp.where(kh <= qh, before_on, 0.0)
    after = jnp.where(kh >= qh, after_on, 0.0)
    return jnp.where(col < 128, before, after)


def split(x):
    hi = x.astype(BF).astype(F32)
    return hi, x - hi


def unit(x):
    x = x.astype(F32)
    return (x * lax.rsqrt(jnp.mean(x * x, axis=-1, keepdims=True) + EPSILON)).astype(BF)


def spread(acc, coarse, h, rows):
    base = h * 2 * rows
    for off in range(2):
        at = pl.ds(base + off, rows, stride=2)
        for t in range(2):
            acc[t, at, :] += coarse[t]


def put(acc, start, pair):
    for t in range(2):
        acc[t, pl.ds(start, pair.shape[0]), :] = pair[:, t * E : (t + 1) * E]


def kernel(
    q_ref, k_ref, v_ref, scale_ref, gain_ref, o_ref,
    qu, kv0, q1, kv1, q2, kv2, q3, kv3, small, ra, rb, rc, rd, re,
    rq3, r3, u3, w3, u_own, u_oth, w_own, w_oth, o3,
    acc0, acc1, acc2, acc3, acc4, pw, send, recv, near_recv, pw_send, pw_recv, local,
):
    d = lax.axis_index("seq")
    me = lax.axis_index("head")
    x, z = d // NZ, d % NZ
    s, r = z // 4, z % 4
    g, par = d // 2, d % 2
    left, right = (d + NSEQ - 1) % NSEQ, (d + 1) % NSEQ
    x_with = (x + 2 * s - 1 + NX) % NX
    x_back = (x - (2 * s - 1) + NX) % NX
    x_far = (x + 2) % NX
    pair_before, pair_after = (g + 15) % 16, (g + 1) % 16

    def at(row, col):
        return row * NZ + col

    bar = pltpu.get_barrier_semaphore()

    def signal(seq, head):
        pl.semaphore_signal(bar, inc=1, device_id=(seq, head), device_id_type=MESH)

    for j in range(1, 8):
        signal(at(x, (z + j) % NZ), me)
        signal(d, (me + j) % NHEAD)
    for i in range(8):
        signal(at(x_back, i), me)
    for i in range(4):
        signal(at(x_far, 4 * s + i), me)
    for i in range(2):
        signal(2 * pair_before + i, me)
        signal(2 * pair_after + i, me)

    for h in range(HD):
        c = slice(h * E, (h + 1) * E)
        qu[:, c] = unit(q_ref[:, c])
        kv0[0, 128:640, c] = unit(k_ref[:, c])
    kv0[1, 128:640, :] = v_ref[...]

    wide = pool_matrix(((128, 1, 0, 1), (64, 2, 0, 1), (32, 3, 0, 1)), 256)
    small_q = pool_matrix(((32, 4, 0, 1), (16, 5, 0, 1), (16, 6, 0, 2)), ROWS)
    small_k = pool_matrix(((32, 4, 0, 1), (16, 5, 0, 1), (16, 6, 0, 1)), ROWS)

    sq = dot(small_q, qu[...])
    sk = dot(small_k, kv0[0, 128:640, :])
    sv = dot(small_k, kv0[1, 128:640, :])
    for h in range(HD):
        c = slice(h * E, (h + 1) * E)
        small[h, 0:64] = sq[:, c].astype(BF)
        small[h, 64:96] = sk[0:32, c].astype(BF)
        small[h, 96:128] = sv[0:32, c].astype(BF)
        small[h, 128:144] = sk[32:48, c].astype(BF)
        small[h, 144:160] = sv[32:48, c].astype(BF)
        small[h, 160:176] = jnp.concatenate([sk[48:56, c], sv[48:56, c]], axis=0).astype(BF)
    for chunk in range(2):
        rows = slice(chunk * 256, chunk * 256 + 256)
        shifted = slice(chunk * 256 + 128, chunk * 256 + 384)
        for which, source in enumerate((qu[rows, :], kv0[0, shifted, :], kv0[1, shifted, :])):
            pooled = dot(wide, source).astype(BF)
            if which == 0:
                q1[chunk * 128 : chunk * 128 + 128, :] = pooled[0:128]
                q2[chunk * 64 : chunk * 64 + 64, :] = pooled[128:192]
                for i in range(2):
                    q3[i, chunk * 32 : chunk * 32 + 32, :] = pooled[192:224, i * 256 : i * 256 + 256]
            else:
                t = which - 1
                kv1[t, 128 + chunk * 128 : 256 + chunk * 128, :] = pooled[0:128]
                kv2[t, 128 + chunk * 64 : 192 + chunk * 64, :] = pooled[128:192]
                for i in range(2):
                    kv3[i, t * 64 + chunk * 32 : t * 64 + chunk * 32 + 32, :] = pooled[
                        192:224, i * 256 : i * 256 + 256
                    ]

    pl.semaphore_wait(bar, 30)
    started = []

    def start(src, dst, seq, rsem):
        copy = pltpu.make_async_remote_copy(
            src_ref=src, dst_ref=dst, send_sem=send.at[len(started)], recv_sem=rsem,
            device_id=(seq, me), device_id_type=MESH,
        )
        copy.start()
        started.append(copy)
        return copy

    own_copy = pltpu.make_async_copy(small.at[r, 32:128], ra.at[r], recv.at[0])
    own_copy.start()
    for i in range(4):
        start(small.at[i, 64:176], rc.at[r], at(x_with, 4 * s + i), recv.at[2])
        start(small.at[i, 128:176], rd.at[r], at(x_back, 4 * (1 - s) + i), recv.at[3])
        start(small.at[i, 160:176], re.at[r], at(x_far, 4 * s + i), recv.at[4])
        start(small.at[i, 0:64], rb.at[r], at(x, 4 * (1 - s) + i), recv.at[1])
    for j in range(1, 4):
        i = (r + j) % 4
        start(small.at[i, 32:128], ra.at[r], at(x, 4 * s + i), recv.at[0])
    start(q3.at[1 - par], rq3.at[par], 2 * g + 1 - par, recv.at[5])
    for i in range(2):
        start(kv3.at[i], r3.at[0, par], 2 * pair_after + i, recv.at[6])
        start(kv3.at[i], r3.at[1, par], 2 * pair_before + i, recv.at[6])
    near = []
    for t, (kv, to_right, from_left, to_left, from_right, n) in enumerate((
        (kv2, 128, 0, 192, 320, 64),
        (kv1, 256, 0, 192, 448, 64),
        (kv0, 512, 0, 128, 640, 128),
    )):
        near.append(start(kv.at[:, to_right : to_right + n], kv.at[:, from_left : from_left + n], right, near_recv.at[t]))
        near.append(start(kv.at[:, to_left : to_left + n], kv.at[:, from_right : from_right + n], left, near_recv.at[3 + t]))
    rq3[par] = q3[par]

    def own_level(h, carry):
        c = pl.ds(pl.multiple_of(h * E, E), E)
        for b in range(4):
            lo, hi = max(b - 1, 0), min(b + 2, 4)
            keys = slice(128 + lo * 128, 128 + hi * 128)
            put(acc0, h * ROWS + b * 128, attn(qu[b * 128 : b * 128 + 128, c], kv0[0, keys, c], kv0[1, keys, c]))
        return carry

    lax.fori_loop(0, HD, own_level, 0)

    for n, ref in enumerate((ra, rb, rc, rd, re)):
        pltpu.make_async_copy(ref, ref, recv.at[n]).wait()
    wrap = jnp.where(s == 1, jnp.where(x == 0, 1.0, 0.0), jnp.where(x == NX - 1, 1.0, 0.0))
    a, b, c_, d_, e_ = ra[...], rb[...], rc[...], rd[...], re[...]

    def flat(y):
        return y.reshape(y.shape[0] * y.shape[1], E)

    k4 = jnp.concatenate([flat(a[:, 32:64]), flat(c_[:, 0:32])], axis=0)
    v4 = jnp.concatenate([flat(a[:, 64:96]), flat(c_[:, 32:64])], axis=0)
    qh = iota((128, 256), 0) // 64
    col = iota((128, 256), 1)
    kh = (col % 128) // 64
    sign = 2 * s - 1
    lead = (kh - qh) * sign
    mask4 = jnp.where(
        col < 128, jnp.where(lead >= 0, 1.0, 0.0), jnp.where(lead <= 0, 1.0 - wrap, 0.0)
    )
    out4 = 16.0 * attn(flat(b[:, 0:32]), k4, v4, mask4)

    q5 = jnp.concatenate([flat(a[:, 0:16]), flat(b[:, 32:48])], axis=0)
    k5 = jnp.concatenate([flat(c_[:, 64:80]), flat(d_[:, 0:16])], axis=0)
    v5 = jnp.concatenate([flat(c_[:, 80:96]), flat(d_[:, 16:32])], axis=0)
    mask5 = jnp.where((iota((128, 128), 0) < 64) | (iota((128, 128), 1) >= 64), 1.0 - wrap, 0.0)
    out56 = 32.0 * attn(q5, k5, v5, mask5)

    q6 = jnp.concatenate([flat(a[:, 16:32]), flat(b[:, 48:64])], axis=0)
    tiles = [y.astype(F32) for y in (e_, c_[:, 96:112], d_[:, 32:48])]
    k6 = jnp.concatenate([y[i, 0:8] for y in tiles for i in range(4)], axis=0).astype(BF)
    v6 = jnp.concatenate([y[i, 8:16] for y in tiles for i in range(4)], axis=0).astype(BF)
    mask6 = jnp.where(iota((128, 96), 1) < 32, 1.0, wrap)
    out56 = out56 + 64.0 * attn(q6, k6, v6, mask6)

    lane = iota((16, E), 1)

    def den_tile(pieces):
        tile = jnp.zeros((16, E), F32)
        for n, piece in enumerate(pieces):
            hi, lo = split(piece)
            tile = jnp.where((lane >= 32 * n) & (lane < 32 * n + 16), hi, tile)
            tile = jnp.where((lane >= 32 * n + 16) & (lane < 32 * n + 32), lo, tile)
        return tile.astype(BF)

    for i in range(4):
        mine = out56[i * 16 : i * 16 + 16]
        u_own[i, 0:16] = mine[:, 0:E].astype(BF)
        u_own[i, 16:32] = den_tile([mine[:, E:]])
        other = out56[64 + i * 16 : 64 + i * 16 + 16]
        four = out4[i * 32 : i * 32 + 32]
        u_oth[i, 0:32] = four[:, 0:E].astype(BF)
        u_oth[i, 32:48] = other[:, 0:E].astype(BF)
        u_oth[i, 48:64] = den_tile([other[:, E:], four[0:16, E:], four[16:32, E:]])
    own_return = pltpu.make_async_copy(u_own.at[r], w_own.at[r], recv.at[7])
    own_return.start()
    for j in range(1, 4):
        i = (r + j) % 4
        start(u_own.at[i], w_own.at[r], at(x, 4 * s + i), recv.at[7])
    for i in range(4):
        start(u_oth.at[i], w_oth.at[r], at(x, 4 * (1 - s) + i), recv.at[8])

    pltpu.make_async_remote_copy(
        src_ref=q3.at[0], dst_ref=rq3.at[1 - par], send_sem=send.at[0], recv_sem=recv.at[5],
        device_id=(d ^ 1, me), device_id_type=MESH,
    ).wait_recv()
    pltpu.make_async_copy(r3, r3, recv.at[6]).wait()
    before_on = jnp.where(d >= 1, 1.0, 0.0)
    after_on = jnp.where(d <= NSEQ - 2, 1.0, 0.0)
    pair_before_on = jnp.where(g >= 1, 1.0, 0.0)
    pair_after_on = jnp.where(g <= 14, 1.0, 0.0)
    col192 = iota((64, 192), 1)
    for half in range(2):
        used = ((0, 0), (1, 0), (1, 1)) if half == 0 else ((0, 0), (0, 1), (1, 1))
        cut = 64 if half == 0 else 128
        mask3 = jnp.where(col192 < cut, pair_before_on, pair_after_on)
        for i in range(2):
            lanes = slice(i * E, (i + 1) * E)
            k3 = jnp.concatenate([r3[side, n, 0:64, lanes] for side, n in used], axis=0)
            v3 = jnp.concatenate([r3[side, n, 64:128, lanes] for side, n in used], axis=0)
            o3[half, i] = 8.0 * attn(rq3[half, :, lanes], k3, v3, mask3)
    lane64 = iota((64, E), 1)
    parts = []
    for i in range(2):
        put(acc3, (2 * par + i) * 64, o3[par, i])
        gone = o3[1 - par, i]
        u3[:, i * E : (i + 1) * E] = gone[:, 0:E].astype(BF)
        parts.extend(split(gone[:, E:]))
    dens = jnp.where(
        lane64 < 64, jnp.where(lane64 < 32, parts[0], parts[1]), jnp.where(lane64 < 96, parts[2], parts[3])
    )
    u3[:, 2 * E : 3 * E] = dens.astype(BF)
    back3 = start(u3, w3, 2 * g + 1 - par, recv.at[9])

    for copy in near:
        copy.wait_recv()
    fine = pool_matrix(((64, 1, 0, 1), (32, 2, 0, 1)), 128)
    coarse = pool_matrix(((32, 1, 0, 1),), 64)
    for t in range(2):
        pooled = dot(fine, kv0[t, 0:128, :]).astype(BF)
        kv1[t, 64:128, :] = pooled[0:64]
        kv2[t, 96:128, :] = pooled[64:96]
        kv2[t, 64:96, :] = dot(coarse, kv1[t, 0:64, :]).astype(BF)
        pooled = dot(fine, kv0[t, 640:768, :]).astype(BF)
        kv1[t, 384:448, :] = pooled[0:64]
        kv2[t, 256:288, :] = pooled[64:96]
        kv2[t, 288:320, :] = dot(coarse, kv1[t, 448:512, :]).astype(BF)

    def near_level(h, carry):
        c = pl.ds(pl.multiple_of(h * E, E), E)
        edges = (
            before_on * attn(qu[0:128, c], kv0[0, 0:128, c], kv0[1, 0:128, c]),
            after_on * attn(qu[384:512, c], kv0[0, 640:768, c], kv0[1, 640:768, c]),
        )
        for n, edge in enumerate(edges):
            for t in range(2):
                acc0[t, pl.ds(h * ROWS + 384 * n, 128), :] += edge[:, t * E : (t + 1) * E]
        for b in range(2):
            mask = half_mask(128, before_on if b == 0 else 1.0, after_on if b == 1 else 1.0)
            k = jnp.concatenate(
                [kv1[0, b * 128 : b * 128 + 128, c], kv1[0, 256 + b * 128 : 384 + b * 128, c]], axis=0
            )
            v = jnp.concatenate(
                [kv1[1, b * 128 : b * 128 + 128, c], kv1[1, 256 + b * 128 : 384 + b * 128, c]], axis=0
            )
            put(acc1, h * 256 + b * 128, 2.0 * attn(q1[b * 128 : b * 128 + 128, c], k, v, mask))
        k = jnp.concatenate([kv2[0, 0:128, c], kv2[0, 256:384, c]], axis=0)
        v = jnp.concatenate([kv2[1, 0:128, c], kv2[1, 256:384, c]], axis=0)
        mask = half_mask(128, before_on, after_on)
        put(acc2, h * 128, 4.0 * attn(q2[:, c], k, v, mask))
        return carry

    lax.fori_loop(0, HD, near_level, 0)

    pltpu.make_async_copy(w_own, w_own, recv.at[7]).wait()
    pltpu.make_async_copy(w_oth, w_oth, recv.at[8]).wait()
    back3.wait_recv()

    def den_of(tile, lo, hi, rows):
        return jnp.broadcast_to(tile[:, lo : lo + 1] + tile[:, hi : hi + 1], (rows, E))

    d3 = w3[:, 2 * E : 3 * E].astype(F32)
    for i in range(2):
        here = pl.ds((2 * (1 - par) + i) * 64, 64)
        acc3[0, here, :] = w3[:, i * E : (i + 1) * E].astype(F32)
        acc3[1, here, :] = den_of(d3, 64 * i, 64 * i + 32, 64)
    for h in range(HD):
        own, oth = w_own[h].astype(F32), w_oth[h].astype(F32)
        num = own[0:16] + oth[32:48]
        dt = oth[48:64]
        den = den_of(own[16:32], 0, 16, 16) + den_of(dt, 0, 16, 16)
        acc4[0, h * 32 : h * 32 + 32, :] = oth[0:32]
        acc4[1, h * 32 : h * 32 + 16, :] = den_of(dt, 32, 48, 16)
        acc4[1, h * 32 + 16 : h * 32 + 32, :] = den_of(dt, 64, 80, 16)
        spread(acc4, (num, den), h, 16)
        for acc, finer, n in ((acc4, acc3, 32), (acc3, acc2, 64), (acc2, acc1, 128), (acc1, acc0, 256)):
            spread(finer, tuple(acc[t, h * n : h * n + n, :] for t in range(2)), h, n)

    squares = jnp.zeros((ROWS, E), F32)
    for h in range(HD):
        rows = slice(h * ROWS, (h + 1) * ROWS)
        scaled = acc0[0, rows, :] / acc0[1, rows, :] * scale_ref[h]
        acc0[0, rows, :] = scaled
        squares = squares + scaled * scaled
    for n in range(4):
        turned = squares[n * 128 : n * 128 + 128].T
        pw[me, :, n * 128 : n * 128 + 128] = jnp.sum(turned, axis=0, keepdims=True)
    power = []
    for j in range(1, 8):
        copy = pltpu.make_async_remote_copy(
            src_ref=pw.at[me], dst_ref=pw.at[me], send_sem=pw_send.at[j], recv_sem=pw_recv.at[me],
            device_id=(d, (me + j) % NHEAD), device_id_type=MESH,
        )
        copy.start()
        power.append(copy)
    for j in range(1, 8):
        peer = (me + j) % NHEAD
        pltpu.make_async_remote_copy(
            src_ref=pw.at[peer], dst_ref=pw.at[peer], send_sem=pw_send.at[j], recv_sem=pw_recv.at[peer],
            device_id=(d, peer), device_id_type=MESH,
        ).wait_recv()
    total = jnp.sum(pw[...], axis=0)
    factor = lax.rsqrt(total / (NHEAD * WIDTH) + EPSILON)
    for n in range(4):
        column = jnp.broadcast_to(factor[:, n * 128 : n * 128 + 128], (128, 128)).T
        for h in range(HD):
            c = slice(h * E, (h + 1) * E)
            scaled = acc0[0, h * ROWS + n * 128 : h * ROWS + n * 128 + 128, :]
            o_ref[n * 128 : n * 128 + 128, c] = (scaled * column * gain_ref[:, c]).astype(BF)
    for copy in started:
        copy.wait_send()
    for copy in power:
        copy.wait_send()


def on_device(queries, key_inputs, value_inputs, head_scale, out_gain):
    vmem = pl.BlockSpec(memory_space=pltpu.VMEM)
    return pl.pallas_call(
        kernel,
        out_shape=jax.ShapeDtypeStruct((ROWS, WIDTH), BF),
        in_specs=[vmem, vmem, vmem, pl.BlockSpec(memory_space=pltpu.SMEM), vmem],
        out_specs=vmem,
        scratch_shapes=[
            pltpu.VMEM((512, WIDTH), BF),
            pltpu.VMEM((2, 768, WIDTH), BF),
            pltpu.VMEM((256, WIDTH), BF),
            pltpu.VMEM((2, 512, WIDTH), BF),
            pltpu.VMEM((128, WIDTH), BF),
            pltpu.VMEM((2, 384, WIDTH), BF),
            pltpu.VMEM((2, 64, 256), BF),
            pltpu.VMEM((2, 128, 256), BF),
            pltpu.VMEM((4, 176, E), BF),
            pltpu.VMEM((4, 96, E), BF),
            pltpu.VMEM((4, 64, E), BF),
            pltpu.VMEM((4, 112, E), BF),
            pltpu.VMEM((4, 48, E), BF),
            pltpu.VMEM((4, 16, E), BF),
            pltpu.VMEM((2, 64, 256), BF),
            pltpu.VMEM((2, 2, 128, 256), BF),
            pltpu.VMEM((64, 384), BF),
            pltpu.VMEM((64, 384), BF),
            pltpu.VMEM((4, 32, E), BF),
            pltpu.VMEM((4, 64, E), BF),
            pltpu.VMEM((4, 32, E), BF),
            pltpu.VMEM((4, 64, E), BF),
            pltpu.VMEM((2, 2, 64, 256), F32),
            pltpu.VMEM((2, HD * 512, E), F32),
            pltpu.VMEM((2, HD * 256, E), F32),
            pltpu.VMEM((2, HD * 128, E), F32),
            pltpu.VMEM((2, HD * 64, E), F32),
            pltpu.VMEM((2, HD * 32, E), F32),
            pltpu.VMEM((NHEAD, 1, ROWS), F32),
            pltpu.SemaphoreType.DMA((48,)),
            pltpu.SemaphoreType.DMA((10,)),
            pltpu.SemaphoreType.DMA((6,)),
            pltpu.SemaphoreType.DMA((8,)),
            pltpu.SemaphoreType.DMA((8,)),
            pltpu.SemaphoreType.DMA,
        ],
        compiler_params=pltpu.CompilerParams(
            collective_id=0, has_side_effects=True, vmem_limit_bytes=48 * 2**20
        ),
    )(queries, key_inputs, value_inputs, head_scale, out_gain.reshape(1, WIDTH))


def solution(mesh):
    placed = (P("seq", "head"), P("seq", "head"), P("seq", "head"), P("head"), P("head"))
    return jax.shard_map(
        on_device, mesh=mesh, in_specs=placed, out_specs=P("seq", "head"), check_vma=False
    )
```

```python
import jax
import jax.numpy as jnp
from jax import lax
from jax.experimental import pallas as pl
from jax.experimental.pallas import tpu as pltpu
from jax.sharding import PartitionSpec as P

MESH = pl.DeviceIdType.MESH
BF = jnp.bfloat16
F32 = jnp.float32
EPSILON = 1e-06
E = 128
ROWS = 512
HD = 4
WIDTH = HD * E
SCALE = E ** (-0.5)
NX, NZ, NSEQ, NHEAD = 4, 8, 32, 8


def iota(shape, dim):
    return lax.broadcasted_iota(jnp.int32, shape, dim)


def pool_matrix(parts, columns):
    out = []
    for rows, shift, offset, repeat in parts:
        group = iota((rows, columns), 0) // repeat + offset
        inside = (iota((rows, columns), 1) >> shift) == group
        out.append(jnp.where(inside, 0.5**shift, 0.0))
    return jnp.concatenate(out, axis=0).astype(BF)


def dot(a, b):
    return jnp.dot(a, b, preferred_element_type=F32)


def attn(q, k, v, mask=None):
    logits = lax.dot_general(q, k, (((1,), (1,)), ((), ())), preferred_element_type=F32)
    p = jnp.exp(logits * SCALE)
    if mask is not None:
        p = p * mask
    va = jnp.concatenate([v, jnp.ones(v.shape, BF)], axis=1)
    return dot(p.astype(BF), va)


def half_mask(rows, before_on, after_on):
    qh = iota((rows, 256), 0) // 64
    col = iota((rows, 256), 1)
    kh = (col % 128) // 64
    before = jnp.where(kh <= qh, before_on, 0.0)
    after = jnp.where(kh >= qh, after_on, 0.0)
    return jnp.where(col < 128, before, after)


def split(x):
    hi = x.astype(BF).astype(F32)
    return hi, x - hi


def unit(x):
    x = x.astype(F32)
    return (x * lax.rsqrt(jnp.mean(x * x, axis=-1, keepdims=True) + EPSILON)).astype(BF)


def spread(acc, coarse, h, rows):
    base = h * 2 * rows
    for off in range(2):
        at = pl.ds(base + off, rows, stride=2)
        for t in range(2):
            acc[t, at, :] += coarse[t]


def put(acc, start, pair):
    for t in range(2):
        acc[t, pl.ds(start, pair.shape[0]), :] = pair[:, t * E : (t + 1) * E]


def kernel(
    q_hbm, k_hbm, v_hbm, scale_hbm, gain_hbm, o_ref,
    q_ref, k_ref, scale_ref, gain_ref, qu, kv0, q1, kv1, q2, kv2, q3, kv3, small, ra, rb, rc, rd, re,
    rq3, r3, u3, w3, u_own, u_oth, w_own, w_oth, o3,
    acc0, acc1, acc2, acc3, acc4, pw, send, recv, near_recv, pw_send, pw_recv, load,
):
    d = lax.axis_index("seq")
    me = lax.axis_index("head")
    x, z = d // NZ, d % NZ
    s, r = z // 4, z % 4
    g, par = d // 2, d % 2
    left, right = (d + NSEQ - 1) % NSEQ, (d + 1) % NSEQ
    x_with = (x + 2 * s - 1 + NX) % NX
    x_back = (x - (2 * s - 1) + NX) % NX
    x_far = (x + 2) % NX
    pair_before, pair_after = (g + 15) % 16, (g + 1) % 16

    def at(row, col):
        return row * NZ + col

    loads = [
        pltpu.make_async_copy(src, dst, load.at[n])
        for n, (src, dst) in enumerate((
            (k_hbm, k_ref), (v_hbm, kv0.at[1, 128:640]), (q_hbm, q_ref), (scale_hbm, scale_ref), (gain_hbm, gain_ref)
        ))
    ]
    for copy in loads:
        copy.start()

    bar = pltpu.get_barrier_semaphore()

    def signal(seq, head):
        pl.semaphore_signal(bar, inc=1, device_id=(seq, head), device_id_type=MESH)

    for j in range(1, 8):
        signal(at(x, (z + j) % NZ), me)
        signal(d, (me + j) % NHEAD)
    for i in range(8):
        signal(at(x_back, i), me)
    for i in range(4):
        signal(at(x_far, 4 * s + i), me)
    for i in range(2):
        signal(2 * pair_before + i, me)
        signal(2 * pair_after + i, me)

    lanes_of = [slice(h * E, (h + 1) * E) for h in range(HD)]
    loads[0].wait()
    for c in lanes_of:
        kv0[0, 128:640, c] = unit(k_ref[:, c])
    loads[2].wait()
    for c in lanes_of:
        qu[:, c] = unit(q_ref[:, c])
    for n in (1, 3, 4):
        loads[n].wait()

    wide = pool_matrix(((128, 1, 0, 1), (64, 2, 0, 1), (32, 3, 0, 1)), 256)
    small_q = pool_matrix(((32, 4, 0, 1), (16, 5, 0, 1)), ROWS)
    small_k = pool_matrix(((32, 4, 0, 1), (16, 5, 0, 1), (16, 6, 0, 1)), ROWS)

    sq = dot(small_q, qu[...])
    sk = dot(small_k, kv0[0, 128:640, :])
    sv = dot(small_k, kv0[1, 128:640, :])
    for h, c in enumerate(lanes_of):
        small[h, 0:48] = sq[:, c].astype(BF)
        small[h, 48:80] = sk[0:32, c].astype(BF)
        small[h, 80:112] = sv[0:32, c].astype(BF)
        small[h, 112:128] = sk[32:48, c].astype(BF)
        small[h, 128:144] = sv[32:48, c].astype(BF)
        small[h, 144:160] = jnp.concatenate([sk[48:56, c], sv[48:56, c]], axis=0).astype(BF)
    for chunk in range(2):
        rows = slice(chunk * 256, chunk * 256 + 256)
        shifted = slice(chunk * 256 + 128, chunk * 256 + 384)
        for which, source in enumerate((qu[rows, :], kv0[0, shifted, :], kv0[1, shifted, :])):
            pooled = dot(wide, source).astype(BF)
            if which == 0:
                q1[chunk * 128 : chunk * 128 + 128, :] = pooled[0:128]
                q2[chunk * 64 : chunk * 64 + 64, :] = pooled[128:192]
                for i in range(2):
                    q3[i, chunk * 32 : chunk * 32 + 32, :] = pooled[192:224, i * 256 : i * 256 + 256]
            else:
                t = which - 1
                kv1[t, 128 + chunk * 128 : 256 + chunk * 128, :] = pooled[0:128]
                kv2[t, 128 + chunk * 64 : 192 + chunk * 64, :] = pooled[128:192]
                for i in range(2):
                    kv3[i, t * 64 + chunk * 32 : t * 64 + chunk * 32 + 32, :] = pooled[
                        192:224, i * 256 : i * 256 + 256
                    ]

    pl.semaphore_wait(bar, 30)
    started = []

    def start(src, dst, seq, rsem):
        copy = pltpu.make_async_remote_copy(
            src_ref=src, dst_ref=dst, send_sem=send.at[len(started)], recv_sem=rsem,
            device_id=(seq, me), device_id_type=MESH,
        )
        copy.start()
        started.append(copy)
        return copy

    own_copy = pltpu.make_async_copy(small.at[r, 32:112], ra.at[r], recv.at[0])
    own_copy.start()
    for i in range(4):
        start(small.at[i, 48:112], rc.at[r], at(x_with, 4 * s + i), recv.at[2])
        start(small.at[i, 112:144], rd.at[r], at(x_back, 4 * (1 - s) + i), recv.at[3])
        start(small.at[i, 144:160], re.at[r], at(x_far, 4 * s + i), recv.at[4])
        start(small.at[i, 0:32], rb.at[r], at(x, 4 * (1 - s) + i), recv.at[1])
    for j in range(1, 4):
        i = (r + j) % 4
        start(small.at[i, 32:112], ra.at[r], at(x, 4 * s + i), recv.at[0])
    start(q3.at[1 - par], rq3.at[par], 2 * g + 1 - par, recv.at[5])
    for i in range(2):
        start(kv3.at[i], r3.at[0, par], 2 * pair_after + i, recv.at[6])
        start(kv3.at[i], r3.at[1, par], 2 * pair_before + i, recv.at[6])
    near = []
    for t, (kv, to_right, from_left, to_left, from_right, n) in enumerate((
        (kv0, 512, 0, 128, 640, 128),
        (kv1, 256, 0, 192, 448, 64),
        (kv2, 128, 0, 192, 320, 64),
    )):
        near.append(start(kv.at[:, to_right : to_right + n], kv.at[:, from_left : from_left + n], right, near_recv.at[t]))
        near.append(start(kv.at[:, to_left : to_left + n], kv.at[:, from_right : from_right + n], left, near_recv.at[3 + t]))
    rq3[par] = q3[par]

    def own_level(h, carry):
        c = pl.ds(pl.multiple_of(h * E, E), E)
        for b in range(4):
            lo, hi = max(b - 1, 0), min(b + 2, 4)
            keys = slice(128 + lo * 128, 128 + hi * 128)
            put(acc0, h * ROWS + b * 128, attn(qu[b * 128 : b * 128 + 128, c], kv0[0, keys, c], kv0[1, keys, c]))
        return carry

    lax.fori_loop(0, HD, own_level, 0)

    for n, ref in enumerate((ra, rb, rc, rd, re)):
        pltpu.make_async_copy(ref, ref, recv.at[n]).wait()
    wrap = jnp.where(s == 1, jnp.where(x == 0, 1.0, 0.0), jnp.where(x == NX - 1, 1.0, 0.0))
    a, b, c_, d_, e_ = ra[...], rb[...], rc[...], rd[...], re[...]

    def flat(y):
        return y.reshape(y.shape[0] * y.shape[1], E)

    kv_c = jnp.concatenate([flat(c_[:, 0:32]), flat(c_[:, 32:64])], axis=1)
    kv_d = jnp.concatenate([flat(d_[:, 0:16]), flat(d_[:, 16:32])], axis=1)
    k4 = jnp.concatenate([flat(a[:, 16:48]), kv_c[:, 0:E]], axis=0)
    v4 = jnp.concatenate([flat(a[:, 48:80]), kv_c[:, E:]], axis=0)
    q4, q5 = flat(b), flat(a[:, 0:16])
    pooled_c = dot(pool_matrix(((64, 1, 0, 1), (32, 2, 0, 1)), 128), kv_c).astype(BF)
    pooled_d = dot(pool_matrix(((32, 1, 0, 1),), 64), kv_d).astype(BF)
    q_oth = dot(pool_matrix(((128, 1, 0, 2), (128, 2, 0, 4)), 128), q4).astype(BF)
    q6 = dot(pool_matrix(((64, 1, 0, 2),), 64), q5).astype(BF)
    qh = iota((128, 256), 0) // 64
    col = iota((128, 256), 1)
    kh = (col % 128) // 64
    sign = 2 * s - 1
    lead = (kh - qh) * sign
    mask4 = jnp.where(
        col < 128, jnp.where(lead >= 0, 1.0, 0.0), jnp.where(lead <= 0, 1.0 - wrap, 0.0)
    )
    k5 = jnp.concatenate([pooled_c[0:64, 0:E], kv_d[:, 0:E]], axis=0)
    v5 = jnp.concatenate([pooled_c[0:64, E:], kv_d[:, E:]], axis=0)
    far = e_.astype(F32)
    k6 = jnp.concatenate(
        [jnp.concatenate([far[i, 0:8] for i in range(4)], axis=0).astype(BF), pooled_c[64:96, 0:E], pooled_d[:, 0:E]], axis=0
    )
    v6 = jnp.concatenate(
        [jnp.concatenate([far[i, 8:16] for i in range(4)], axis=0).astype(BF), pooled_c[64:96, E:], pooled_d[:, E:]], axis=0
    )
    mask6 = jnp.where(iota((128, 96), 1) < 32, 1.0, wrap)
    out_own = 32.0 * (1.0 - wrap) * attn(q5, k5, v5) + 64.0 * attn(q6, k6, v6, mask6[0:64])
    out_oth = (
        16.0 * attn(q4, k4, v4, mask4)
        + 32.0 * (1.0 - wrap) * attn(q_oth[0:128], kv_d[:, 0:E], kv_d[:, E:])
        + 64.0 * attn(q_oth[128:256], k6, v6, mask6)
    )

    lane = iota((16, E), 1)

    def den_tile(pieces):
        tile = jnp.zeros((16, E), F32)
        for n, piece in enumerate(pieces):
            hi, lo = split(piece)
            tile = jnp.where((lane >= 32 * n) & (lane < 32 * n + 16), hi, tile)
            tile = jnp.where((lane >= 32 * n + 16) & (lane < 32 * n + 32), lo, tile)
        return tile.astype(BF)

    for i in range(4):
        mine = out_own[i * 16 : i * 16 + 16]
        u_own[i, 0:16] = mine[:, 0:E].astype(BF)
        u_own[i, 16:32] = den_tile([mine[:, E:]])
        other = out_oth[i * 32 : i * 32 + 32]
        u_oth[i, 0:32] = other[:, 0:E].astype(BF)
        u_oth[i, 32:48] = den_tile([other[0:16, E:], other[16:32, E:]])
    own_return = pltpu.make_async_copy(u_own.at[r], w_own.at[r], recv.at[7])
    own_return.start()
    for j in range(1, 4):
        i = (r + j) % 4
        start(u_own.at[i], w_own.at[r], at(x, 4 * s + i), recv.at[7])
    for i in range(4):
        start(u_oth.at[i], w_oth.at[r], at(x, 4 * (1 - s) + i), recv.at[8])

    pltpu.make_async_remote_copy(
        src_ref=q3.at[0], dst_ref=rq3.at[1 - par], send_sem=send.at[0], recv_sem=recv.at[5],
        device_id=(d ^ 1, me), device_id_type=MESH,
    ).wait_recv()
    pltpu.make_async_copy(r3, r3, recv.at[6]).wait()
    before_on = jnp.where(d >= 1, 1.0, 0.0)
    after_on = jnp.where(d <= NSEQ - 2, 1.0, 0.0)
    pair_before_on = jnp.where(g >= 1, 1.0, 0.0)
    pair_after_on = jnp.where(g <= 14, 1.0, 0.0)
    col192 = iota((64, 192), 1)
    for half in range(2):
        used = ((0, 0), (1, 0), (1, 1)) if half == 0 else ((0, 0), (0, 1), (1, 1))
        cut = 64 if half == 0 else 128
        mask3 = jnp.where(col192 < cut, pair_before_on, pair_after_on)
        for i in range(2):
            lanes = slice(i * E, (i + 1) * E)
            k3 = jnp.concatenate([r3[side, n, 0:64, lanes] for side, n in used], axis=0)
            v3 = jnp.concatenate([r3[side, n, 64:128, lanes] for side, n in used], axis=0)
            o3[half, i] = 8.0 * attn(rq3[half, :, lanes], k3, v3, mask3)
    lane64 = iota((64, E), 1)
    parts = []
    for i in range(2):
        put(acc3, (2 * par + i) * 64, o3[par, i])
        gone = o3[1 - par, i]
        u3[:, i * E : (i + 1) * E] = gone[:, 0:E].astype(BF)
        parts.extend(split(gone[:, E:]))
    dens = jnp.where(
        lane64 < 64, jnp.where(lane64 < 32, parts[0], parts[1]), jnp.where(lane64 < 96, parts[2], parts[3])
    )
    u3[:, 2 * E : 3 * E] = dens.astype(BF)
    back3 = start(u3, w3, 2 * g + 1 - par, recv.at[9])

    fine = pool_matrix(((64, 1, 0, 1), (32, 2, 0, 1)), 128)
    coarse = pool_matrix(((32, 1, 0, 1),), 64)
    for copy in near[0:2]:
        copy.wait_recv()

    def edges(h, carry):
        c = pl.ds(pl.multiple_of(h * E, E), E)
        pair = (
            before_on * attn(qu[0:128, c], kv0[0, 0:128, c], kv0[1, 0:128, c]),
            after_on * attn(qu[384:512, c], kv0[0, 640:768, c], kv0[1, 640:768, c]),
        )
        for n, edge in enumerate(pair):
            for t in range(2):
                acc0[t, pl.ds(h * ROWS + 384 * n, 128), :] += edge[:, t * E : (t + 1) * E]
        return carry

    lax.fori_loop(0, HD, edges, 0)
    for t in range(2):
        pooled = dot(fine, kv0[t, 0:128, :]).astype(BF)
        kv1[t, 64:128, :] = pooled[0:64]
        kv2[t, 96:128, :] = pooled[64:96]
        pooled = dot(fine, kv0[t, 640:768, :]).astype(BF)
        kv1[t, 384:448, :] = pooled[0:64]
        kv2[t, 256:288, :] = pooled[64:96]
    for copy in near[2:4]:
        copy.wait_recv()

    def level_1(h, carry):
        c = pl.ds(pl.multiple_of(h * E, E), E)
        for b in range(2):
            mask = half_mask(128, before_on if b == 0 else 1.0, after_on if b == 1 else 1.0)
            k, v = (
                jnp.concatenate(
                    [kv1[t, b * 128 : b * 128 + 128, c], kv1[t, 256 + b * 128 : 384 + b * 128, c]], axis=0
                )
                for t in range(2)
            )
            put(acc1, h * 256 + b * 128, 2.0 * attn(q1[b * 128 : b * 128 + 128, c], k, v, mask))
        return carry

    lax.fori_loop(0, HD, level_1, 0)
    for t in range(2):
        kv2[t, 64:96, :] = dot(coarse, kv1[t, 0:64, :]).astype(BF)
        kv2[t, 288:320, :] = dot(coarse, kv1[t, 448:512, :]).astype(BF)
    for copy in near[4:6]:
        copy.wait_recv()

    def level_2(h, carry):
        c = pl.ds(pl.multiple_of(h * E, E), E)
        k, v = (jnp.concatenate([kv2[t, 0:128, c], kv2[t, 256:384, c]], axis=0) for t in range(2))
        put(acc2, h * 128, 4.0 * attn(q2[:, c], k, v, half_mask(128, before_on, after_on)))
        return carry

    lax.fori_loop(0, HD, level_2, 0)

    pltpu.make_async_copy(w_own, w_own, recv.at[7]).wait()
    pltpu.make_async_copy(w_oth, w_oth, recv.at[8]).wait()
    back3.wait_recv()

    def den_of(tile, lo, hi, rows):
        return jnp.broadcast_to(tile[:, lo : lo + 1] + tile[:, hi : hi + 1], (rows, E))

    d3 = w3[:, 2 * E : 3 * E].astype(F32)
    for i in range(2):
        here = pl.ds((2 * (1 - par) + i) * 64, 64)
        acc3[0, here, :] = w3[:, i * E : (i + 1) * E].astype(F32)
        acc3[1, here, :] = den_of(d3, 64 * i, 64 * i + 32, 64)
    for h in range(HD):
        own, oth = w_own[h].astype(F32), w_oth[h].astype(F32)
        acc4[0, h * 32 : h * 32 + 32, :] = oth[0:32]
        acc4[1, h * 32 : h * 32 + 16, :] = den_of(oth[32:48], 0, 16, 16)
        acc4[1, h * 32 + 16 : h * 32 + 32, :] = den_of(oth[32:48], 32, 48, 16)
        spread(acc4, (own[0:16], den_of(own[16:32], 0, 16, 16)), h, 16)
        for acc, finer, n in ((acc4, acc3, 32), (acc3, acc2, 64), (acc2, acc1, 128), (acc1, acc0, 256)):
            spread(finer, tuple(acc[t, h * n : h * n + n, :] for t in range(2)), h, n)

    squares = jnp.zeros((ROWS, E), F32)
    for h in range(HD):
        rows = slice(h * ROWS, (h + 1) * ROWS)
        scaled = acc0[0, rows, :] / acc0[1, rows, :] * scale_ref[h]
        acc0[0, rows, :] = scaled
        squares = squares + scaled * scaled
    for n in range(4):
        turned = squares[n * 128 : n * 128 + 128].T
        pw[me, :, n * 128 : n * 128 + 128] = jnp.sum(turned, axis=0, keepdims=True)
    power = []
    for j in range(1, 8):
        copy = pltpu.make_async_remote_copy(
            src_ref=pw.at[me], dst_ref=pw.at[me], send_sem=pw_send.at[j], recv_sem=pw_recv.at[me],
            device_id=(d, (me + j) % NHEAD), device_id_type=MESH,
        )
        copy.start()
        power.append(copy)
    for j in range(1, 8):
        peer = (me + j) % NHEAD
        pltpu.make_async_remote_copy(
            src_ref=pw.at[peer], dst_ref=pw.at[peer], send_sem=pw_send.at[j], recv_sem=pw_recv.at[peer],
            device_id=(d, peer), device_id_type=MESH,
        ).wait_recv()
    total = jnp.sum(pw[...], axis=0)
    factor = lax.rsqrt(total / (NHEAD * WIDTH) + EPSILON)
    for n in range(4):
        column = jnp.broadcast_to(factor[:, n * 128 : n * 128 + 128], (128, 128)).T
        for h in range(HD):
            c = slice(h * E, (h + 1) * E)
            scaled = acc0[0, h * ROWS + n * 128 : h * ROWS + n * 128 + 128, :]
            o_ref[n * 128 : n * 128 + 128, c] = (scaled * column * gain_ref[:, c]).astype(BF)
    for copy in started:
        copy.wait_send()
    for copy in power:
        copy.wait_send()


def on_device(queries, key_inputs, value_inputs, head_scale, out_gain):
    vmem = pl.BlockSpec(memory_space=pltpu.VMEM)
    hbm = pl.BlockSpec(memory_space=pltpu.HBM)
    return pl.pallas_call(
        kernel,
        out_shape=jax.ShapeDtypeStruct((ROWS, WIDTH), BF),
        in_specs=[hbm] * 5,
        out_specs=vmem,
        scratch_shapes=[
            pltpu.VMEM((512, WIDTH), BF),
            pltpu.VMEM((512, WIDTH), BF),
            pltpu.SMEM((HD,), F32),
            pltpu.VMEM((1, WIDTH), F32),
            pltpu.VMEM((512, WIDTH), BF),
            pltpu.VMEM((2, 768, WIDTH), BF),
            pltpu.VMEM((256, WIDTH), BF),
            pltpu.VMEM((2, 512, WIDTH), BF),
            pltpu.VMEM((128, WIDTH), BF),
            pltpu.VMEM((2, 384, WIDTH), BF),
            pltpu.VMEM((2, 64, 256), BF),
            pltpu.VMEM((2, 128, 256), BF),
            pltpu.VMEM((4, 160, E), BF),
            pltpu.VMEM((4, 80, E), BF),
            pltpu.VMEM((4, 32, E), BF),
            pltpu.VMEM((4, 64, E), BF),
            pltpu.VMEM((4, 32, E), BF),
            pltpu.VMEM((4, 16, E), BF),
            pltpu.VMEM((2, 64, 256), BF),
            pltpu.VMEM((2, 2, 128, 256), BF),
            pltpu.VMEM((64, 384), BF),
            pltpu.VMEM((64, 384), BF),
            pltpu.VMEM((4, 32, E), BF),
            pltpu.VMEM((4, 48, E), BF),
            pltpu.VMEM((4, 32, E), BF),
            pltpu.VMEM((4, 48, E), BF),
            pltpu.VMEM((2, 2, 64, 256), F32),
            pltpu.VMEM((2, HD * 512, E), F32),
            pltpu.VMEM((2, HD * 256, E), F32),
            pltpu.VMEM((2, HD * 128, E), F32),
            pltpu.VMEM((2, HD * 64, E), F32),
            pltpu.VMEM((2, HD * 32, E), F32),
            pltpu.VMEM((NHEAD, 1, ROWS), F32),
            pltpu.SemaphoreType.DMA((48,)),
            pltpu.SemaphoreType.DMA((10,)),
            pltpu.SemaphoreType.DMA((6,)),
            pltpu.SemaphoreType.DMA((8,)),
            pltpu.SemaphoreType.DMA((8,)),
            pltpu.SemaphoreType.DMA((5,)),
        ],
        compiler_params=pltpu.CompilerParams(
            collective_id=0, has_side_effects=True, vmem_limit_bytes=60 * 2**20
        ),
    )(queries, key_inputs, value_inputs, head_scale, out_gain.reshape(1, WIDTH))


def solution(mesh):
    placed = (P("seq", "head"), P("seq", "head"), P("seq", "head"), P("head"), P("head"))
    return jax.shard_map(
        on_device, mesh=mesh, in_specs=placed, out_specs=P("seq", "head"), check_vma=False
    )
```

```python
import jax
import jax.numpy as jnp
from jax import lax
from jax.experimental import pallas as pl
from jax.experimental.pallas import tpu as pltpu
from jax.sharding import PartitionSpec as P

MESH = pl.DeviceIdType.MESH
BF = jnp.bfloat16
F32 = jnp.float32
EPSILON = 1e-06
E = 128
ROWS = 512
HD = 4
WIDTH = HD * E
SCALE = E ** (-0.5)
NX, NZ, NSEQ, NHEAD = 4, 8, 32, 8


def iota(shape, dim):
    return lax.broadcasted_iota(jnp.int32, shape, dim)


def pool_matrix(parts, columns):
    out = []
    for rows, shift, offset, repeat in parts:
        group = iota((rows, columns), 0) // repeat + offset
        inside = (iota((rows, columns), 1) >> shift) == group
        out.append(jnp.where(inside, 0.5**shift, 0.0))
    return jnp.concatenate(out, axis=0).astype(BF)


def detail_matrix(rows, shift, chunk, columns):
    k = iota((rows, columns), 0)
    group = k % 16
    for bit in range(3 - shift):
        group = group * 2 + (k >> (4 + bit)) % 2
    col = iota((rows, columns), 1) - 128 * chunk
    sign = jnp.where((col >> (shift - 1)) % 2 == 0, 0.5**shift, -(0.5**shift))
    return jnp.where((col >> shift) == group, sign, 0.0)


def rebuild(coarse, detail):
    return jnp.concatenate([coarse + detail, coarse - detail], axis=0)


def dot(a, b):
    return jnp.dot(a, b, preferred_element_type=F32)


def attn(q, k, v, mask=None):
    logits = lax.dot_general(q, k, (((1,), (1,)), ((), ())), preferred_element_type=F32)
    p = jnp.exp(logits * SCALE)
    if mask is not None:
        p = p * mask
    va = jnp.concatenate([v, jnp.ones(v.shape, BF)], axis=1)
    return dot(p.astype(BF), va)


def half_mask(rows, before_on, after_on):
    qh = iota((rows, 256), 0) // 64
    col = iota((rows, 256), 1)
    kh = (col % 128) // 64
    before = jnp.where(kh <= qh, before_on, 0.0)
    after = jnp.where(kh >= qh, after_on, 0.0)
    return jnp.where(col < 128, before, after)


def split(x):
    hi = x.astype(BF).astype(F32)
    return hi, x - hi


def unit(x):
    x = x.astype(F32)
    return (x * lax.rsqrt(jnp.mean(x * x, axis=-1, keepdims=True) + EPSILON)).astype(BF)


def spread(acc, coarse, h, rows):
    base = h * 2 * rows
    for off in range(2):
        at = pl.ds(base + off, rows, stride=2)
        for t in range(2):
            acc[t, at, :] += coarse[t]


def put(acc, start, pair):
    for t in range(2):
        acc[t, pl.ds(start, pair.shape[0]), :] = pair[:, t * E : (t + 1) * E]


def kernel(
    q_hbm, k_hbm, v_hbm, scale_hbm, gain_hbm, o_ref,
    q_ref, k_ref, scale_ref, gain_ref, qu, kv0, q1, kv1, q2, kv2, q3, out_near, in_near, hop2, hop3, small, ra, rb, rc, rd, re,
    u_own, u_oth, w_own, w_oth,
    acc0, acc1, acc2, acc3, acc4, pw, send, recv, near_recv, pw_send, pw_recv, load,
):
    d = lax.axis_index("seq")
    me = lax.axis_index("head")
    x, z = d // NZ, d % NZ
    s, r = z // 4, z % 4
    g, par = d // 2, d % 2
    left, right = (d + NSEQ - 1) % NSEQ, (d + 1) % NSEQ
    x_with = (x + 2 * s - 1 + NX) % NX
    x_back = (x - (2 * s - 1) + NX) % NX
    x_far = (x + 2) % NX

    def at(row, col):
        return row * NZ + col

    loads = [
        pltpu.make_async_copy(src, dst, load.at[n])
        for n, (src, dst) in enumerate((
            (k_hbm, k_ref), (v_hbm, kv0.at[1, 128:640]), (q_hbm, q_ref), (scale_hbm, scale_ref), (gain_hbm, gain_ref)
        ))
    ]
    for copy in loads:
        copy.start()

    bar = pltpu.get_barrier_semaphore()

    def signal(seq, head):
        pl.semaphore_signal(bar, inc=1, device_id=(seq, head), device_id_type=MESH)

    for j in range(1, 8):
        signal(at(x, (z + j) % NZ), me)
        signal(d, (me + j) % NHEAD)
    for i in range(4):
        signal(at(x_back, 4 * s + i), me)
        signal(at(x_with, 4 * s + i), me)
        signal(at(x_far, 4 * s + i), me)
    signal(left, me)
    signal(right, me)

    lanes_of = [slice(h * E, (h + 1) * E) for h in range(HD)]
    loads[0].wait()
    for c in lanes_of:
        kv0[0, 128:640, c] = unit(k_ref[:, c])
    loads[2].wait()
    for c in lanes_of:
        qu[:, c] = unit(q_ref[:, c])
    for n in (1, 3, 4):
        loads[n].wait()

    pools_q = pool_matrix(((128, 1, 0, 1), (64, 2, 0, 1), (32, 3, 0, 1)), 256)
    pools_kv = jnp.concatenate(
        [pool_matrix(((128, 1, 0, 1), (32, 3, 0, 1)), 256)]
        + [detail_matrix(16, 3, c, 256).astype(BF) for c in range(2)]
        + [detail_matrix(32, 2, c, 256).astype(BF) for c in range(2)],
        axis=0,
    )
    finest = detail_matrix(64, 1, 0, 128).astype(BF)
    small_q = pool_matrix(((32, 4, 0, 1), (16, 5, 0, 1)), ROWS)
    small_k = pool_matrix(((32, 4, 0, 1), (16, 5, 0, 1), (16, 6, 0, 1)), ROWS)

    sq = dot(small_q, qu[...])
    sk = dot(small_k, kv0[0, 128:640, :])
    sv = dot(small_k, kv0[1, 128:640, :])
    for h, c in enumerate(lanes_of):
        small[h, 0:48] = sq[:, c].astype(BF)
        small[h, 48:80] = sk[0:32, c].astype(BF)
        small[h, 80:112] = sv[0:32, c].astype(BF)
        small[h, 112:128] = sk[32:48, c].astype(BF)
        small[h, 128:144] = sv[32:48, c].astype(BF)
        small[h, 144:160] = jnp.concatenate([sk[48:56, c], sv[48:56, c]], axis=0).astype(BF)
    for half in range(2):
        rows = slice(half * 256, half * 256 + 256)
        pooled = dot(pools_q, qu[rows, :]).astype(BF)
        q1[half * 128 : half * 128 + 128, :] = pooled[0:128]
        q2[half * 64 : half * 64 + 64, :] = pooled[128:192]
        q3[half * 32 : half * 32 + 32, :] = pooled[192:224]
        for t in range(2):
            pooled = dot(pools_kv, kv0[t, half * 256 + 128 : half * 256 + 384, :]).astype(BF)
            kv1[t, 128 + half * 128 : 256 + half * 128, :] = pooled[0:128]
            out_near[t, half * 32 : half * 32 + 32, :] = pooled[128:160]
            out_near[t, 64 + half * 32 : 96 + half * 32, :] = pooled[160:192]
            out_near[t, 128 + half * 64 : 192 + half * 64, :] = pooled[192:256]
            edge = 128 + half * 384
            finest_rows = dot(finest, kv0[t, edge : edge + 128, :]).astype(BF)
            out_near[t, 256 + half * 64 : 320 + half * 64, :] = finest_rows

    pl.semaphore_wait(bar, 28)
    started = []

    def start(src, dst, seq, rsem):
        copy = pltpu.make_async_remote_copy(
            src_ref=src, dst_ref=dst, send_sem=send.at[len(started)], recv_sem=rsem,
            device_id=(seq, me), device_id_type=MESH,
        )
        copy.start()
        started.append(copy)
        return copy

    near = []

    def send_near(n):
        to_left, to_right = ((0, 0), (64, 64), (128, 192), (256, 320))[n]
        into = slice(64 * n, 64 * n + 64)
        near.append((
            start(out_near.at[:, to_right : to_right + 64], in_near.at[0, :, into], right, near_recv.at[n]),
            start(out_near.at[:, to_left : to_left + 64], in_near.at[1, :, into], left, near_recv.at[4 + n]),
        ))

    def wait_both(copies):
        for copy in copies:
            copy.wait_recv()

    send_near(0)
    own_copy = pltpu.make_async_copy(small.at[r, 32:112], ra.at[r], recv.at[0])
    own_copy.start()
    for i in range(4):
        start(small.at[i, 48:112], rc.at[r], at(x_with, 4 * s + i), recv.at[2])
        start(small.at[i, 112:144], rd.at[r], at(x_back, 4 * s + i), recv.at[3])
        start(small.at[i, 144:160], re.at[r], at(x_far, 4 * s + i), recv.at[4])
        start(small.at[i, 0:32], rb.at[r], at(x, 4 * (1 - s) + i), recv.at[1])
    for j in range(1, 4):
        i = (r + j) % 4
        start(small.at[i, 32:112], ra.at[r], at(x, 4 * s + i), recv.at[0])
    send_near(1)

    def own_level(h, carry):
        c = pl.ds(pl.multiple_of(h * E, E), E)
        for b in range(4):
            lo, hi = max(b - 1, 0), min(b + 2, 4)
            keys = slice(128 + lo * 128, 128 + hi * 128)
            put(acc0, h * ROWS + b * 128, attn(qu[b * 128 : b * 128 + 128, c], kv0[0, keys, c], kv0[1, keys, c]))
        return carry

    lax.fori_loop(0, 2, own_level, 0)
    wait_both(near[0])
    second = (
        start(in_near.at[0, :, 0:64], hop2.at[0], right, near_recv.at[8]),
        start(in_near.at[1, :, 0:64], hop2.at[1], left, near_recv.at[9]),
    )
    send_near(2)
    lax.fori_loop(2, HD, own_level, 0)

    for n, ref in enumerate((ra, rb, rc, rd, re)):
        pltpu.make_async_copy(ref, ref, recv.at[n]).wait()
    wrap = jnp.where(s == 1, jnp.where(x == 0, 1.0, 0.0), jnp.where(x == NX - 1, 1.0, 0.0))
    wrap_d = jnp.where(s == 1, jnp.where(x == NX - 1, 1.0, 0.0), jnp.where(x == 0, 1.0, 0.0))
    a, b, c_, d_, e_ = ra[...], rb[...], rc[...], rd[...], re[...]

    def flat(y):
        return y.reshape(y.shape[0] * y.shape[1], E)

    kv_c = jnp.concatenate([flat(c_[:, 0:32]), flat(c_[:, 32:64])], axis=1)
    kv_d = jnp.concatenate([flat(d_[:, 0:16]), flat(d_[:, 16:32])], axis=1)
    k4 = jnp.concatenate([flat(a[:, 16:48]), kv_c[:, 0:E]], axis=0)
    v4 = jnp.concatenate([flat(a[:, 48:80]), kv_c[:, E:]], axis=0)
    q4, q5 = flat(b), flat(a[:, 0:16])
    pooled_c = dot(pool_matrix(((64, 1, 0, 1), (32, 2, 0, 1)), 128), kv_c).astype(BF)
    pooled_d = dot(pool_matrix(((32, 1, 0, 1),), 64), kv_d).astype(BF)
    q_oth = dot(pool_matrix(((128, 1, 0, 2), (128, 2, 0, 4)), 128), q4).astype(BF)
    q6 = dot(pool_matrix(((64, 1, 0, 2),), 64), q5).astype(BF)
    qh = iota((128, 256), 0) // 64
    col = iota((128, 256), 1)
    kh = (col % 128) // 64
    sign = 2 * s - 1
    lead = (kh - qh) * sign
    mask4 = jnp.where(
        col < 128, jnp.where(lead >= 0, 1.0, 0.0), jnp.where(lead <= 0, 1.0 - wrap, 0.0)
    )
    k5 = jnp.concatenate([pooled_c[0:64, 0:E], kv_d[:, 0:E]], axis=0)
    v5 = jnp.concatenate([pooled_c[0:64, E:], kv_d[:, E:]], axis=0)
    far = e_.astype(F32)
    k6 = jnp.concatenate(
        [jnp.concatenate([far[i, 0:8] for i in range(4)], axis=0).astype(BF), pooled_c[64:96, 0:E], pooled_d[:, 0:E]], axis=0
    )
    v6 = jnp.concatenate(
        [jnp.concatenate([far[i, 8:16] for i in range(4)], axis=0).astype(BF), pooled_c[64:96, E:], pooled_d[:, E:]], axis=0
    )
    col6 = iota((128, 96), 1)
    mask6 = jnp.where(col6 < 32, 1.0, jnp.where(col6 < 64, wrap, wrap_d))
    mask5 = jnp.where(iota((64, 128), 1) < 64, 1.0 - wrap, 1.0 - wrap_d)
    out_own = 32.0 * attn(q5, k5, v5, mask5) + 64.0 * attn(q6, k6, v6, mask6[0:64])
    out_oth = (
        16.0 * attn(q4, k4, v4, mask4)
        + 32.0 * (1.0 - wrap_d) * attn(q_oth[0:128], kv_d[:, 0:E], kv_d[:, E:])
        + 64.0 * attn(q_oth[128:256], k6, v6, mask6)
    )

    lane = iota((16, E), 1)

    def den_tile(pieces):
        tile = jnp.zeros((16, E), F32)
        for n, piece in enumerate(pieces):
            hi, lo = split(piece)
            tile = jnp.where((lane >= 32 * n) & (lane < 32 * n + 16), hi, tile)
            tile = jnp.where((lane >= 32 * n + 16) & (lane < 32 * n + 32), lo, tile)
        return tile.astype(BF)

    for i in range(4):
        mine = out_own[i * 16 : i * 16 + 16]
        u_own[i, 0:16] = mine[:, 0:E].astype(BF)
        u_own[i, 16:32] = den_tile([mine[:, E:]])
        other = out_oth[i * 32 : i * 32 + 32]
        u_oth[i, 0:32] = other[:, 0:E].astype(BF)
        u_oth[i, 32:48] = den_tile([other[0:16, E:], other[16:32, E:]])
    own_return = pltpu.make_async_copy(u_own.at[r], w_own.at[r], recv.at[7])
    own_return.start()
    for j in range(1, 4):
        i = (r + j) % 4
        start(u_own.at[i], w_own.at[r], at(x, 4 * s + i), recv.at[7])
    for i in range(4):
        start(u_oth.at[i], w_oth.at[r], at(x, 4 * (1 - s) + i), recv.at[8])

    before_on = jnp.where(d >= 1, 1.0, 0.0)
    after_on = jnp.where(d <= NSEQ - 2, 1.0, 0.0)
    pair_before_on = jnp.where(g >= 1, 1.0, 0.0)
    pair_after_on = jnp.where(g <= NSEQ // 2 - 2, 1.0, 0.0)
    wait_both(second)
    third = start(hop2.at[par], hop3, 2 * g + 1 - par, near_recv.at[10])
    send_near(3)

    def head_lanes(h):
        return pl.ds(pl.multiple_of(h * E, E), E)

    def rows_of(side, t, n, chunk, rows):
        return in_near[side, t, 64 * n + rows * chunk : 64 * n + rows * chunk + rows, :].astype(F32)

    wait_both(near[1])
    for side in range(2):
        for t in range(2):
            for chunk in range(4):
                coarse = rebuild(rows_of(side, t, 0, chunk, 16), rows_of(side, t, 1, chunk, 16))
                at_row = 256 * side + 32 * chunk
                kv2[t, at_row : at_row + 32, :] = coarse.astype(BF)

    def level_2(h, carry):
        c = head_lanes(h)
        k, v = (jnp.concatenate([kv2[t, 0:128, c], kv2[t, 256:384, c]], axis=0) for t in range(2))
        put(acc2, h * 128, 4.0 * attn(q2[:, c], k, v, half_mask(128, before_on, after_on)))
        return carry

    lax.fori_loop(0, HD, level_2, 0)

    def middle(side, t, n):
        chunk = n + (2 if side == 0 else 0)
        coarse = rebuild(rows_of(side, t, 0, chunk, 16), rows_of(side, t, 1, chunk, 16))
        return rebuild(coarse, rows_of(side, t, 2, n, 32))

    wait_both(near[2])
    for side in range(2):
        for t in range(2):
            for n in range(2):
                at_row = 384 * side + 64 * n
                kv1[t, at_row : at_row + 64, :] = middle(side, t, n).astype(BF)

    def level_1(h, carry):
        c = head_lanes(h)
        for b in range(2):
            mask = half_mask(128, before_on if b == 0 else 1.0, after_on if b == 1 else 1.0)
            k, v = (
                jnp.concatenate(
                    [kv1[t, b * 128 : b * 128 + 128, c], kv1[t, 256 + b * 128 : 384 + b * 128, c]], axis=0
                )
                for t in range(2)
            )
            put(acc1, h * 256 + b * 128, 2.0 * attn(q1[b * 128 : b * 128 + 128, c], k, v, mask))
        return carry

    lax.fori_loop(0, HD, level_1, 0)

    third.wait_recv()
    col192 = iota((64, 192), 1)
    last_on = jnp.where(par == 0, pair_after_on, pair_before_on)
    mask3 = jnp.where(col192 < 64, pair_before_on, jnp.where(col192 < 128, pair_after_on, last_on))

    def level_3(h, carry):
        c = head_lanes(h)
        k, v = (jnp.concatenate([hop2[0, t, :, c], hop2[1, t, :, c], hop3[t, :, c]], axis=0) for t in range(2))
        put(acc3, h * 64, 8.0 * attn(q3[:, c], k, v, mask3))
        return carry

    lax.fori_loop(0, HD, level_3, 0)

    wait_both(near[3])
    for side in range(2):
        for t in range(2):
            fine = rebuild(middle(side, t, 1 - side), in_near[side, t, 192:256, :].astype(F32))
            kv0[t, 640 * side : 640 * side + 128, :] = fine.astype(BF)

    def edges(h, carry):
        c = head_lanes(h)
        pair = (
            before_on * attn(qu[0:128, c], kv0[0, 0:128, c], kv0[1, 0:128, c]),
            after_on * attn(qu[384:512, c], kv0[0, 640:768, c], kv0[1, 640:768, c]),
        )
        for n, edge in enumerate(pair):
            for t in range(2):
                acc0[t, pl.ds(h * ROWS + 384 * n, 128), :] += edge[:, t * E : (t + 1) * E]
        return carry

    lax.fori_loop(0, HD, edges, 0)

    pltpu.make_async_copy(w_own, w_own, recv.at[7]).wait()
    pltpu.make_async_copy(w_oth, w_oth, recv.at[8]).wait()

    def den_of(tile, lo, hi, rows):
        return jnp.broadcast_to(tile[:, lo : lo + 1] + tile[:, hi : hi + 1], (rows, E))

    for h in range(HD):
        own, oth = w_own[h].astype(F32), w_oth[h].astype(F32)
        acc4[0, h * 32 : h * 32 + 32, :] = oth[0:32]
        acc4[1, h * 32 : h * 32 + 16, :] = den_of(oth[32:48], 0, 16, 16)
        acc4[1, h * 32 + 16 : h * 32 + 32, :] = den_of(oth[32:48], 32, 48, 16)
        spread(acc4, (own[0:16], den_of(own[16:32], 0, 16, 16)), h, 16)
        for acc, finer, n in ((acc4, acc3, 32), (acc3, acc2, 64), (acc2, acc1, 128), (acc1, acc0, 256)):
            spread(finer, tuple(acc[t, h * n : h * n + n, :] for t in range(2)), h, n)

    squares = jnp.zeros((ROWS, E), F32)
    for h in range(HD):
        rows = slice(h * ROWS, (h + 1) * ROWS)
        scaled = acc0[0, rows, :] / acc0[1, rows, :] * scale_ref[h]
        acc0[0, rows, :] = scaled
        squares = squares + scaled * scaled
    for n in range(4):
        turned = squares[n * 128 : n * 128 + 128].T
        pw[me, :, n * 128 : n * 128 + 128] = jnp.sum(turned, axis=0, keepdims=True)
    power = []
    for j in (4, 3, 5, 2, 6, 1, 7):
        copy = pltpu.make_async_remote_copy(
            src_ref=pw.at[me], dst_ref=pw.at[me], send_sem=pw_send.at[j], recv_sem=pw_recv.at[me],
            device_id=(d, (me + j) % NHEAD), device_id_type=MESH,
        )
        copy.start()
        power.append(copy)
    for j in range(1, 8):
        peer = (me + j) % NHEAD
        pltpu.make_async_remote_copy(
            src_ref=pw.at[peer], dst_ref=pw.at[peer], send_sem=pw_send.at[j], recv_sem=pw_recv.at[peer],
            device_id=(d, peer), device_id_type=MESH,
        ).wait_recv()
    total = jnp.sum(pw[...], axis=0)
    factor = lax.rsqrt(total / (NHEAD * WIDTH) + EPSILON)
    for n in range(4):
        column = jnp.broadcast_to(factor[:, n * 128 : n * 128 + 128], (128, 128)).T
        for h in range(HD):
            c = slice(h * E, (h + 1) * E)
            scaled = acc0[0, h * ROWS + n * 128 : h * ROWS + n * 128 + 128, :]
            o_ref[n * 128 : n * 128 + 128, c] = (scaled * column * gain_ref[:, c]).astype(BF)
    for copy in started:
        copy.wait_send()
    for copy in power:
        copy.wait_send()


def on_device(queries, key_inputs, value_inputs, head_scale, out_gain):
    vmem = pl.BlockSpec(memory_space=pltpu.VMEM)
    hbm = pl.BlockSpec(memory_space=pltpu.HBM)
    return pl.pallas_call(
        kernel,
        out_shape=jax.ShapeDtypeStruct((ROWS, WIDTH), BF),
        in_specs=[hbm] * 5,
        out_specs=vmem,
        scratch_shapes=[
            pltpu.VMEM((512, WIDTH), BF),
            pltpu.VMEM((512, WIDTH), BF),
            pltpu.SMEM((HD,), F32),
            pltpu.VMEM((1, WIDTH), F32),
            pltpu.VMEM((512, WIDTH), BF),
            pltpu.VMEM((2, 768, WIDTH), BF),
            pltpu.VMEM((256, WIDTH), BF),
            pltpu.VMEM((2, 512, WIDTH), BF),
            pltpu.VMEM((128, WIDTH), BF),
            pltpu.VMEM((2, 384, WIDTH), BF),
            pltpu.VMEM((64, WIDTH), BF),
            pltpu.VMEM((2, 384, WIDTH), BF),
            pltpu.VMEM((2, 2, 256, WIDTH), BF),
            pltpu.VMEM((2, 2, 64, WIDTH), BF),
            pltpu.VMEM((2, 64, WIDTH), BF),
            pltpu.VMEM((4, 160, E), BF),
            pltpu.VMEM((4, 80, E), BF),
            pltpu.VMEM((4, 32, E), BF),
            pltpu.VMEM((4, 64, E), BF),
            pltpu.VMEM((4, 32, E), BF),
            pltpu.VMEM((4, 16, E), BF),
            pltpu.VMEM((4, 32, E), BF),
            pltpu.VMEM((4, 48, E), BF),
            pltpu.VMEM((4, 32, E), BF),
            pltpu.VMEM((4, 48, E), BF),
            pltpu.VMEM((2, HD * 512, E), F32),
            pltpu.VMEM((2, HD * 256, E), F32),
            pltpu.VMEM((2, HD * 128, E), F32),
            pltpu.VMEM((2, HD * 64, E), F32),
            pltpu.VMEM((2, HD * 32, E), F32),
            pltpu.VMEM((NHEAD, 1, ROWS), F32),
            pltpu.SemaphoreType.DMA((40,)),
            pltpu.SemaphoreType.DMA((10,)),
            pltpu.SemaphoreType.DMA((11,)),
            pltpu.SemaphoreType.DMA((8,)),
            pltpu.SemaphoreType.DMA((8,)),
            pltpu.SemaphoreType.DMA((5,)),
        ],
        compiler_params=pltpu.CompilerParams(
            collective_id=0, has_side_effects=True, vmem_limit_bytes=60 * 2**20
        ),
    )(queries, key_inputs, value_inputs, head_scale, out_gain.reshape(1, WIDTH))


def solution(mesh):
    placed = (P("seq", "head"), P("seq", "head"), P("seq", "head"), P("head"), P("head"))
    return jax.shard_map(
        on_device, mesh=mesh, in_specs=placed, out_specs=P("seq", "head"), check_vma=False
    )
```

```python
import jax
import jax.numpy as jnp
from jax import lax
from jax.experimental import pallas as pl
from jax.experimental.pallas import tpu as pltpu
from jax.sharding import PartitionSpec as P

MESH = pl.DeviceIdType.MESH
BF = jnp.bfloat16
F32 = jnp.float32
EPSILON = 1e-06
E = 128
ROWS = 512
HD = 4
WIDTH = HD * E
SCALE = E ** (-0.5)
NX, NZ, NSEQ, NHEAD = 4, 8, 32, 8


def iota(shape, dim):
    return lax.broadcasted_iota(jnp.int32, shape, dim)


def pool_matrix(parts, columns):
    out = []
    for rows, shift, offset, repeat in parts:
        group = iota((rows, columns), 0) // repeat + offset
        inside = (iota((rows, columns), 1) >> shift) == group
        out.append(jnp.where(inside, 0.5**shift, 0.0))
    return jnp.concatenate(out, axis=0).astype(BF)


def detail_matrix(rows, shift, chunk, columns):
    k = iota((rows, columns), 0)
    group = k % 16
    for bit in range(3 - shift):
        group = group * 2 + (k >> (4 + bit)) % 2
    col = iota((rows, columns), 1) - 128 * chunk
    sign = jnp.where((col >> (shift - 1)) % 2 == 0, 0.5**shift, -(0.5**shift))
    return jnp.where((col >> shift) == group, sign, 0.0)


def rebuild(coarse, detail):
    return jnp.concatenate([coarse + detail, coarse - detail], axis=0)


def dot(a, b):
    return jnp.dot(a, b, preferred_element_type=F32)


def attn(q, k, v, mask=None):
    logits = lax.dot_general(q, k, (((1,), (1,)), ((), ())), preferred_element_type=F32)
    p = jnp.exp(logits * SCALE)
    if mask is not None:
        p = p * mask
    va = jnp.concatenate([v, jnp.ones(v.shape, BF)], axis=1)
    return dot(p.astype(BF), va)


def half_mask(rows, before_on, after_on):
    qh = iota((rows, 256), 0) // 64
    col = iota((rows, 256), 1)
    kh = (col % 128) // 64
    before = jnp.where(kh <= qh, before_on, 0.0)
    after = jnp.where(kh >= qh, after_on, 0.0)
    return jnp.where(col < 128, before, after)


def split(x):
    hi = x.astype(BF).astype(F32)
    return hi, x - hi


def unit(x):
    x = x.astype(F32)
    return (x * lax.rsqrt(jnp.mean(x * x, axis=-1, keepdims=True) + EPSILON)).astype(BF)


def spread(acc, coarse, h, rows):
    base = h * 2 * rows
    for off in range(2):
        at = pl.ds(base + off, rows, stride=2)
        for t in range(2):
            acc[t, at, :] += coarse[t]


def put(acc, start, pair):
    for t in range(2):
        acc[t, pl.ds(start, pair.shape[0]), :] = pair[:, t * E : (t + 1) * E]


def kernel(
    q_hbm, k_hbm, v_hbm, scale_hbm, gain_hbm, o_ref,
    q_ref, k_ref, scale_ref, gain_ref, qu, kv0, q1, kv1, q2, kv2, q3, out_near, in_near, hop2, hop3, small, ra, rb, rc, rd, re,
    u_own, u_oth, w_own, w_oth,
    acc0, acc1, acc2, acc3, acc4, pw, send, recv, near_recv, pw_send, pw_recv, load,
):
    d = lax.axis_index("seq")
    me = lax.axis_index("head")
    x, z = d // NZ, d % NZ
    s, r = z // 4, z % 4
    g, par = d // 2, d % 2
    left, right = (d + NSEQ - 1) % NSEQ, (d + 1) % NSEQ
    x_with = (x + 2 * s - 1 + NX) % NX
    x_back = (x - (2 * s - 1) + NX) % NX
    x_far = (x + 2) % NX

    def at(row, col):
        return row * NZ + col

    loads = [
        pltpu.make_async_copy(src, dst, load.at[n])
        for n, (src, dst) in enumerate((
            (k_hbm, k_ref), (v_hbm, kv0.at[1, 128:640]), (q_hbm, q_ref), (scale_hbm, scale_ref), (gain_hbm, gain_ref)
        ))
    ]
    for copy in loads:
        copy.start()

    bar = pltpu.get_barrier_semaphore()

    def signal(seq, head):
        pl.semaphore_signal(bar, inc=1, device_id=(seq, head), device_id_type=MESH)

    for j in range(1, 8):
        signal(at(x, (z + j) % NZ), me)
        signal(d, (me + j) % NHEAD)
    for i in range(4):
        signal(at(x_back, 4 * s + i), me)
        signal(at(x_with, 4 * s + i), me)
        signal(at(x_far, 4 * s + i), me)
    signal(left, me)
    signal(right, me)

    lanes_of = [slice(h * E, (h + 1) * E) for h in range(HD)]
    loads[0].wait()
    for c in lanes_of:
        kv0[0, 128:640, c] = unit(k_ref[:, c])
    loads[1].wait()

    pools_kv = jnp.concatenate(
        [pool_matrix(((128, 1, 0, 1), (32, 3, 0, 1)), 256)]
        + [detail_matrix(16, 3, c, 256).astype(BF) for c in range(2)]
        + [detail_matrix(32, 2, c, 256).astype(BF) for c in range(2)],
        axis=0,
    )
    finest = detail_matrix(64, 1, 0, 128).astype(BF)
    for half in range(2):
        for t in range(2):
            pooled = dot(pools_kv, kv0[t, half * 256 + 128 : half * 256 + 384, :]).astype(BF)
            kv1[t, 128 + half * 128 : 256 + half * 128, :] = pooled[0:128]
            out_near[t, half * 32 : half * 32 + 32, :] = pooled[128:160]
            out_near[t, 64 + half * 32 : 96 + half * 32, :] = pooled[160:192]
            out_near[t, 128 + half * 64 : 192 + half * 64, :] = pooled[192:256]
            edge = 128 + half * 384
            finest_rows = dot(finest, kv0[t, edge : edge + 128, :]).astype(BF)
            out_near[t, 256 + half * 64 : 320 + half * 64, :] = finest_rows

    pl.semaphore_wait(bar, 28)
    started = []

    def start(src, dst, seq, rsem):
        copy = pltpu.make_async_remote_copy(
            src_ref=src, dst_ref=dst, send_sem=send.at[len(started)], recv_sem=rsem,
            device_id=(seq, me), device_id_type=MESH,
        )
        copy.start()
        started.append(copy)
        return copy

    near = []

    def send_near(n):
        to_left, to_right = ((0, 0), (64, 64), (128, 192), (256, 320))[n]
        into = slice(64 * n, 64 * n + 64)
        near.append((
            start(out_near.at[:, to_right : to_right + 64], in_near.at[0, :, into], right, near_recv.at[n]),
            start(out_near.at[:, to_left : to_left + 64], in_near.at[1, :, into], left, near_recv.at[4 + n]),
        ))

    def wait_both(copies):
        for copy in copies:
            copy.wait_recv()

    send_near(0)

    loads[2].wait()
    for c in lanes_of:
        qu[:, c] = unit(q_ref[:, c])
    small_q = pool_matrix(((32, 4, 0, 1), (16, 5, 0, 1)), ROWS)
    small_k = pool_matrix(((32, 4, 0, 1), (16, 5, 0, 1), (16, 6, 0, 1)), ROWS)

    sq = dot(small_q, qu[...])
    sk = dot(small_k, kv0[0, 128:640, :])
    sv = dot(small_k, kv0[1, 128:640, :])
    for h, c in enumerate(lanes_of):
        small[h, 0:48] = sq[:, c].astype(BF)
        small[h, 48:80] = sk[0:32, c].astype(BF)
        small[h, 80:112] = sv[0:32, c].astype(BF)
        small[h, 112:128] = sk[32:48, c].astype(BF)
        small[h, 128:144] = sv[32:48, c].astype(BF)
        small[h, 144:160] = jnp.concatenate([sk[48:56, c], sv[48:56, c]], axis=0).astype(BF)
    own_copy = pltpu.make_async_copy(small.at[r, 32:112], ra.at[r], recv.at[0])
    own_copy.start()
    for i in range(4):
        start(small.at[i, 48:112], rc.at[r], at(x_with, 4 * s + i), recv.at[2])
        start(small.at[i, 112:144], rd.at[r], at(x_back, 4 * s + i), recv.at[3])
        start(small.at[i, 144:160], re.at[r], at(x_far, 4 * s + i), recv.at[4])
        start(small.at[i, 0:32], rb.at[r], at(x, 4 * (1 - s) + i), recv.at[1])
    for j in range(1, 4):
        i = (r + j) % 4
        start(small.at[i, 32:112], ra.at[r], at(x, 4 * s + i), recv.at[0])
    send_near(1)
    pools_q = pool_matrix(((128, 1, 0, 1), (64, 2, 0, 1), (32, 3, 0, 1)), 256)
    for half in range(2):
        pooled = dot(pools_q, qu[half * 256 : half * 256 + 256, :]).astype(BF)
        q1[half * 128 : half * 128 + 128, :] = pooled[0:128]
        q2[half * 64 : half * 64 + 64, :] = pooled[128:192]
        q3[half * 32 : half * 32 + 32, :] = pooled[192:224]
    for n in (3, 4):
        loads[n].wait()

    def own_level(h, carry):
        c = pl.ds(pl.multiple_of(h * E, E), E)
        for b in range(4):
            lo, hi = max(b - 1, 0), min(b + 2, 4)
            keys = slice(128 + lo * 128, 128 + hi * 128)
            put(acc0, h * ROWS + b * 128, attn(qu[b * 128 : b * 128 + 128, c], kv0[0, keys, c], kv0[1, keys, c]))
        return carry

    lax.fori_loop(0, 2, own_level, 0)
    wait_both(near[0])
    second = (
        start(in_near.at[0, :, 0:64], hop2.at[0], right, near_recv.at[8]),
        start(in_near.at[1, :, 0:64], hop2.at[1], left, near_recv.at[9]),
    )
    send_near(2)
    lax.fori_loop(2, HD, own_level, 0)

    for n, ref in enumerate((ra, rb, rc, rd, re)):
        pltpu.make_async_copy(ref, ref, recv.at[n]).wait()
    wrap = jnp.where(s == 1, jnp.where(x == 0, 1.0, 0.0), jnp.where(x == NX - 1, 1.0, 0.0))
    wrap_d = jnp.where(s == 1, jnp.where(x == NX - 1, 1.0, 0.0), jnp.where(x == 0, 1.0, 0.0))
    a, b, c_, d_, e_ = ra[...], rb[...], rc[...], rd[...], re[...]

    def flat(y):
        return y.reshape(y.shape[0] * y.shape[1], E)

    kv_c = jnp.concatenate([flat(c_[:, 0:32]), flat(c_[:, 32:64])], axis=1)
    kv_d = jnp.concatenate([flat(d_[:, 0:16]), flat(d_[:, 16:32])], axis=1)
    k4 = jnp.concatenate([flat(a[:, 16:48]), kv_c[:, 0:E]], axis=0)
    v4 = jnp.concatenate([flat(a[:, 48:80]), kv_c[:, E:]], axis=0)
    q4, q5 = flat(b), flat(a[:, 0:16])
    pooled_c = dot(pool_matrix(((64, 1, 0, 1), (32, 2, 0, 1)), 128), kv_c).astype(BF)
    pooled_d = dot(pool_matrix(((32, 1, 0, 1),), 64), kv_d).astype(BF)
    q_oth = dot(pool_matrix(((128, 1, 0, 2), (128, 2, 0, 4)), 128), q4).astype(BF)
    q6 = dot(pool_matrix(((64, 1, 0, 2),), 64), q5).astype(BF)
    qh = iota((128, 256), 0) // 64
    col = iota((128, 256), 1)
    kh = (col % 128) // 64
    sign = 2 * s - 1
    lead = (kh - qh) * sign
    mask4 = jnp.where(
        col < 128, jnp.where(lead >= 0, 1.0, 0.0), jnp.where(lead <= 0, 1.0 - wrap, 0.0)
    )
    k5 = jnp.concatenate([pooled_c[0:64, 0:E], kv_d[:, 0:E]], axis=0)
    v5 = jnp.concatenate([pooled_c[0:64, E:], kv_d[:, E:]], axis=0)
    far = e_.astype(F32)
    k6 = jnp.concatenate(
        [jnp.concatenate([far[i, 0:8] for i in range(4)], axis=0).astype(BF), pooled_c[64:96, 0:E], pooled_d[:, 0:E]], axis=0
    )
    v6 = jnp.concatenate(
        [jnp.concatenate([far[i, 8:16] for i in range(4)], axis=0).astype(BF), pooled_c[64:96, E:], pooled_d[:, E:]], axis=0
    )
    col6 = iota((128, 96), 1)
    mask6 = jnp.where(col6 < 32, 1.0, jnp.where(col6 < 64, wrap, wrap_d))
    mask5 = jnp.where(iota((64, 128), 1) < 64, 1.0 - wrap, 1.0 - wrap_d)
    out_own = 32.0 * attn(q5, k5, v5, mask5) + 64.0 * attn(q6, k6, v6, mask6[0:64])
    out_oth = (
        16.0 * attn(q4, k4, v4, mask4)
        + 32.0 * (1.0 - wrap_d) * attn(q_oth[0:128], kv_d[:, 0:E], kv_d[:, E:])
        + 64.0 * attn(q_oth[128:256], k6, v6, mask6)
    )

    lane = iota((16, E), 1)

    def den_tile(pieces):
        tile = jnp.zeros((16, E), F32)
        for n, piece in enumerate(pieces):
            hi, lo = split(piece)
            tile = jnp.where((lane >= 32 * n) & (lane < 32 * n + 16), hi, tile)
            tile = jnp.where((lane >= 32 * n + 16) & (lane < 32 * n + 32), lo, tile)
        return tile.astype(BF)

    for i in range(4):
        mine = out_own[i * 16 : i * 16 + 16]
        u_own[i, 0:16] = mine[:, 0:E].astype(BF)
        u_own[i, 16:32] = den_tile([mine[:, E:]])
        other = out_oth[i * 32 : i * 32 + 32]
        u_oth[i, 0:32] = other[:, 0:E].astype(BF)
        u_oth[i, 32:48] = den_tile([other[0:16, E:], other[16:32, E:]])
    own_return = pltpu.make_async_copy(u_own.at[r], w_own.at[r], recv.at[7])
    own_return.start()
    for j in range(1, 4):
        i = (r + j) % 4
        start(u_own.at[i], w_own.at[r], at(x, 4 * s + i), recv.at[7])
    for i in range(4):
        start(u_oth.at[i], w_oth.at[r], at(x, 4 * (1 - s) + i), recv.at[8])

    before_on = jnp.where(d >= 1, 1.0, 0.0)
    after_on = jnp.where(d <= NSEQ - 2, 1.0, 0.0)
    pair_before_on = jnp.where(g >= 1, 1.0, 0.0)
    pair_after_on = jnp.where(g <= NSEQ // 2 - 2, 1.0, 0.0)
    wait_both(second)
    third = start(hop2.at[par], hop3, 2 * g + 1 - par, near_recv.at[10])
    send_near(3)

    def head_lanes(h):
        return pl.ds(pl.multiple_of(h * E, E), E)

    def rows_of(side, t, n, chunk, rows):
        return in_near[side, t, 64 * n + rows * chunk : 64 * n + rows * chunk + rows, :].astype(F32)

    wait_both(near[1])
    for side in range(2):
        for t in range(2):
            for chunk in range(4):
                coarse = rebuild(rows_of(side, t, 0, chunk, 16), rows_of(side, t, 1, chunk, 16))
                at_row = 256 * side + 32 * chunk
                kv2[t, at_row : at_row + 32, :] = coarse.astype(BF)

    def level_2(h, carry):
        c = head_lanes(h)
        k, v = (jnp.concatenate([kv2[t, 0:128, c], kv2[t, 256:384, c]], axis=0) for t in range(2))
        put(acc2, h * 128, 4.0 * attn(q2[:, c], k, v, half_mask(128, before_on, after_on)))
        return carry

    lax.fori_loop(0, HD, level_2, 0)

    def middle(side, t, n):
        chunk = n + (2 if side == 0 else 0)
        coarse = rebuild(rows_of(side, t, 0, chunk, 16), rows_of(side, t, 1, chunk, 16))
        return rebuild(coarse, rows_of(side, t, 2, n, 32))

    wait_both(near[2])
    for side in range(2):
        for t in range(2):
            for n in range(2):
                at_row = 384 * side + 64 * n
                kv1[t, at_row : at_row + 64, :] = middle(side, t, n).astype(BF)

    def level_1(h, carry):
        c = head_lanes(h)
        for b in range(2):
            mask = half_mask(128, before_on if b == 0 else 1.0, after_on if b == 1 else 1.0)
            k, v = (
                jnp.concatenate(
                    [kv1[t, b * 128 : b * 128 + 128, c], kv1[t, 256 + b * 128 : 384 + b * 128, c]], axis=0
                )
                for t in range(2)
            )
            put(acc1, h * 256 + b * 128, 2.0 * attn(q1[b * 128 : b * 128 + 128, c], k, v, mask))
        return carry

    lax.fori_loop(0, HD, level_1, 0)

    third.wait_recv()
    col192 = iota((64, 192), 1)
    last_on = jnp.where(par == 0, pair_after_on, pair_before_on)
    mask3 = jnp.where(col192 < 64, pair_before_on, jnp.where(col192 < 128, pair_after_on, last_on))

    def level_3(h, carry):
        c = head_lanes(h)
        k, v = (jnp.concatenate([hop2[0, t, :, c], hop2[1, t, :, c], hop3[t, :, c]], axis=0) for t in range(2))
        put(acc3, h * 64, 8.0 * attn(q3[:, c], k, v, mask3))
        return carry

    lax.fori_loop(0, HD, level_3, 0)

    pltpu.make_async_copy(w_own, w_own, recv.at[7]).wait()
    pltpu.make_async_copy(w_oth, w_oth, recv.at[8]).wait()

    def den_of(tile, lo, hi, rows):
        return jnp.broadcast_to(tile[:, lo : lo + 1] + tile[:, hi : hi + 1], (rows, E))

    for h in range(HD):
        own, oth = w_own[h].astype(F32), w_oth[h].astype(F32)
        acc4[0, h * 32 : h * 32 + 32, :] = oth[0:32]
        acc4[1, h * 32 : h * 32 + 16, :] = den_of(oth[32:48], 0, 16, 16)
        acc4[1, h * 32 + 16 : h * 32 + 32, :] = den_of(oth[32:48], 32, 48, 16)
        spread(acc4, (own[0:16], den_of(own[16:32], 0, 16, 16)), h, 16)
        for acc, finer, n in ((acc4, acc3, 32), (acc3, acc2, 64), (acc2, acc1, 128), (acc1, acc0, 256)):
            spread(finer, tuple(acc[t, h * n : h * n + n, :] for t in range(2)), h, n)

    power = []

    def share_power(part, starts):
        for n, first in enumerate(starts):
            squares = jnp.zeros((128, E), F32)
            for h in range(HD):
                rows = slice(h * ROWS + first, h * ROWS + first + 128)
                scaled = acc0[0, rows, :] / acc0[1, rows, :] * scale_ref[h]
                acc0[0, rows, :] = scaled
                squares = squares + scaled * scaled
            pw[part, me, :, n * 128 : n * 128 + 128] = jnp.sum(squares.T, axis=0, keepdims=True)
        for j in (4, 3, 5, 2, 6, 1, 7):
            copy = pltpu.make_async_remote_copy(
                src_ref=pw.at[part, me], dst_ref=pw.at[part, me],
                send_sem=pw_send.at[part, j], recv_sem=pw_recv.at[part, me],
                device_id=(d, (me + j) % NHEAD), device_id_type=MESH,
            )
            copy.start()
            power.append(copy)

    def write_out(part, starts):
        for j in range(1, 8):
            peer = (me + j) % NHEAD
            pltpu.make_async_remote_copy(
                src_ref=pw.at[part, peer], dst_ref=pw.at[part, peer],
                send_sem=pw_send.at[part, j], recv_sem=pw_recv.at[part, peer],
                device_id=(d, peer), device_id_type=MESH,
            ).wait_recv()
        total = jnp.sum(pw[part], axis=0)
        factor = lax.rsqrt(total / (NHEAD * WIDTH) + EPSILON)
        for n, first in enumerate(starts):
            column = jnp.broadcast_to(factor[:, n * 128 : n * 128 + 128], (128, 128)).T
            for h, c in enumerate(lanes_of):
                scaled = acc0[0, h * ROWS + first : h * ROWS + first + 128, :]
                o_ref[first : first + 128, c] = (scaled * column * gain_ref[:, c]).astype(BF)

    share_power(0, (128, 256))

    wait_both(near[3])
    for side in range(2):
        for t in range(2):
            fine = rebuild(middle(side, t, 1 - side), in_near[side, t, 192:256, :].astype(F32))
            kv0[t, 640 * side : 640 * side + 128, :] = fine.astype(BF)

    def edges(h, carry):
        c = head_lanes(h)
        pair = (
            before_on * attn(qu[0:128, c], kv0[0, 0:128, c], kv0[1, 0:128, c]),
            after_on * attn(qu[384:512, c], kv0[0, 640:768, c], kv0[1, 640:768, c]),
        )
        for n, edge in enumerate(pair):
            for t in range(2):
                acc0[t, pl.ds(h * ROWS + 384 * n, 128), :] += edge[:, t * E : (t + 1) * E]
        return carry

    lax.fori_loop(0, HD, edges, 0)
    share_power(1, (0, 384))
    write_out(0, (128, 256))
    write_out(1, (0, 384))
    for copy in started:
        copy.wait_send()
    for copy in power:
        copy.wait_send()


def on_device(queries, key_inputs, value_inputs, head_scale, out_gain):
    vmem = pl.BlockSpec(memory_space=pltpu.VMEM)
    hbm = pl.BlockSpec(memory_space=pltpu.HBM)
    return pl.pallas_call(
        kernel,
        out_shape=jax.ShapeDtypeStruct((ROWS, WIDTH), BF),
        in_specs=[hbm] * 5,
        out_specs=vmem,
        scratch_shapes=[
            pltpu.VMEM((512, WIDTH), BF),
            pltpu.VMEM((512, WIDTH), BF),
            pltpu.SMEM((HD,), F32),
            pltpu.VMEM((1, WIDTH), F32),
            pltpu.VMEM((512, WIDTH), BF),
            pltpu.VMEM((2, 768, WIDTH), BF),
            pltpu.VMEM((256, WIDTH), BF),
            pltpu.VMEM((2, 512, WIDTH), BF),
            pltpu.VMEM((128, WIDTH), BF),
            pltpu.VMEM((2, 384, WIDTH), BF),
            pltpu.VMEM((64, WIDTH), BF),
            pltpu.VMEM((2, 384, WIDTH), BF),
            pltpu.VMEM((2, 2, 256, WIDTH), BF),
            pltpu.VMEM((2, 2, 64, WIDTH), BF),
            pltpu.VMEM((2, 64, WIDTH), BF),
            pltpu.VMEM((4, 160, E), BF),
            pltpu.VMEM((4, 80, E), BF),
            pltpu.VMEM((4, 32, E), BF),
            pltpu.VMEM((4, 64, E), BF),
            pltpu.VMEM((4, 32, E), BF),
            pltpu.VMEM((4, 16, E), BF),
            pltpu.VMEM((4, 32, E), BF),
            pltpu.VMEM((4, 48, E), BF),
            pltpu.VMEM((4, 32, E), BF),
            pltpu.VMEM((4, 48, E), BF),
            pltpu.VMEM((2, HD * 512, E), F32),
            pltpu.VMEM((2, HD * 256, E), F32),
            pltpu.VMEM((2, HD * 128, E), F32),
            pltpu.VMEM((2, HD * 64, E), F32),
            pltpu.VMEM((2, HD * 32, E), F32),
            pltpu.VMEM((2, NHEAD, 1, ROWS // 2), F32),
            pltpu.SemaphoreType.DMA((40,)),
            pltpu.SemaphoreType.DMA((10,)),
            pltpu.SemaphoreType.DMA((11,)),
            pltpu.SemaphoreType.DMA((2, 8)),
            pltpu.SemaphoreType.DMA((2, 8)),
            pltpu.SemaphoreType.DMA((5,)),
        ],
        compiler_params=pltpu.CompilerParams(
            collective_id=0, has_side_effects=True, vmem_limit_bytes=int(53.25 * 2**20)
        ),
    )(queries, key_inputs, value_inputs, head_scale, out_gain.reshape(1, WIDTH))


def solution(mesh):
    placed = (P("seq", "head"), P("seq", "head"), P("seq", "head"), P("head"), P("head"))
    return jax.shard_map(
        on_device, mesh=mesh, in_specs=placed, out_specs=P("seq", "head"), check_vma=False
    )
```

```python
import math

import jax
import jax.numpy as jnp
from jax import lax
from jax.experimental import pallas as pl
from jax.experimental.pallas import tpu as pltpu
from jax.sharding import PartitionSpec as P

MESH = pl.DeviceIdType.MESH
BF = jnp.bfloat16
F32 = jnp.float32
EPSILON = 1e-06
E = 128
ROWS = 512
HD = 4
WIDTH = HD * E
SCALE = E ** (-0.5) * math.log2(math.e)
NX, NZ, NSEQ, NHEAD = 4, 8, 32, 8


def iota(shape, dim):
    return lax.broadcasted_iota(jnp.int32, shape, dim)


def pool_matrix(parts, columns):
    out = []
    for rows, shift, offset, repeat in parts:
        group = iota((rows, columns), 0) // repeat + offset
        inside = (iota((rows, columns), 1) >> shift) == group
        out.append(jnp.where(inside, 0.5**shift, 0.0))
    return jnp.concatenate(out, axis=0).astype(BF)


def detail_matrix(rows, shift, chunk, columns):
    k = iota((rows, columns), 0)
    group = k % 16
    for bit in range(3 - shift):
        group = group * 2 + (k >> (4 + bit)) % 2
    col = iota((rows, columns), 1) - 128 * chunk
    sign = jnp.where((col >> (shift - 1)) % 2 == 0, 0.5**shift, -(0.5**shift))
    return jnp.where((col >> shift) == group, sign, 0.0)


def rebuild(coarse, detail):
    return jnp.concatenate([coarse + detail, coarse - detail], axis=0)


def dot(a, b):
    return jnp.dot(a, b, preferred_element_type=F32)


def attn_all(jobs):
    logits = [
        lax.dot_general(q, k, (((1,), (1,)), ((), ())), preferred_element_type=F32) for q, k, v, mask in jobs
    ]
    weights = [jnp.exp2(x * SCALE) for x in logits]
    weights = [(p if job[3] is None else p * job[3]).astype(BF) for p, job in zip(weights, jobs)]
    return [dot(p, jnp.concatenate([job[2], jnp.ones(job[2].shape, BF)], axis=1)) for p, job in zip(weights, jobs)]


def attn(q, k, v, mask=None):
    return attn_all([(q, k, v, mask)])[0]


def half_mask(rows, before_on, after_on):
    qh = iota((rows, 256), 0) // 64
    col = iota((rows, 256), 1)
    kh = (col % 128) // 64
    before = jnp.where(kh <= qh, before_on, 0.0)
    after = jnp.where(kh >= qh, after_on, 0.0)
    return jnp.where(col < 128, before, after)


def split(x):
    hi = x.astype(BF).astype(F32)
    return hi, x - hi


def unit(x):
    x = x.astype(F32)
    return (x * lax.rsqrt(jnp.mean(x * x, axis=-1, keepdims=True) + EPSILON)).astype(BF)


def spread(acc, coarse, h, rows):
    base = h * 2 * rows
    for off in range(2):
        at = pl.ds(base + off, rows, stride=2)
        for t in range(2):
            acc[t, at, :] += coarse[t]


def put(acc, start, pair):
    for t in range(2):
        acc[t, pl.ds(start, pair.shape[0]), :] = pair[:, t * E : (t + 1) * E]


def kernel(
    q_hbm, k_hbm, v_hbm, scale_hbm, gain_hbm, o_ref,
    q_ref, k_ref, scale_ref, gain_ref, qu, kv0, q1, kv1, q2, kv2, q3, out_near, in_near, hop2, hop3, small, ra, rb, rc, rd, re,
    u_own, u_oth, w_own, w_oth,
    acc0, acc1, acc2, acc3, acc4, pw, send, recv, near_recv, pw_send, pw_recv, load,
):
    d = lax.axis_index("seq")
    me = lax.axis_index("head")
    x, z = d // NZ, d % NZ
    s, r = z // 4, z % 4
    g, par = d // 2, d % 2
    left, right = (d + NSEQ - 1) % NSEQ, (d + 1) % NSEQ
    x_with = (x + 2 * s - 1 + NX) % NX
    x_back = (x - (2 * s - 1) + NX) % NX
    x_far = (x + 2) % NX

    def at(row, col):
        return row * NZ + col

    bar = pltpu.get_barrier_semaphore()

    def signal(seq, head):
        pl.semaphore_signal(bar, inc=1, device_id=(seq, head), device_id_type=MESH)

    for j in range(1, 8):
        signal(at(x, (z + j) % NZ), me)
        signal(d, (me + j) % NHEAD)
    for i in range(4):
        signal(at(x_back, 4 * s + i), me)
        signal(at(x_with, 4 * s + i), me)
        signal(at(x_far, 4 * s + i), me)
    signal(left, me)
    signal(right, me)

    loads = [
        pltpu.make_async_copy(src, dst, load.at[n])
        for n, (src, dst) in enumerate((
            (k_hbm, k_ref), (v_hbm, kv0.at[1, 128:640]), (q_hbm, q_ref), (scale_hbm, scale_ref), (gain_hbm, gain_ref)
        ))
    ]
    for copy in loads:
        copy.start()

    lanes_of = [slice(h * E, (h + 1) * E) for h in range(HD)]
    loads[0].wait()
    for c in lanes_of:
        kv0[0, 128:640, c] = unit(k_ref[:, c])
    loads[1].wait()

    pools_kv = jnp.concatenate(
        [pool_matrix(((128, 1, 0, 1), (32, 3, 0, 1)), 256)]
        + [detail_matrix(16, 3, c, 256).astype(BF) for c in range(2)]
        + [detail_matrix(32, 2, c, 256).astype(BF) for c in range(2)],
        axis=0,
    )
    finest = detail_matrix(64, 1, 0, 128).astype(BF)
    for half in range(2):
        for t in range(2):
            pooled = dot(pools_kv, kv0[t, half * 256 + 128 : half * 256 + 384, :]).astype(BF)
            kv1[t, 128 + half * 128 : 256 + half * 128, :] = pooled[0:128]
            out_near[t, half * 32 : half * 32 + 32, :] = pooled[128:160]
            out_near[t, 64 + half * 32 : 96 + half * 32, :] = pooled[160:192]
            out_near[t, 128 + half * 64 : 192 + half * 64, :] = pooled[192:256]
            edge = 128 + half * 384
            finest_rows = dot(finest, kv0[t, edge : edge + 128, :]).astype(BF)
            out_near[t, 256 + half * 64 : 320 + half * 64, :] = finest_rows

    pl.semaphore_wait(bar, 28)
    started = []

    def start(src, dst, seq, rsem):
        copy = pltpu.make_async_remote_copy(
            src_ref=src, dst_ref=dst, send_sem=send.at[len(started)], recv_sem=rsem,
            device_id=(seq, me), device_id_type=MESH,
        )
        copy.start()
        started.append(copy)
        return copy

    near = []

    def send_near(n):
        to_left, to_right = ((0, 0), (64, 64), (128, 192), (256, 320))[n]
        into = slice(64 * n, 64 * n + 64)
        near.append((
            start(out_near.at[:, to_right : to_right + 64], in_near.at[0, :, into], right, near_recv.at[n]),
            start(out_near.at[:, to_left : to_left + 64], in_near.at[1, :, into], left, near_recv.at[4 + n]),
        ))

    def wait_both(copies):
        for copy in copies:
            copy.wait_recv()

    send_near(0)

    loads[2].wait()
    for c in lanes_of:
        qu[:, c] = unit(q_ref[:, c])
    small_q = pool_matrix(((32, 4, 0, 1), (16, 5, 0, 1)), ROWS)
    small_k = pool_matrix(((32, 4, 0, 1), (16, 5, 0, 1), (16, 6, 0, 1)), ROWS)

    sq = dot(small_q, qu[...])
    sk = dot(small_k, kv0[0, 128:640, :])
    sv = dot(small_k, kv0[1, 128:640, :])
    for h, c in enumerate(lanes_of):
        small[h, 0:48] = sq[:, c].astype(BF)
        small[h, 48:80] = sk[0:32, c].astype(BF)
        small[h, 80:112] = sv[0:32, c].astype(BF)
        small[h, 112:128] = sk[32:48, c].astype(BF)
        small[h, 128:144] = sv[32:48, c].astype(BF)
        small[h, 144:160] = jnp.concatenate([sk[48:56, c], sv[48:56, c]], axis=0).astype(BF)
    own_copy = pltpu.make_async_copy(small.at[r, 32:112], ra.at[r], recv.at[0])
    own_copy.start()
    for i in range(4):
        start(small.at[i, 48:112], rc.at[r], at(x_with, 4 * s + i), recv.at[2])
        start(small.at[i, 112:144], rd.at[r], at(x_back, 4 * s + i), recv.at[3])
        start(small.at[i, 144:160], re.at[r], at(x_far, 4 * s + i), recv.at[4])
        start(small.at[i, 0:32], rb.at[r], at(x, 4 * (1 - s) + i), recv.at[1])
    for j in range(1, 4):
        i = (r + j) % 4
        start(small.at[i, 32:112], ra.at[r], at(x, 4 * s + i), recv.at[0])
    send_near(1)
    pools_q = pool_matrix(((128, 1, 0, 1), (64, 2, 0, 1), (32, 3, 0, 1)), 256)
    for half in range(2):
        pooled = dot(pools_q, qu[half * 256 : half * 256 + 256, :]).astype(BF)
        q1[half * 128 : half * 128 + 128, :] = pooled[0:128]
        q2[half * 64 : half * 64 + 64, :] = pooled[128:192]
        q3[half * 32 : half * 32 + 32, :] = pooled[192:224]
    for n in (3, 4):
        loads[n].wait()

    def own_level(heads):
        jobs, places = [], []
        for h in heads:
            c = lanes_of[h]
            for b in range(4):
                keys = slice(128 + max(b - 1, 0) * 128, 128 + min(b + 2, 4) * 128)
                jobs.append((qu[b * 128 : b * 128 + 128, c], kv0[0, keys, c], kv0[1, keys, c], None))
                places.append(h * ROWS + b * 128)
        for place, out in zip(places, attn_all(jobs)):
            put(acc0, place, out)

    own_level((0,))
    own_level((1,))
    wait_both(near[0])
    second = (
        start(in_near.at[0, :, 0:64], hop2.at[0], right, near_recv.at[8]),
        start(in_near.at[1, :, 0:64], hop2.at[1], left, near_recv.at[9]),
    )
    send_near(2)
    own_level((2,))
    own_level((3,))

    for n, ref in enumerate((ra, rb, rc, rd, re)):
        pltpu.make_async_copy(ref, ref, recv.at[n]).wait()
    wrap = jnp.where(s == 1, jnp.where(x == 0, 1.0, 0.0), jnp.where(x == NX - 1, 1.0, 0.0))
    wrap_d = jnp.where(s == 1, jnp.where(x == NX - 1, 1.0, 0.0), jnp.where(x == 0, 1.0, 0.0))
    a, b, c_, d_, e_ = ra[...], rb[...], rc[...], rd[...], re[...]

    def flat(y):
        return y.reshape(y.shape[0] * y.shape[1], E)

    kv_c = jnp.concatenate([flat(c_[:, 0:32]), flat(c_[:, 32:64])], axis=1)
    kv_d = jnp.concatenate([flat(d_[:, 0:16]), flat(d_[:, 16:32])], axis=1)
    k4 = jnp.concatenate([flat(a[:, 16:48]), kv_c[:, 0:E]], axis=0)
    v4 = jnp.concatenate([flat(a[:, 48:80]), kv_c[:, E:]], axis=0)
    q4, q5 = flat(b), flat(a[:, 0:16])
    pooled_c = dot(pool_matrix(((64, 1, 0, 1), (32, 2, 0, 1)), 128), kv_c).astype(BF)
    pooled_d = dot(pool_matrix(((32, 1, 0, 1),), 64), kv_d).astype(BF)
    q_oth = dot(pool_matrix(((128, 1, 0, 2), (128, 2, 0, 4)), 128), q4).astype(BF)
    q6 = dot(pool_matrix(((64, 1, 0, 2),), 64), q5).astype(BF)
    qh = iota((128, 256), 0) // 64
    col = iota((128, 256), 1)
    kh = (col % 128) // 64
    sign = 2 * s - 1
    lead = (kh - qh) * sign
    mask4 = jnp.where(
        col < 128, jnp.where(lead >= 0, 16.0, 0.0), jnp.where(lead <= 0, 16.0 - 16.0 * wrap, 0.0)
    )
    k5 = jnp.concatenate([pooled_c[0:64, 0:E], kv_d[:, 0:E]], axis=0)
    v5 = jnp.concatenate([pooled_c[0:64, E:], kv_d[:, E:]], axis=0)
    far = e_.astype(F32)
    k6 = jnp.concatenate(
        [jnp.concatenate([far[i, 0:8] for i in range(4)], axis=0).astype(BF), pooled_c[64:96, 0:E], pooled_d[:, 0:E]], axis=0
    )
    v6 = jnp.concatenate(
        [jnp.concatenate([far[i, 8:16] for i in range(4)], axis=0).astype(BF), pooled_c[64:96, E:], pooled_d[:, E:]], axis=0
    )
    col6 = iota((128, 96), 1)
    mask6 = 64.0 * jnp.where(col6 < 32, 1.0, jnp.where(col6 < 64, wrap, wrap_d))
    mask5 = 32.0 * jnp.where(iota((64, 128), 1) < 64, 1.0 - wrap, 1.0 - wrap_d)
    outs = attn_all([
        (q4, k4, v4, mask4),
        (q5, k5, v5, mask5),
        (q6, k6, v6, mask6[0:64]),
        (q_oth[0:128], kv_d[:, 0:E], kv_d[:, E:], None),
        (q_oth[128:256], k6, v6, mask6),
    ])
    out_own = outs[1] + outs[2]
    out_oth = outs[0] + 32.0 * (1.0 - wrap_d) * outs[3] + outs[4]

    lane = iota((16, E), 1)

    def den_tile(pieces):
        tile = jnp.zeros((16, E), F32)
        for n, piece in enumerate(pieces):
            hi, lo = split(piece)
            tile = jnp.where((lane >= 32 * n) & (lane < 32 * n + 16), hi, tile)
            tile = jnp.where((lane >= 32 * n + 16) & (lane < 32 * n + 32), lo, tile)
        return tile.astype(BF)

    for i in range(4):
        mine = out_own[i * 16 : i * 16 + 16]
        u_own[i, 0:16] = mine[:, 0:E].astype(BF)
        u_own[i, 16:32] = den_tile([mine[:, E:]])
        other = out_oth[i * 32 : i * 32 + 32]
        u_oth[i, 0:32] = other[:, 0:E].astype(BF)
        u_oth[i, 32:48] = den_tile([other[0:16, E:], other[16:32, E:]])
    own_return = pltpu.make_async_copy(u_own.at[r], w_own.at[r], recv.at[7])
    own_return.start()
    for j in range(1, 4):
        i = (r + j) % 4
        start(u_own.at[i], w_own.at[r], at(x, 4 * s + i), recv.at[7])
    for i in range(4):
        start(u_oth.at[i], w_oth.at[r], at(x, 4 * (1 - s) + i), recv.at[8])

    before_on = jnp.where(d >= 1, 1.0, 0.0)
    after_on = jnp.where(d <= NSEQ - 2, 1.0, 0.0)
    pair_before_on = jnp.where(g >= 1, 1.0, 0.0)
    pair_after_on = jnp.where(g <= NSEQ // 2 - 2, 1.0, 0.0)
    wait_both(second)
    third = start(hop2.at[par], hop3, 2 * g + 1 - par, near_recv.at[10])
    send_near(3)

    def rows_of(side, t, n, chunk, rows):
        return in_near[side, t, 64 * n + rows * chunk : 64 * n + rows * chunk + rows, :].astype(F32)

    wait_both(near[1])
    for side in range(2):
        for t in range(2):
            for chunk in range(4):
                coarse = rebuild(rows_of(side, t, 0, chunk, 16), rows_of(side, t, 1, chunk, 16))
                at_row = 256 * side + 32 * chunk
                kv2[t, at_row : at_row + 32, :] = coarse.astype(BF)

    def pair_rows(kv, t, first, second, c):
        return jnp.concatenate([kv[t, first : first + 128, c], kv[t, second : second + 128, c]], axis=0)

    mask2 = 4.0 * half_mask(128, before_on, after_on)
    outs = attn_all([
        (q2[:, c], pair_rows(kv2, 0, 0, 256, c), pair_rows(kv2, 1, 0, 256, c), mask2) for c in lanes_of
    ])
    for h, out in enumerate(outs):
        put(acc2, h * 128, out)

    def middle(side, t, n):
        chunk = n + (2 if side == 0 else 0)
        coarse = rebuild(rows_of(side, t, 0, chunk, 16), rows_of(side, t, 1, chunk, 16))
        return rebuild(coarse, rows_of(side, t, 2, n, 32))

    wait_both(near[2])
    for side in range(2):
        for t in range(2):
            for n in range(2):
                at_row = 384 * side + 64 * n
                kv1[t, at_row : at_row + 64, :] = middle(side, t, n).astype(BF)

    masks1 = (2.0 * half_mask(128, before_on, 1.0), 2.0 * half_mask(128, 1.0, after_on))
    for b, mask1 in enumerate(masks1):
        lo, hi = b * 128, 256 + b * 128
        outs = attn_all([
            (q1[lo : lo + 128, c], pair_rows(kv1, 0, lo, hi, c), pair_rows(kv1, 1, lo, hi, c), mask1) for c in lanes_of
        ])
        for h, out in enumerate(outs):
            put(acc1, h * 256 + b * 128, out)

    third.wait_recv()
    col192 = iota((64, 192), 1)
    last_on = jnp.where(par == 0, pair_after_on, pair_before_on)
    mask3 = 8.0 * jnp.where(col192 < 64, pair_before_on, jnp.where(col192 < 128, pair_after_on, last_on))

    outs = attn_all([
        (q3[:, c],)
        + tuple(jnp.concatenate([hop2[0, n, :, c], hop2[1, n, :, c], hop3[n, :, c]], axis=0) for n in range(2))
        + (mask3,)
        for c in lanes_of
    ])
    for h, out in enumerate(outs):
        put(acc3, h * 64, out)

    pltpu.make_async_copy(w_own, w_own, recv.at[7]).wait()
    pltpu.make_async_copy(w_oth, w_oth, recv.at[8]).wait()

    def den_of(tile, lo, hi, rows):
        return jnp.broadcast_to(tile[:, lo : lo + 1] + tile[:, hi : hi + 1], (rows, E))

    for h in range(HD):
        own, oth = w_own[h].astype(F32), w_oth[h].astype(F32)
        acc4[0, h * 32 : h * 32 + 32, :] = oth[0:32]
        acc4[1, h * 32 : h * 32 + 16, :] = den_of(oth[32:48], 0, 16, 16)
        acc4[1, h * 32 + 16 : h * 32 + 32, :] = den_of(oth[32:48], 32, 48, 16)
        spread(acc4, (own[0:16], den_of(own[16:32], 0, 16, 16)), h, 16)
        for acc, finer, n in ((acc4, acc3, 32), (acc3, acc2, 64), (acc2, acc1, 128), (acc1, acc0, 256)):
            spread(finer, tuple(acc[t, h * n : h * n + n, :] for t in range(2)), h, n)

    power = []

    def share_power(part, starts):
        for n, first in enumerate(starts):
            squares = jnp.zeros((128, E), F32)
            for h in range(HD):
                rows = slice(h * ROWS + first, h * ROWS + first + 128)
                scaled = acc0[0, rows, :] / acc0[1, rows, :] * scale_ref[h]
                acc0[0, rows, :] = scaled
                squares = squares + scaled * scaled
            pw[part, me, :, n * 128 : n * 128 + 128] = jnp.sum(squares.T, axis=0, keepdims=True)
        for j in (4, 3, 5, 2, 6, 1, 7):
            copy = pltpu.make_async_remote_copy(
                src_ref=pw.at[part, me], dst_ref=pw.at[part, me],
                send_sem=pw_send.at[part, j], recv_sem=pw_recv.at[part, me],
                device_id=(d, (me + j) % NHEAD), device_id_type=MESH,
            )
            copy.start()
            power.append(copy)

    def write_out(part, starts):
        for j in range(1, 8):
            peer = (me + j) % NHEAD
            pltpu.make_async_remote_copy(
                src_ref=pw.at[part, peer], dst_ref=pw.at[part, peer],
                send_sem=pw_send.at[part, j], recv_sem=pw_recv.at[part, peer],
                device_id=(d, peer), device_id_type=MESH,
            ).wait_recv()
        total = jnp.sum(pw[part], axis=0)
        factor = lax.rsqrt(total / (NHEAD * WIDTH) + EPSILON)
        for n, first in enumerate(starts):
            column = jnp.broadcast_to(factor[:, n * 128 : n * 128 + 128], (128, 128)).T
            for h, c in enumerate(lanes_of):
                scaled = acc0[0, h * ROWS + first : h * ROWS + first + 128, :]
                o_ref[first : first + 128, c] = (scaled * column * gain_ref[:, c]).astype(BF)

    share_power(0, (128, 256))

    wait_both(near[3])
    for side in range(2):
        for t in range(2):
            fine = rebuild(middle(side, t, 1 - side), in_near[side, t, 192:256, :].astype(F32))
            kv0[t, 640 * side : 640 * side + 128, :] = fine.astype(BF)

    ends = ((0, 0, before_on), (384, 640, after_on))
    outs = attn_all([
        (qu[first : first + 128, c], kv0[0, key : key + 128, c], kv0[1, key : key + 128, c], None)
        for c in lanes_of
        for first, key, on in ends
    ])
    for n, out in enumerate(outs):
        first, key, on = ends[n % 2]
        for t in range(2):
            acc0[t, pl.ds(n // 2 * ROWS + first, 128), :] += on * out[:, t * E : (t + 1) * E]
    share_power(1, (0, 384))
    write_out(0, (128, 256))
    write_out(1, (0, 384))
    for copy in started:
        copy.wait_send()
    for copy in power:
        copy.wait_send()


def on_device(queries, key_inputs, value_inputs, head_scale, out_gain):
    vmem = pl.BlockSpec(memory_space=pltpu.VMEM)
    hbm = pl.BlockSpec(memory_space=pltpu.HBM)
    return pl.pallas_call(
        kernel,
        out_shape=jax.ShapeDtypeStruct((ROWS, WIDTH), BF),
        in_specs=[hbm] * 5,
        out_specs=vmem,
        scratch_shapes=[
            pltpu.VMEM((512, WIDTH), BF),
            pltpu.VMEM((512, WIDTH), BF),
            pltpu.SMEM((HD,), F32),
            pltpu.VMEM((1, WIDTH), F32),
            pltpu.VMEM((512, WIDTH), BF),
            pltpu.VMEM((2, 768, WIDTH), BF),
            pltpu.VMEM((256, WIDTH), BF),
            pltpu.VMEM((2, 512, WIDTH), BF),
            pltpu.VMEM((128, WIDTH), BF),
            pltpu.VMEM((2, 384, WIDTH), BF),
            pltpu.VMEM((64, WIDTH), BF),
            pltpu.VMEM((2, 384, WIDTH), BF),
            pltpu.VMEM((2, 2, 256, WIDTH), BF),
            pltpu.VMEM((2, 2, 64, WIDTH), BF),
            pltpu.VMEM((2, 64, WIDTH), BF),
            pltpu.VMEM((4, 160, E), BF),
            pltpu.VMEM((4, 80, E), BF),
            pltpu.VMEM((4, 32, E), BF),
            pltpu.VMEM((4, 64, E), BF),
            pltpu.VMEM((4, 32, E), BF),
            pltpu.VMEM((4, 16, E), BF),
            pltpu.VMEM((4, 32, E), BF),
            pltpu.VMEM((4, 48, E), BF),
            pltpu.VMEM((4, 32, E), BF),
            pltpu.VMEM((4, 48, E), BF),
            pltpu.VMEM((2, HD * 512, E), F32),
            pltpu.VMEM((2, HD * 256, E), F32),
            pltpu.VMEM((2, HD * 128, E), F32),
            pltpu.VMEM((2, HD * 64, E), F32),
            pltpu.VMEM((2, HD * 32, E), F32),
            pltpu.VMEM((2, NHEAD, 1, ROWS // 2), F32),
            pltpu.SemaphoreType.DMA((40,)),
            pltpu.SemaphoreType.DMA((10,)),
            pltpu.SemaphoreType.DMA((11,)),
            pltpu.SemaphoreType.DMA((2, 8)),
            pltpu.SemaphoreType.DMA((2, 8)),
            pltpu.SemaphoreType.DMA((5,)),
        ],
        compiler_params=pltpu.CompilerParams(
            collective_id=0, has_side_effects=True, vmem_limit_bytes=int(53.25 * 2**20)
        ),
    )(queries, key_inputs, value_inputs, head_scale, out_gain.reshape(1, WIDTH))


def solution(mesh):
    placed = (P("seq", "head"), P("seq", "head"), P("seq", "head"), P("head"), P("head"))
    return jax.shard_map(
        on_device, mesh=mesh, in_specs=placed, out_specs=P("seq", "head"), check_vma=False
    )
```

```python
import math

import jax
import jax.numpy as jnp
from jax import lax
from jax.experimental import pallas as pl
from jax.experimental.pallas import tpu as pltpu
from jax.sharding import PartitionSpec as P

MESH = pl.DeviceIdType.MESH
BF = jnp.bfloat16
F32 = jnp.float32
EPSILON = 1e-06
E = 128
ROWS = 512
HD = 4
WIDTH = HD * E
SCALE = E ** (-0.5) * math.log2(math.e)
NX, NZ, NSEQ, NHEAD = 4, 8, 32, 8


def iota(shape, dim):
    return lax.broadcasted_iota(jnp.int32, shape, dim)


def pool_matrix(parts, columns):
    out = []
    for rows, shift, offset, repeat in parts:
        group = iota((rows, columns), 0) // repeat + offset
        inside = (iota((rows, columns), 1) >> shift) == group
        out.append(jnp.where(inside, 0.5**shift, 0.0))
    return jnp.concatenate(out, axis=0).astype(BF)


def detail_matrix(rows, shift, chunk, columns):
    k = iota((rows, columns), 0)
    group = k % 16
    for bit in range(3 - shift):
        group = group * 2 + (k >> (4 + bit)) % 2
    col = iota((rows, columns), 1) - 128 * chunk
    sign = jnp.where((col >> (shift - 1)) % 2 == 0, 0.5**shift, -(0.5**shift))
    return jnp.where((col >> shift) == group, sign, 0.0)


def rebuild(coarse, detail):
    return jnp.concatenate([coarse + detail, coarse - detail], axis=0)


def dot(a, b):
    return jnp.dot(a, b, preferred_element_type=F32)


def attn_all(jobs):
    logits = [
        lax.dot_general(q, k, (((1,), (1,)), ((), ())), preferred_element_type=F32) for q, k, v, mask in jobs
    ]
    weights = [jnp.exp2(x * SCALE) for x in logits]
    weights = [(p if job[3] is None else p * job[3]).astype(BF) for p, job in zip(weights, jobs)]
    return [dot(p, jnp.concatenate([job[2], jnp.ones(job[2].shape, BF)], axis=1)) for p, job in zip(weights, jobs)]


def attn(q, k, v, mask=None):
    return attn_all([(q, k, v, mask)])[0]


def half_mask(rows, before_on, after_on):
    qh = iota((rows, 256), 0) // 64
    col = iota((rows, 256), 1)
    kh = (col % 128) // 64
    before = jnp.where(kh <= qh, before_on, 0.0)
    after = jnp.where(kh >= qh, after_on, 0.0)
    return jnp.where(col < 128, before, after)


def split(x):
    hi = x.astype(BF).astype(F32)
    return hi, x - hi


def unit(x):
    x = x.astype(F32)
    return (x * lax.rsqrt(jnp.mean(x * x, axis=-1, keepdims=True) + EPSILON)).astype(BF)


def spread(acc, coarse, h, rows):
    base = h * 2 * rows
    for off in range(2):
        at = pl.ds(base + off, rows, stride=2)
        for t in range(2):
            acc[t, at, :] += coarse[t]


def put(acc, start, pair):
    for t in range(2):
        acc[t, pl.ds(start, pair.shape[0]), :] = pair[:, t * E : (t + 1) * E]


def kernel(
    q_hbm, k_hbm, v_hbm, scale_hbm, o_ref,
    q_ref, k_ref, scale_ref, qu, kv0, q1, kv1, q2, kv2, q3, out_near, in_near, hop2, hop3, small, ra, rb, rc, rd, re,
    u_own, u_oth, w_own, w_oth,
    acc0, acc1, acc2, acc3, acc4, pw, send, recv, near_recv, pw_send, pw_recv, load,
):
    d = lax.axis_index("seq")
    me = lax.axis_index("head")
    x, z = d // NZ, d % NZ
    s, r = z // 4, z % 4
    g, par = d // 2, d % 2
    left, right = (d + NSEQ - 1) % NSEQ, (d + 1) % NSEQ
    x_with = (x + 2 * s - 1 + NX) % NX
    x_back = (x - (2 * s - 1) + NX) % NX
    x_far = (x + 2) % NX

    def at(row, col):
        return row * NZ + col

    bar = pltpu.get_barrier_semaphore()

    def signal(seq, head):
        pl.semaphore_signal(bar, inc=1, device_id=(seq, head), device_id_type=MESH)

    for j in range(1, 8):
        signal(at(x, (z + j) % NZ), me)
        signal(d, (me + j) % NHEAD)
    for i in range(4):
        signal(at(x_back, 4 * s + i), me)
        signal(at(x_with, 4 * s + i), me)
        signal(at(x_far, 4 * s + i), me)
    signal(left, me)
    signal(right, me)

    loads = [
        pltpu.make_async_copy(src, dst, load.at[n])
        for n, (src, dst) in enumerate((
            (k_hbm, k_ref), (v_hbm, kv0.at[1, 128:640]), (q_hbm, q_ref), (scale_hbm, scale_ref)
        ))
    ]
    for copy in loads:
        copy.start()

    lanes_of = [slice(h * E, (h + 1) * E) for h in range(HD)]
    loads[0].wait()
    for c in lanes_of:
        kv0[0, 128:640, c] = unit(k_ref[:, c])
    loads[1].wait()

    pools_kv = jnp.concatenate(
        [pool_matrix(((128, 1, 0, 1), (32, 3, 0, 1)), 256)]
        + [detail_matrix(16, 3, c, 256).astype(BF) for c in range(2)]
        + [detail_matrix(32, 2, c, 256).astype(BF) for c in range(2)],
        axis=0,
    )
    finest = detail_matrix(64, 1, 0, 128).astype(BF)
    for half in range(2):
        for t in range(2):
            pooled = dot(pools_kv, kv0[t, half * 256 + 128 : half * 256 + 384, :]).astype(BF)
            kv1[t, 128 + half * 128 : 256 + half * 128, :] = pooled[0:128]
            out_near[t, half * 32 : half * 32 + 32, :] = pooled[128:160]
            out_near[t, 64 + half * 32 : 96 + half * 32, :] = pooled[160:192]
            out_near[t, 128 + half * 64 : 192 + half * 64, :] = pooled[192:256]
            edge = 128 + half * 384
            finest_rows = dot(finest, kv0[t, edge : edge + 128, :]).astype(BF)
            out_near[t, 256 + half * 64 : 320 + half * 64, :] = finest_rows

    pl.semaphore_wait(bar, 28)
    started = []

    def start(src, dst, seq, rsem):
        copy = pltpu.make_async_remote_copy(
            src_ref=src, dst_ref=dst, send_sem=send.at[len(started)], recv_sem=rsem,
            device_id=(seq, me), device_id_type=MESH,
        )
        copy.start()
        started.append(copy)
        return copy

    near = []

    def send_near(n):
        to_left, to_right = ((0, 0), (64, 64), (128, 192), (256, 320))[n]
        into = slice(64 * n, 64 * n + 64)
        near.append((
            start(out_near.at[:, to_right : to_right + 64], in_near.at[0, :, into], right, near_recv.at[n]),
            start(out_near.at[:, to_left : to_left + 64], in_near.at[1, :, into], left, near_recv.at[4 + n]),
        ))

    def wait_both(copies):
        for copy in copies:
            copy.wait_recv()

    send_near(0)

    loads[2].wait()
    for c in lanes_of:
        qu[:, c] = unit(q_ref[:, c])
    small_q = pool_matrix(((32, 4, 0, 1), (16, 5, 0, 1)), ROWS)
    small_k = pool_matrix(((32, 4, 0, 1), (16, 5, 0, 1), (16, 6, 0, 1)), ROWS)

    sq = dot(small_q, qu[...])
    sk = dot(small_k, kv0[0, 128:640, :])
    sv = dot(small_k, kv0[1, 128:640, :])
    for h, c in enumerate(lanes_of):
        small[h, 0:48] = sq[:, c].astype(BF)
        small[h, 48:80] = sk[0:32, c].astype(BF)
        small[h, 80:112] = sv[0:32, c].astype(BF)
        small[h, 112:128] = sk[32:48, c].astype(BF)
        small[h, 128:144] = sv[32:48, c].astype(BF)
        small[h, 144:160] = jnp.concatenate([sk[48:56, c], sv[48:56, c]], axis=0).astype(BF)
    own_copy = pltpu.make_async_copy(small.at[r, 32:112], ra.at[r], recv.at[0])
    own_copy.start()
    for i in range(4):
        start(small.at[i, 48:112], rc.at[r], at(x_with, 4 * s + i), recv.at[2])
        start(small.at[i, 112:144], rd.at[r], at(x_back, 4 * s + i), recv.at[3])
        start(small.at[i, 144:160], re.at[r], at(x_far, 4 * s + i), recv.at[4])
        start(small.at[i, 0:32], rb.at[r], at(x, 4 * (1 - s) + i), recv.at[1])
    for j in range(1, 4):
        i = (r + j) % 4
        start(small.at[i, 32:112], ra.at[r], at(x, 4 * s + i), recv.at[0])
    send_near(1)
    pools_q = pool_matrix(((128, 1, 0, 1), (64, 2, 0, 1), (32, 3, 0, 1)), 256)
    for half in range(2):
        pooled = dot(pools_q, qu[half * 256 : half * 256 + 256, :]).astype(BF)
        q1[half * 128 : half * 128 + 128, :] = pooled[0:128]
        q2[half * 64 : half * 64 + 64, :] = pooled[128:192]
        q3[half * 32 : half * 32 + 32, :] = pooled[192:224]
    loads[3].wait()

    def own_level(heads):
        jobs, places = [], []
        for h in heads:
            c = lanes_of[h]
            for b in range(4):
                keys = slice(128 + max(b - 1, 0) * 128, 128 + min(b + 2, 4) * 128)
                jobs.append((qu[b * 128 : b * 128 + 128, c], kv0[0, keys, c], kv0[1, keys, c], None))
                places.append(h * ROWS + b * 128)
        for place, out in zip(places, attn_all(jobs)):
            put(acc0, place, out)

    own_level((0,))
    own_level((1,))
    wait_both(near[0])
    second = (
        start(in_near.at[0, :, 0:64], hop2.at[0], right, near_recv.at[8]),
        start(in_near.at[1, :, 0:64], hop2.at[1], left, near_recv.at[9]),
    )
    send_near(2)
    own_level((2,))
    own_level((3,))

    for n, ref in enumerate((ra, rb, rc, rd, re)):
        pltpu.make_async_copy(ref, ref, recv.at[n]).wait()
    wrap = jnp.where(s == 1, jnp.where(x == 0, 1.0, 0.0), jnp.where(x == NX - 1, 1.0, 0.0))
    wrap_d = jnp.where(s == 1, jnp.where(x == NX - 1, 1.0, 0.0), jnp.where(x == 0, 1.0, 0.0))
    a, b, c_, d_, e_ = ra[...], rb[...], rc[...], rd[...], re[...]

    def flat(y):
        return y.reshape(y.shape[0] * y.shape[1], E)

    kv_c = jnp.concatenate([flat(c_[:, 0:32]), flat(c_[:, 32:64])], axis=1)
    kv_d = jnp.concatenate([flat(d_[:, 0:16]), flat(d_[:, 16:32])], axis=1)
    k4 = jnp.concatenate([flat(a[:, 16:48]), kv_c[:, 0:E]], axis=0)
    v4 = jnp.concatenate([flat(a[:, 48:80]), kv_c[:, E:]], axis=0)
    q4, q5 = flat(b), flat(a[:, 0:16])
    pooled_c = dot(pool_matrix(((64, 1, 0, 1), (32, 2, 0, 1)), 128), kv_c).astype(BF)
    pooled_d = dot(pool_matrix(((32, 1, 0, 1),), 64), kv_d).astype(BF)
    q_oth = dot(pool_matrix(((128, 1, 0, 2), (128, 2, 0, 4)), 128), q4).astype(BF)
    q6 = dot(pool_matrix(((64, 1, 0, 2),), 64), q5).astype(BF)
    qh = iota((128, 256), 0) // 64
    col = iota((128, 256), 1)
    kh = (col % 128) // 64
    sign = 2 * s - 1
    lead = (kh - qh) * sign
    mask4 = jnp.where(
        col < 128, jnp.where(lead >= 0, 16.0, 0.0), jnp.where(lead <= 0, 16.0 - 16.0 * wrap, 0.0)
    )
    k5 = jnp.concatenate([pooled_c[0:64, 0:E], kv_d[:, 0:E]], axis=0)
    v5 = jnp.concatenate([pooled_c[0:64, E:], kv_d[:, E:]], axis=0)
    far = e_.astype(F32)
    k6 = jnp.concatenate(
        [jnp.concatenate([far[i, 0:8] for i in range(4)], axis=0).astype(BF), pooled_c[64:96, 0:E], pooled_d[:, 0:E]], axis=0
    )
    v6 = jnp.concatenate(
        [jnp.concatenate([far[i, 8:16] for i in range(4)], axis=0).astype(BF), pooled_c[64:96, E:], pooled_d[:, E:]], axis=0
    )
    col6 = iota((128, 96), 1)
    mask6 = 64.0 * jnp.where(col6 < 32, 1.0, jnp.where(col6 < 64, wrap, wrap_d))
    mask5 = 32.0 * jnp.where(iota((64, 128), 1) < 64, 1.0 - wrap, 1.0 - wrap_d)
    outs = attn_all([
        (q4, k4, v4, mask4),
        (q5, k5, v5, mask5),
        (q6, k6, v6, mask6[0:64]),
        (q_oth[0:128], kv_d[:, 0:E], kv_d[:, E:], None),
        (q_oth[128:256], k6, v6, mask6),
    ])
    out_own = outs[1] + outs[2]
    out_oth = outs[0] + 32.0 * (1.0 - wrap_d) * outs[3] + outs[4]

    lane = iota((16, E), 1)

    def den_tile(pieces):
        tile = jnp.zeros((16, E), F32)
        for n, piece in enumerate(pieces):
            hi, lo = split(piece)
            tile = jnp.where((lane >= 32 * n) & (lane < 32 * n + 16), hi, tile)
            tile = jnp.where((lane >= 32 * n + 16) & (lane < 32 * n + 32), lo, tile)
        return tile.astype(BF)

    for i in range(4):
        mine = out_own[i * 16 : i * 16 + 16]
        u_own[i, 0:16] = mine[:, 0:E].astype(BF)
        u_own[i, 16:32] = den_tile([mine[:, E:]])
        other = out_oth[i * 32 : i * 32 + 32]
        u_oth[i, 0:32] = other[:, 0:E].astype(BF)
        u_oth[i, 32:48] = den_tile([other[0:16, E:], other[16:32, E:]])
    own_return = pltpu.make_async_copy(u_own.at[r], w_own.at[r], recv.at[7])
    own_return.start()
    for j in range(1, 4):
        i = (r + j) % 4
        start(u_own.at[i], w_own.at[r], at(x, 4 * s + i), recv.at[7])
    for i in range(4):
        start(u_oth.at[i], w_oth.at[r], at(x, 4 * (1 - s) + i), recv.at[8])

    before_on = jnp.where(d >= 1, 1.0, 0.0)
    after_on = jnp.where(d <= NSEQ - 2, 1.0, 0.0)
    pair_before_on = jnp.where(g >= 1, 1.0, 0.0)
    pair_after_on = jnp.where(g <= NSEQ // 2 - 2, 1.0, 0.0)
    wait_both(second)
    third = start(hop2.at[par], hop3, 2 * g + 1 - par, near_recv.at[10])
    send_near(3)

    def rows_of(side, t, n, chunk, rows):
        return in_near[side, t, 64 * n + rows * chunk : 64 * n + rows * chunk + rows, :].astype(F32)

    wait_both(near[1])
    for side in range(2):
        for t in range(2):
            for chunk in range(4):
                coarse = rebuild(rows_of(side, t, 0, chunk, 16), rows_of(side, t, 1, chunk, 16))
                at_row = 256 * side + 32 * chunk
                kv2[t, at_row : at_row + 32, :] = coarse.astype(BF)

    def pair_rows(kv, t, first, second, c):
        return jnp.concatenate([kv[t, first : first + 128, c], kv[t, second : second + 128, c]], axis=0)

    mask2 = 4.0 * half_mask(128, before_on, after_on)
    outs = attn_all([
        (q2[:, c], pair_rows(kv2, 0, 0, 256, c), pair_rows(kv2, 1, 0, 256, c), mask2) for c in lanes_of
    ])
    for h, out in enumerate(outs):
        put(acc2, h * 128, out)

    def middle(side, t, n):
        chunk = n + (2 if side == 0 else 0)
        coarse = rebuild(rows_of(side, t, 0, chunk, 16), rows_of(side, t, 1, chunk, 16))
        return rebuild(coarse, rows_of(side, t, 2, n, 32))

    wait_both(near[2])
    for side in range(2):
        for t in range(2):
            for n in range(2):
                at_row = 384 * side + 64 * n
                kv1[t, at_row : at_row + 64, :] = middle(side, t, n).astype(BF)

    masks1 = (2.0 * half_mask(128, before_on, 1.0), 2.0 * half_mask(128, 1.0, after_on))
    for b, mask1 in enumerate(masks1):
        lo, hi = b * 128, 256 + b * 128
        outs = attn_all([
            (q1[lo : lo + 128, c], pair_rows(kv1, 0, lo, hi, c), pair_rows(kv1, 1, lo, hi, c), mask1) for c in lanes_of
        ])
        for h, out in enumerate(outs):
            put(acc1, h * 256 + b * 128, out)

    third.wait_recv()
    col192 = iota((64, 192), 1)
    last_on = jnp.where(par == 0, pair_after_on, pair_before_on)
    mask3 = 8.0 * jnp.where(col192 < 64, pair_before_on, jnp.where(col192 < 128, pair_after_on, last_on))

    outs = attn_all([
        (q3[:, c],)
        + tuple(jnp.concatenate([hop2[0, n, :, c], hop2[1, n, :, c], hop3[n, :, c]], axis=0) for n in range(2))
        + (mask3,)
        for c in lanes_of
    ])
    for h, out in enumerate(outs):
        put(acc3, h * 64, out)

    pltpu.make_async_copy(w_own, w_own, recv.at[7]).wait()
    pltpu.make_async_copy(w_oth, w_oth, recv.at[8]).wait()

    def den_of(tile, lo, hi, rows):
        return jnp.broadcast_to(tile[:, lo : lo + 1] + tile[:, hi : hi + 1], (rows, E))

    for h in range(HD):
        own, oth = w_own[h].astype(F32), w_oth[h].astype(F32)
        acc4[0, h * 32 : h * 32 + 32, :] = oth[0:32]
        acc4[1, h * 32 : h * 32 + 16, :] = den_of(oth[32:48], 0, 16, 16)
        acc4[1, h * 32 + 16 : h * 32 + 32, :] = den_of(oth[32:48], 32, 48, 16)
        spread(acc4, (own[0:16], den_of(own[16:32], 0, 16, 16)), h, 16)
        for acc, finer, n in ((acc4, acc3, 32), (acc3, acc2, 64), (acc2, acc1, 128), (acc1, acc0, 256)):
            spread(finer, tuple(acc[t, h * n : h * n + n, :] for t in range(2)), h, n)

    power = []

    def share_power(part, starts):
        for n, first in enumerate(starts):
            squares = jnp.zeros((128, E), F32)
            for h in range(HD):
                rows = slice(h * ROWS + first, h * ROWS + first + 128)
                scaled = acc0[0, rows, :] / acc0[1, rows, :] * scale_ref[h]
                acc0[0, rows, :] = scaled
                squares = squares + scaled * scaled
            pw[part, me, :, n * 128 : n * 128 + 128] = jnp.sum(squares.T, axis=0, keepdims=True)
        for j in (4, 3, 5, 2, 6, 1, 7):
            copy = pltpu.make_async_remote_copy(
                src_ref=pw.at[part, me], dst_ref=pw.at[part, me],
                send_sem=pw_send.at[part, j], recv_sem=pw_recv.at[part, me],
                device_id=(d, (me + j) % NHEAD), device_id_type=MESH,
            )
            copy.start()
            power.append(copy)

    def write_out(part, starts):
        for j in range(1, 8):
            peer = (me + j) % NHEAD
            pltpu.make_async_remote_copy(
                src_ref=pw.at[part, peer], dst_ref=pw.at[part, peer],
                send_sem=pw_send.at[part, j], recv_sem=pw_recv.at[part, peer],
                device_id=(d, peer), device_id_type=MESH,
            ).wait_recv()
        total = jnp.sum(pw[part], axis=0)
        factor = lax.rsqrt(total / (NHEAD * WIDTH) + EPSILON)
        for n, first in enumerate(starts):
            column = jnp.broadcast_to(factor[:, n * 128 : n * 128 + 128], (128, 128)).T
            for h, c in enumerate(lanes_of):
                scaled = acc0[0, h * ROWS + first : h * ROWS + first + 128, :]
                o_ref[first : first + 128, c] = (scaled * column).astype(BF)

    share_power(0, (128, 256))

    wait_both(near[3])
    for side in range(2):
        for t in range(2):
            fine = rebuild(middle(side, t, 1 - side), in_near[side, t, 192:256, :].astype(F32))
            kv0[t, 640 * side : 640 * side + 128, :] = fine.astype(BF)

    ends = ((0, 0, before_on), (384, 640, after_on))
    outs = attn_all([
        (qu[first : first + 128, c], kv0[0, key : key + 128, c], kv0[1, key : key + 128, c], None)
        for c in lanes_of
        for first, key, on in ends
    ])
    for n, out in enumerate(outs):
        first, key, on = ends[n % 2]
        for t in range(2):
            acc0[t, pl.ds(n // 2 * ROWS + first, 128), :] += on * out[:, t * E : (t + 1) * E]
    share_power(1, (0, 384))
    write_out(0, (128, 256))
    write_out(1, (0, 384))
    for copy in started:
        copy.wait_send()
    for copy in power:
        copy.wait_send()


def on_device(queries, key_inputs, value_inputs, head_scale, out_gain):
    vmem = pl.BlockSpec(memory_space=pltpu.VMEM)
    hbm = pl.BlockSpec(memory_space=pltpu.HBM)
    normed = pl.pallas_call(
        kernel,
        out_shape=jax.ShapeDtypeStruct((ROWS, WIDTH), BF),
        in_specs=[hbm] * 4,
        out_specs=vmem,
        scratch_shapes=[
            pltpu.VMEM((512, WIDTH), BF),
            pltpu.VMEM((512, WIDTH), BF),
            pltpu.SMEM((HD,), F32),
            pltpu.VMEM((512, WIDTH), BF),
            pltpu.VMEM((2, 768, WIDTH), BF),
            pltpu.VMEM((256, WIDTH), BF),
            pltpu.VMEM((2, 512, WIDTH), BF),
            pltpu.VMEM((128, WIDTH), BF),
            pltpu.VMEM((2, 384, WIDTH), BF),
            pltpu.VMEM((64, WIDTH), BF),
            pltpu.VMEM((2, 384, WIDTH), BF),
            pltpu.VMEM((2, 2, 256, WIDTH), BF),
            pltpu.VMEM((2, 2, 64, WIDTH), BF),
            pltpu.VMEM((2, 64, WIDTH), BF),
            pltpu.VMEM((4, 160, E), BF),
            pltpu.VMEM((4, 80, E), BF),
            pltpu.VMEM((4, 32, E), BF),
            pltpu.VMEM((4, 64, E), BF),
            pltpu.VMEM((4, 32, E), BF),
            pltpu.VMEM((4, 16, E), BF),
            pltpu.VMEM((4, 32, E), BF),
            pltpu.VMEM((4, 48, E), BF),
            pltpu.VMEM((4, 32, E), BF),
            pltpu.VMEM((4, 48, E), BF),
            pltpu.VMEM((2, HD * 512, E), F32),
            pltpu.VMEM((2, HD * 256, E), F32),
            pltpu.VMEM((2, HD * 128, E), F32),
            pltpu.VMEM((2, HD * 64, E), F32),
            pltpu.VMEM((2, HD * 32, E), F32),
            pltpu.VMEM((2, NHEAD, 1, ROWS // 2), F32),
            pltpu.SemaphoreType.DMA((40,)),
            pltpu.SemaphoreType.DMA((10,)),
            pltpu.SemaphoreType.DMA((11,)),
            pltpu.SemaphoreType.DMA((2, 8)),
            pltpu.SemaphoreType.DMA((2, 8)),
            pltpu.SemaphoreType.DMA((5,)),
        ],
        compiler_params=pltpu.CompilerParams(
            collective_id=0, has_side_effects=True, vmem_limit_bytes=int(53.25 * 2**20)
        ),
    )(queries, key_inputs, value_inputs, head_scale)
    return (normed.astype(F32) * out_gain[None, :]).astype(BF)


def solution(mesh):
    placed = (P("seq", "head"), P("seq", "head"), P("seq", "head"), P("head"), P("head"))
    return jax.shard_map(
        on_device, mesh=mesh, in_specs=placed, out_specs=P("seq", "head"), check_vma=False
    )
```

```python
import math

import jax
import jax.numpy as jnp
from jax import lax
from jax.experimental import pallas as pl
from jax.experimental.pallas import tpu as pltpu
from jax.sharding import PartitionSpec as P

MESH = pl.DeviceIdType.MESH
BF = jnp.bfloat16
F32 = jnp.float32
EPSILON = 1e-06
E = 128
ROWS = 512
HD = 4
WIDTH = HD * E
SCALE = E ** (-0.5) * math.log2(math.e)
NX, NZ, NSEQ, NHEAD = 4, 8, 32, 8


def iota(shape, dim):
    return lax.broadcasted_iota(jnp.int32, shape, dim)


def pool_matrix(parts, columns):
    out = []
    for rows, shift, offset, repeat in parts:
        group = iota((rows, columns), 0) // repeat + offset
        inside = (iota((rows, columns), 1) >> shift) == group
        out.append(jnp.where(inside, 0.5**shift, 0.0))
    return jnp.concatenate(out, axis=0).astype(BF)


def detail_matrix(rows, shift, chunk, columns):
    k = iota((rows, columns), 0)
    group = k % 16
    for bit in range(3 - shift):
        group = group * 2 + (k >> (4 + bit)) % 2
    col = iota((rows, columns), 1) - 128 * chunk
    sign = jnp.where((col >> (shift - 1)) % 2 == 0, 0.5**shift, -(0.5**shift))
    return jnp.where((col >> shift) == group, sign, 0.0)


def rebuild(coarse, detail):
    return jnp.concatenate([coarse + detail, coarse - detail], axis=0)


def dot(a, b):
    return jnp.dot(a, b, preferred_element_type=F32)


def attn_all(jobs):
    logits = [
        lax.dot_general(q, k, (((1,), (1,)), ((), ())), preferred_element_type=F32) for q, k, v, mask in jobs
    ]
    weights = [jnp.exp2(x * SCALE) for x in logits]
    weights = [(p if job[3] is None else p * job[3]).astype(BF) for p, job in zip(weights, jobs)]
    return [dot(p, jnp.concatenate([job[2], jnp.ones(job[2].shape, BF)], axis=1)) for p, job in zip(weights, jobs)]


def attn(q, k, v, mask=None):
    return attn_all([(q, k, v, mask)])[0]


def half_mask(rows, before_on, after_on):
    qh = iota((rows, 256), 0) // 64
    col = iota((rows, 256), 1)
    kh = (col % 128) // 64
    before = jnp.where(kh <= qh, before_on, 0.0)
    after = jnp.where(kh >= qh, after_on, 0.0)
    return jnp.where(col < 128, before, after)


def split(x):
    hi = x.astype(BF).astype(F32)
    return hi, x - hi


def unit(x):
    x = x.astype(F32)
    return (x * lax.rsqrt(jnp.mean(x * x, axis=-1, keepdims=True) + EPSILON)).astype(BF)


def spread(acc, coarse, h, rows):
    base = h * 2 * rows
    for off in range(2):
        at = pl.ds(base + off, rows, stride=2)
        for t in range(2):
            acc[t, at, :] += coarse[t]


def put(acc, start, pair):
    for t in range(2):
        acc[t, pl.ds(start, pair.shape[0]), :] = pair[:, t * E : (t + 1) * E]


def kernel(
    q_hbm, k_hbm, v_hbm, scale_hbm, o_ref,
    q_ref, k_ref, scale_ref, qu, kv0, q1, kv1, q2, kv2, q3, out_near, in_near, hop2, hop3, small, ra, rb, rc, rd, re,
    u_own, u_oth, w_own, w_oth,
    acc0, acc1, acc2, acc3, acc4, pw, send, recv, near_recv, pw_send, pw_recv, load,
):
    d = lax.axis_index("seq")
    me = lax.axis_index("head")
    x, z = d // NZ, d % NZ
    s, r = z // 4, z % 4
    g, par = d // 2, d % 2
    left, right = (d + NSEQ - 1) % NSEQ, (d + 1) % NSEQ
    x_with = (x + 2 * s - 1 + NX) % NX
    x_back = (x - (2 * s - 1) + NX) % NX
    x_far = (x + 2) % NX

    def at(row, col):
        return row * NZ + col

    bar = pltpu.get_barrier_semaphore()

    def signal(seq, head):
        pl.semaphore_signal(bar, inc=1, device_id=(seq, head), device_id_type=MESH)

    for j in range(1, 8):
        signal(at(x, (z + j) % NZ), me)
        signal(d, (me + j) % NHEAD)
    for i in range(4):
        signal(at(x_back, 4 * s + i), me)
        signal(at(x_with, 4 * s + i), me)
        signal(at(x_far, 4 * s + i), me)
    signal(left, me)
    signal(right, me)

    loads = [
        pltpu.make_async_copy(src, dst, load.at[n])
        for n, (src, dst) in enumerate((
            (k_hbm, k_ref), (v_hbm, kv0.at[1, 128:640]), (q_hbm, q_ref), (scale_hbm, scale_ref)
        ))
    ]
    for copy in loads:
        copy.start()

    lanes_of = [slice(h * E, (h + 1) * E) for h in range(HD)]
    loads[0].wait()
    for c in lanes_of:
        kv0[0, 128:640, c] = unit(k_ref[:, c])
    loads[1].wait()

    pools_kv = jnp.concatenate(
        [pool_matrix(((128, 1, 0, 1), (32, 3, 0, 1)), 256)]
        + [detail_matrix(16, 3, c, 256).astype(BF) for c in range(2)]
        + [detail_matrix(32, 2, c, 256).astype(BF) for c in range(2)],
        axis=0,
    )
    finest = detail_matrix(64, 1, 0, 128).astype(BF)
    for half in range(2):
        for t in range(2):
            pooled = dot(pools_kv, kv0[t, half * 256 + 128 : half * 256 + 384, :]).astype(BF)
            kv1[t, 128 + half * 128 : 256 + half * 128, :] = pooled[0:128]
            out_near[t, half * 32 : half * 32 + 32, :] = pooled[128:160]
            out_near[t, 64 + half * 32 : 96 + half * 32, :] = pooled[160:192]
            out_near[t, 128 + half * 64 : 192 + half * 64, :] = pooled[192:256]
            edge = 128 + half * 384
            finest_rows = dot(finest, kv0[t, edge : edge + 128, :]).astype(BF)
            out_near[t, 256 + half * 64 : 320 + half * 64, :] = finest_rows

    pl.semaphore_wait(bar, 28)
    started = []

    def start(src, dst, seq, rsem):
        copy = pltpu.make_async_remote_copy(
            src_ref=src, dst_ref=dst, send_sem=send.at[len(started)], recv_sem=rsem,
            device_id=(seq, me), device_id_type=MESH,
        )
        copy.start()
        started.append(copy)
        return copy

    near = []

    def send_near(n):
        to_left, to_right = ((0, 0), (64, 64), (128, 192), (256, 320))[n]
        into = slice(64 * n, 64 * n + 64)
        near.append((
            start(out_near.at[:, to_right : to_right + 64], in_near.at[0, :, into], right, near_recv.at[n]),
            start(out_near.at[:, to_left : to_left + 64], in_near.at[1, :, into], left, near_recv.at[4 + n]),
        ))

    def wait_both(copies):
        for copy in copies:
            copy.wait_recv()

    send_near(0)

    loads[2].wait()
    for c in lanes_of:
        qu[:, c] = unit(q_ref[:, c])
    small_q = pool_matrix(((32, 4, 0, 1), (16, 5, 0, 1)), ROWS)
    small_k = pool_matrix(((32, 4, 0, 1), (16, 5, 0, 1), (16, 6, 0, 1)), ROWS)

    sq = dot(small_q, qu[...])
    sk = dot(small_k, kv0[0, 128:640, :])
    sv = dot(small_k, kv0[1, 128:640, :])
    for h, c in enumerate(lanes_of):
        small[h, 0:48] = sq[:, c].astype(BF)
        small[h, 48:80] = sk[0:32, c].astype(BF)
        small[h, 80:112] = sv[0:32, c].astype(BF)
        small[h, 112:128] = sk[32:48, c].astype(BF)
        small[h, 128:144] = sv[32:48, c].astype(BF)
        small[h, 144:160] = jnp.concatenate([sk[48:56, c], sv[48:56, c]], axis=0).astype(BF)
    own_copy = pltpu.make_async_copy(small.at[r, 32:112], ra.at[r], recv.at[0])
    own_copy.start()
    for i in range(4):
        start(small.at[i, 48:112], rc.at[r], at(x_with, 4 * s + i), recv.at[2])
        start(small.at[i, 112:144], rd.at[r], at(x_back, 4 * s + i), recv.at[3])
        start(small.at[i, 144:160], re.at[r], at(x_far, 4 * s + i), recv.at[4])
        start(small.at[i, 0:32], rb.at[r], at(x, 4 * (1 - s) + i), recv.at[1])
    for j in range(1, 4):
        i = (r + j) % 4
        start(small.at[i, 32:112], ra.at[r], at(x, 4 * s + i), recv.at[0])
    pools_q = pool_matrix(((128, 1, 0, 1), (64, 2, 0, 1), (32, 3, 0, 1)), 256)
    for half in range(2):
        pooled = dot(pools_q, qu[half * 256 : half * 256 + 256, :]).astype(BF)
        q1[half * 128 : half * 128 + 128, :] = pooled[0:128]
        q2[half * 64 : half * 64 + 64, :] = pooled[128:192]
        q3[half * 32 : half * 32 + 32, :] = pooled[192:224]
    loads[3].wait()

    def own_level(heads):
        jobs, places = [], []
        for h in heads:
            c = lanes_of[h]
            for b in range(4):
                keys = slice(128 + max(b - 1, 0) * 128, 128 + min(b + 2, 4) * 128)
                jobs.append((qu[b * 128 : b * 128 + 128, c], kv0[0, keys, c], kv0[1, keys, c], None))
                places.append(h * ROWS + b * 128)
        for place, out in zip(places, attn_all(jobs)):
            put(acc0, place, out)

    own_level((0,))
    own_level((1,))
    wait_both(near[0])
    second = (
        start(in_near.at[0, :, 0:64], hop2.at[0], right, near_recv.at[8]),
        start(in_near.at[1, :, 0:64], hop2.at[1], left, near_recv.at[9]),
    )
    send_near(1)
    send_near(2)
    own_level((2,))
    own_level((3,))

    for n, ref in enumerate((ra, rb, rc, rd, re)):
        pltpu.make_async_copy(ref, ref, recv.at[n]).wait()
    wrap = jnp.where(s == 1, jnp.where(x == 0, 1.0, 0.0), jnp.where(x == NX - 1, 1.0, 0.0))
    wrap_d = jnp.where(s == 1, jnp.where(x == NX - 1, 1.0, 0.0), jnp.where(x == 0, 1.0, 0.0))
    a, b, c_, d_, e_ = ra[...], rb[...], rc[...], rd[...], re[...]

    def flat(y):
        return y.reshape(y.shape[0] * y.shape[1], E)

    kv_c = jnp.concatenate([flat(c_[:, 0:32]), flat(c_[:, 32:64])], axis=1)
    kv_d = jnp.concatenate([flat(d_[:, 0:16]), flat(d_[:, 16:32])], axis=1)
    k4 = jnp.concatenate([flat(a[:, 16:48]), kv_c[:, 0:E]], axis=0)
    v4 = jnp.concatenate([flat(a[:, 48:80]), kv_c[:, E:]], axis=0)
    q4, q5 = flat(b), flat(a[:, 0:16])
    pooled_c = dot(pool_matrix(((64, 1, 0, 1), (32, 2, 0, 1)), 128), kv_c).astype(BF)
    pooled_d = dot(pool_matrix(((32, 1, 0, 1),), 64), kv_d).astype(BF)
    q_oth = dot(pool_matrix(((128, 1, 0, 2), (128, 2, 0, 4)), 128), q4).astype(BF)
    q6 = dot(pool_matrix(((64, 1, 0, 2),), 64), q5).astype(BF)
    qh = iota((128, 256), 0) // 64
    col = iota((128, 256), 1)
    kh = (col % 128) // 64
    sign = 2 * s - 1
    lead = (kh - qh) * sign
    mask4 = jnp.where(
        col < 128, jnp.where(lead >= 0, 16.0, 0.0), jnp.where(lead <= 0, 16.0 - 16.0 * wrap, 0.0)
    )
    k5 = jnp.concatenate([pooled_c[0:64, 0:E], kv_d[:, 0:E]], axis=0)
    v5 = jnp.concatenate([pooled_c[0:64, E:], kv_d[:, E:]], axis=0)
    far = e_.astype(F32)
    k6 = jnp.concatenate(
        [jnp.concatenate([far[i, 0:8] for i in range(4)], axis=0).astype(BF), pooled_c[64:96, 0:E], pooled_d[:, 0:E]], axis=0
    )
    v6 = jnp.concatenate(
        [jnp.concatenate([far[i, 8:16] for i in range(4)], axis=0).astype(BF), pooled_c[64:96, E:], pooled_d[:, E:]], axis=0
    )
    col6 = iota((128, 96), 1)
    mask6 = 64.0 * jnp.where(col6 < 32, 1.0, jnp.where(col6 < 64, wrap, wrap_d))
    mask5 = 32.0 * jnp.where(iota((64, 128), 1) < 64, 1.0 - wrap, 1.0 - wrap_d)
    outs = attn_all([
        (q4, k4, v4, mask4),
        (q5, k5, v5, mask5),
        (q6, k6, v6, mask6[0:64]),
        (q_oth[0:128], kv_d[:, 0:E], kv_d[:, E:], None),
        (q_oth[128:256], k6, v6, mask6),
    ])
    out_own = outs[1] + outs[2]
    out_oth = outs[0] + 32.0 * (1.0 - wrap_d) * outs[3] + outs[4]

    lane = iota((16, E), 1)

    def den_tile(pieces):
        tile = jnp.zeros((16, E), F32)
        for n, piece in enumerate(pieces):
            hi, lo = split(piece)
            tile = jnp.where((lane >= 32 * n) & (lane < 32 * n + 16), hi, tile)
            tile = jnp.where((lane >= 32 * n + 16) & (lane < 32 * n + 32), lo, tile)
        return tile.astype(BF)

    for i in range(4):
        mine = out_own[i * 16 : i * 16 + 16]
        u_own[i, 0:16] = mine[:, 0:E].astype(BF)
        u_own[i, 16:32] = den_tile([mine[:, E:]])
        other = out_oth[i * 32 : i * 32 + 32]
        u_oth[i, 0:32] = other[:, 0:E].astype(BF)
        u_oth[i, 32:48] = den_tile([other[0:16, E:], other[16:32, E:]])
    for i in range(4):
        start(u_oth.at[i], w_oth.at[r], at(x, 4 * (1 - s) + i), recv.at[8])
    own_return = pltpu.make_async_copy(u_own.at[r], w_own.at[r], recv.at[7])
    own_return.start()
    for j in range(1, 4):
        i = (r + j) % 4
        start(u_own.at[i], w_own.at[r], at(x, 4 * s + i), recv.at[7])

    before_on = jnp.where(d >= 1, 1.0, 0.0)
    after_on = jnp.where(d <= NSEQ - 2, 1.0, 0.0)
    pair_before_on = jnp.where(g >= 1, 1.0, 0.0)
    pair_after_on = jnp.where(g <= NSEQ // 2 - 2, 1.0, 0.0)
    wait_both(second)
    third = start(hop2.at[par], hop3, 2 * g + 1 - par, near_recv.at[10])
    send_near(3)

    def rows_of(side, t, n, chunk, rows):
        return in_near[side, t, 64 * n + rows * chunk : 64 * n + rows * chunk + rows, :].astype(F32)

    wait_both(near[1])
    for side in range(2):
        for t in range(2):
            for chunk in range(4):
                coarse = rebuild(rows_of(side, t, 0, chunk, 16), rows_of(side, t, 1, chunk, 16))
                at_row = 256 * side + 32 * chunk
                kv2[t, at_row : at_row + 32, :] = coarse.astype(BF)

    def pair_rows(kv, t, first, second, c):
        return jnp.concatenate([kv[t, first : first + 128, c], kv[t, second : second + 128, c]], axis=0)

    mask2 = 4.0 * half_mask(128, before_on, after_on)
    outs = attn_all([
        (q2[:, c], pair_rows(kv2, 0, 0, 256, c), pair_rows(kv2, 1, 0, 256, c), mask2) for c in lanes_of
    ])
    for h, out in enumerate(outs):
        put(acc2, h * 128, out)

    def middle(side, t, n):
        chunk = n + (2 if side == 0 else 0)
        coarse = rebuild(rows_of(side, t, 0, chunk, 16), rows_of(side, t, 1, chunk, 16))
        return rebuild(coarse, rows_of(side, t, 2, n, 32))

    wait_both(near[2])
    for side in range(2):
        for t in range(2):
            for n in range(2):
                at_row = 384 * side + 64 * n
                kv1[t, at_row : at_row + 64, :] = middle(side, t, n).astype(BF)

    masks1 = (2.0 * half_mask(128, before_on, 1.0), 2.0 * half_mask(128, 1.0, after_on))
    for b, mask1 in enumerate(masks1):
        lo, hi = b * 128, 256 + b * 128
        outs = attn_all([
            (q1[lo : lo + 128, c], pair_rows(kv1, 0, lo, hi, c), pair_rows(kv1, 1, lo, hi, c), mask1) for c in lanes_of
        ])
        for h, out in enumerate(outs):
            put(acc1, h * 256 + b * 128, out)

    third.wait_recv()
    col192 = iota((64, 192), 1)
    last_on = jnp.where(par == 0, pair_after_on, pair_before_on)
    mask3 = 8.0 * jnp.where(col192 < 64, pair_before_on, jnp.where(col192 < 128, pair_after_on, last_on))

    outs = attn_all([
        (q3[:, c],)
        + tuple(jnp.concatenate([hop2[0, n, :, c], hop2[1, n, :, c], hop3[n, :, c]], axis=0) for n in range(2))
        + (mask3,)
        for c in lanes_of
    ])
    for h, out in enumerate(outs):
        put(acc3, h * 64, out)

    pltpu.make_async_copy(w_own, w_own, recv.at[7]).wait()
    pltpu.make_async_copy(w_oth, w_oth, recv.at[8]).wait()

    def den_of(tile, lo, hi, rows):
        return jnp.broadcast_to(tile[:, lo : lo + 1] + tile[:, hi : hi + 1], (rows, E))

    for h in range(HD):
        own, oth = w_own[h].astype(F32), w_oth[h].astype(F32)
        acc4[0, h * 32 : h * 32 + 32, :] = oth[0:32]
        acc4[1, h * 32 : h * 32 + 16, :] = den_of(oth[32:48], 0, 16, 16)
        acc4[1, h * 32 + 16 : h * 32 + 32, :] = den_of(oth[32:48], 32, 48, 16)
        spread(acc4, (own[0:16], den_of(own[16:32], 0, 16, 16)), h, 16)
        for acc, finer, n in ((acc4, acc3, 32), (acc3, acc2, 64), (acc2, acc1, 128), (acc1, acc0, 256)):
            spread(finer, tuple(acc[t, h * n : h * n + n, :] for t in range(2)), h, n)

    power = []

    def share_power(part, starts):
        for n, first in enumerate(starts):
            squares = jnp.zeros((128, E), F32)
            for h in range(HD):
                rows = slice(h * ROWS + first, h * ROWS + first + 128)
                scaled = acc0[0, rows, :] / acc0[1, rows, :] * scale_ref[h]
                acc0[0, rows, :] = scaled
                squares = squares + scaled * scaled
            pw[part, me, :, n * 128 : n * 128 + 128] = jnp.sum(squares.T, axis=0, keepdims=True)
        for j in (4, 3, 5, 2, 6, 1, 7):
            copy = pltpu.make_async_remote_copy(
                src_ref=pw.at[part, me], dst_ref=pw.at[part, me],
                send_sem=pw_send.at[part, j], recv_sem=pw_recv.at[part, me],
                device_id=(d, (me + j) % NHEAD), device_id_type=MESH,
            )
            copy.start()
            power.append(copy)

    def write_out(part, starts):
        for j in range(1, 8):
            peer = (me + j) % NHEAD
            pltpu.make_async_remote_copy(
                src_ref=pw.at[part, peer], dst_ref=pw.at[part, peer],
                send_sem=pw_send.at[part, j], recv_sem=pw_recv.at[part, peer],
                device_id=(d, peer), device_id_type=MESH,
            ).wait_recv()
        total = jnp.sum(pw[part], axis=0)
        factor = lax.rsqrt(total / (NHEAD * WIDTH) + EPSILON)
        for n, first in enumerate(starts):
            column = jnp.broadcast_to(factor[:, n * 128 : n * 128 + 128], (128, 128)).T
            for h, c in enumerate(lanes_of):
                scaled = acc0[0, h * ROWS + first : h * ROWS + first + 128, :]
                o_ref[first : first + 128, c] = (scaled * column).astype(BF)

    wait_both(near[3])
    for side in range(2):
        for t in range(2):
            fine = rebuild(middle(side, t, 1 - side), in_near[side, t, 192:256, :].astype(F32))
            kv0[t, 640 * side : 640 * side + 128, :] = fine.astype(BF)

    ends = ((0, 0, before_on), (384, 640, after_on))
    outs = attn_all([
        (qu[first : first + 128, c], kv0[0, key : key + 128, c], kv0[1, key : key + 128, c], None)
        for c in lanes_of
        for first, key, on in ends
    ])
    for n, out in enumerate(outs):
        first, key, on = ends[n % 2]
        for t in range(2):
            acc0[t, pl.ds(n // 2 * ROWS + first, 128), :] += on * out[:, t * E : (t + 1) * E]
    share_power(0, (0, 128, 256, 384))
    write_out(0, (0, 128, 256, 384))
    for copy in started:
        copy.wait_send()
    for copy in power:
        copy.wait_send()


def on_device(queries, key_inputs, value_inputs, head_scale, out_gain):
    vmem = pl.BlockSpec(memory_space=pltpu.VMEM)
    hbm = pl.BlockSpec(memory_space=pltpu.HBM)
    normed = pl.pallas_call(
        kernel,
        out_shape=jax.ShapeDtypeStruct((ROWS, WIDTH), BF),
        in_specs=[hbm] * 4,
        out_specs=vmem,
        scratch_shapes=[
            pltpu.VMEM((512, WIDTH), BF),
            pltpu.VMEM((512, WIDTH), BF),
            pltpu.SMEM((HD,), F32),
            pltpu.VMEM((512, WIDTH), BF),
            pltpu.VMEM((2, 768, WIDTH), BF),
            pltpu.VMEM((256, WIDTH), BF),
            pltpu.VMEM((2, 512, WIDTH), BF),
            pltpu.VMEM((128, WIDTH), BF),
            pltpu.VMEM((2, 384, WIDTH), BF),
            pltpu.VMEM((64, WIDTH), BF),
            pltpu.VMEM((2, 384, WIDTH), BF),
            pltpu.VMEM((2, 2, 256, WIDTH), BF),
            pltpu.VMEM((2, 2, 64, WIDTH), BF),
            pltpu.VMEM((2, 64, WIDTH), BF),
            pltpu.VMEM((4, 160, E), BF),
            pltpu.VMEM((4, 80, E), BF),
            pltpu.VMEM((4, 32, E), BF),
            pltpu.VMEM((4, 64, E), BF),
            pltpu.VMEM((4, 32, E), BF),
            pltpu.VMEM((4, 16, E), BF),
            pltpu.VMEM((4, 32, E), BF),
            pltpu.VMEM((4, 48, E), BF),
            pltpu.VMEM((4, 32, E), BF),
            pltpu.VMEM((4, 48, E), BF),
            pltpu.VMEM((2, HD * 512, E), F32),
            pltpu.VMEM((2, HD * 256, E), F32),
            pltpu.VMEM((2, HD * 128, E), F32),
            pltpu.VMEM((2, HD * 64, E), F32),
            pltpu.VMEM((2, HD * 32, E), F32),
            pltpu.VMEM((1, NHEAD, 1, ROWS), F32),
            pltpu.SemaphoreType.DMA((40,)),
            pltpu.SemaphoreType.DMA((10,)),
            pltpu.SemaphoreType.DMA((11,)),
            pltpu.SemaphoreType.DMA((1, 8)),
            pltpu.SemaphoreType.DMA((1, 8)),
            pltpu.SemaphoreType.DMA((5,)),
        ],
        compiler_params=pltpu.CompilerParams(
            collective_id=0, has_side_effects=True, vmem_limit_bytes=int(53.25 * 2**20)
        ),
    )(queries, key_inputs, value_inputs, head_scale)
    return (normed.astype(F32) * out_gain[None, :]).astype(BF)


def solution(mesh):
    placed = (P("seq", "head"), P("seq", "head"), P("seq", "head"), P("head"), P("head"))
    return jax.shard_map(
        on_device, mesh=mesh, in_specs=placed, out_specs=P("seq", "head"), check_vma=False
    )
```

```python
import math

import jax
import jax.numpy as jnp
from jax import lax
from jax.experimental import pallas as pl
from jax.experimental.pallas import tpu as pltpu
from jax.sharding import PartitionSpec as P

MESH = pl.DeviceIdType.MESH
BF = jnp.bfloat16
F32 = jnp.float32
EPSILON = 1e-06
E = 128
ROWS = 512
HD = 4
WIDTH = HD * E
SCALE = E ** (-0.5) * math.log2(math.e)
NX, NZ, NSEQ, NHEAD = 4, 8, 32, 8


def iota(shape, dim):
    return lax.broadcasted_iota(jnp.int32, shape, dim)


def pool_matrix(parts, columns):
    out = []
    for rows, shift, offset, repeat in parts:
        group = iota((rows, columns), 0) // repeat + offset
        inside = (iota((rows, columns), 1) >> shift) == group
        out.append(jnp.where(inside, 0.5**shift, 0.0))
    return jnp.concatenate(out, axis=0).astype(BF)


def detail_matrix(rows, shift, chunk, columns):
    k = iota((rows, columns), 0)
    group = k % 16
    for bit in range(3 - shift):
        group = group * 2 + (k >> (4 + bit)) % 2
    col = iota((rows, columns), 1) - 128 * chunk
    sign = jnp.where((col >> (shift - 1)) % 2 == 0, 0.5**shift, -(0.5**shift))
    return jnp.where((col >> shift) == group, sign, 0.0)


def rebuild(coarse, detail):
    return jnp.concatenate([coarse + detail, coarse - detail], axis=0)


def dot(a, b):
    return jnp.dot(a, b, preferred_element_type=F32)


def attn_all(jobs):
    logits = [
        lax.dot_general(q, k, (((1,), (1,)), ((), ())), preferred_element_type=F32) for q, k, v, mask in jobs
    ]
    weights = [jnp.exp2(x * SCALE) for x in logits]
    weights = [(p if job[3] is None else p * job[3]).astype(BF) for p, job in zip(weights, jobs)]
    return [dot(p, jnp.concatenate([job[2], jnp.ones(job[2].shape, BF)], axis=1)) for p, job in zip(weights, jobs)]


def attn(q, k, v, mask=None):
    return attn_all([(q, k, v, mask)])[0]


def half_mask(rows, before_on, after_on):
    qh = iota((rows, 256), 0) // 64
    col = iota((rows, 256), 1)
    kh = (col % 128) // 64
    before = jnp.where(kh <= qh, before_on, 0.0)
    after = jnp.where(kh >= qh, after_on, 0.0)
    return jnp.where(col < 128, before, after)


def split(x):
    hi = x.astype(BF).astype(F32)
    return hi, x - hi


def unit(x):
    x = x.astype(F32)
    return (x * lax.rsqrt(jnp.mean(x * x, axis=-1, keepdims=True) + EPSILON)).astype(BF)


def spread(acc, coarse, h, rows):
    base = h * 2 * rows
    for off in range(2):
        at = pl.ds(base + off, rows, stride=2)
        for t in range(2):
            acc[t, at, :] += coarse[t]


def put(acc, start, pair):
    for t in range(2):
        acc[t, pl.ds(start, pair.shape[0]), :] = pair[:, t * E : (t + 1) * E]


def kernel(
    q_hbm, k_hbm, v_hbm, scale_hbm, o_ref,
    q_ref, k_ref, scale_ref, qu, kv0, q1, kv1, q2, kv2, q3, out_near, in_near, hop2, hop3, small, ra, rb, rc, rd, re,
    u_own, u_oth, w_own, w_oth,
    acc0, acc1, acc2, acc3, acc4, pw, send, recv, near_recv, pw_send, pw_recv, load,
):
    d = lax.axis_index("seq")
    me = lax.axis_index("head")
    x, z = d // NZ, d % NZ
    s, r = z // 4, z % 4
    g, par = d // 2, d % 2
    left, right = (d + NSEQ - 1) % NSEQ, (d + 1) % NSEQ
    x_with = (x + 2 * s - 1 + NX) % NX
    x_back = (x - (2 * s - 1) + NX) % NX
    x_far = (x + 2) % NX

    def at(row, col):
        return row * NZ + col

    bar = pltpu.get_barrier_semaphore()

    def signal(seq, head):
        pl.semaphore_signal(bar, inc=1, device_id=(seq, head), device_id_type=MESH)

    for i in range(4):
        signal(at(x_back, 4 * s + i), me)
        signal(at(x_with, 4 * s + i), me)
        signal(at(x_far, 4 * s + i), me)
    for j in (4, 3, 5, 2, 6, 1, 7):
        signal(at(x, (z + j) % NZ), me)
    signal(left, me)
    signal(right, me)
    for j in (4, 3, 5, 2, 6, 1, 7):
        signal(d, (me + j) % NHEAD)

    loads = [
        pltpu.make_async_copy(src, dst, load.at[n])
        for n, (src, dst) in enumerate((
            (k_hbm, k_ref), (v_hbm, kv0.at[1, 128:640]), (q_hbm, q_ref), (scale_hbm, scale_ref)
        ))
    ]
    for copy in loads:
        copy.start()

    lanes_of = [slice(h * E, (h + 1) * E) for h in range(HD)]
    loads[0].wait()
    for c in lanes_of:
        kv0[0, 128:640, c] = unit(k_ref[:, c])
    loads[1].wait()

    pools_kv = jnp.concatenate(
        [pool_matrix(((128, 1, 0, 1), (32, 3, 0, 1)), 256)]
        + [detail_matrix(16, 3, c, 256).astype(BF) for c in range(2)]
        + [detail_matrix(32, 2, c, 256).astype(BF) for c in range(2)],
        axis=0,
    )
    finest = detail_matrix(64, 1, 0, 128).astype(BF)
    for half in range(2):
        for t in range(2):
            pooled = dot(pools_kv, kv0[t, half * 256 + 128 : half * 256 + 384, :]).astype(BF)
            kv1[t, 128 + half * 128 : 256 + half * 128, :] = pooled[0:128]
            out_near[t, half * 32 : half * 32 + 32, :] = pooled[128:160]
            out_near[t, 64 + half * 32 : 96 + half * 32, :] = pooled[160:192]
            out_near[t, 128 + half * 64 : 192 + half * 64, :] = pooled[192:256]
            edge = 128 + half * 384
            finest_rows = dot(finest, kv0[t, edge : edge + 128, :]).astype(BF)
            out_near[t, 256 + half * 64 : 320 + half * 64, :] = finest_rows

    pl.semaphore_wait(bar, 28)
    started = []

    def start(src, dst, seq, rsem):
        copy = pltpu.make_async_remote_copy(
            src_ref=src, dst_ref=dst, send_sem=send.at[len(started)], recv_sem=rsem,
            device_id=(seq, me), device_id_type=MESH,
        )
        copy.start()
        started.append(copy)
        return copy

    near = []

    def send_near(n):
        to_left, to_right = ((0, 0), (64, 64), (128, 192), (256, 320))[n]
        into = slice(64 * n, 64 * n + 64)
        near.append((
            start(out_near.at[:, to_right : to_right + 64], in_near.at[0, :, into], right, near_recv.at[n]),
            start(out_near.at[:, to_left : to_left + 64], in_near.at[1, :, into], left, near_recv.at[4 + n]),
        ))

    def wait_both(copies):
        for copy in copies:
            copy.wait_recv()

    send_near(0)

    loads[2].wait()
    for c in lanes_of:
        qu[:, c] = unit(q_ref[:, c])
    small_q = pool_matrix(((32, 4, 0, 1), (16, 5, 0, 1)), ROWS)
    small_k = pool_matrix(((32, 4, 0, 1), (16, 5, 0, 1), (16, 6, 0, 1)), ROWS)

    sq = dot(small_q, qu[...])
    sk = dot(small_k, kv0[0, 128:640, :])
    sv = dot(small_k, kv0[1, 128:640, :])
    for h, c in enumerate(lanes_of):
        small[h, 0:48] = sq[:, c].astype(BF)
        small[h, 48:80] = sk[0:32, c].astype(BF)
        small[h, 80:112] = sv[0:32, c].astype(BF)
        small[h, 112:128] = sk[32:48, c].astype(BF)
        small[h, 128:144] = sv[32:48, c].astype(BF)
        small[h, 144:160] = jnp.concatenate([sk[48:56, c], sv[48:56, c]], axis=0).astype(BF)
    own_copy = pltpu.make_async_copy(small.at[r, 32:112], ra.at[r], recv.at[0])
    own_copy.start()
    for i in range(4):
        start(small.at[i, 48:112], rc.at[r], at(x_with, 4 * s + i), recv.at[2])
        start(small.at[i, 112:144], rd.at[r], at(x_back, 4 * s + i), recv.at[3])
        start(small.at[i, 144:160], re.at[r], at(x_far, 4 * s + i), recv.at[4])
        start(small.at[i, 0:32], rb.at[r], at(x, 4 * (1 - s) + i), recv.at[1])
    for j in range(1, 4):
        i = (r + j) % 4
        start(small.at[i, 32:112], ra.at[r], at(x, 4 * s + i), recv.at[0])
    send_near(1)
    pools_q = pool_matrix(((128, 1, 0, 1), (64, 2, 0, 1), (32, 3, 0, 1)), 256)
    for half in range(2):
        pooled = dot(pools_q, qu[half * 256 : half * 256 + 256, :]).astype(BF)
        q1[half * 128 : half * 128 + 128, :] = pooled[0:128]
        q2[half * 64 : half * 64 + 64, :] = pooled[128:192]
        q3[half * 32 : half * 32 + 32, :] = pooled[192:224]
    loads[3].wait()

    def own_level(heads):
        jobs, places = [], []
        for h in heads:
            c = lanes_of[h]
            for b in range(4):
                keys = slice(128 + max(b - 1, 0) * 128, 128 + min(b + 2, 4) * 128)
                jobs.append((qu[b * 128 : b * 128 + 128, c], kv0[0, keys, c], kv0[1, keys, c], None))
                places.append(h * ROWS + b * 128)
        for place, out in zip(places, attn_all(jobs)):
            put(acc0, place, out)

    own_level((0,))
    own_level((1,))
    wait_both(near[0])
    second = (
        start(in_near.at[0, :, 0:64], hop2.at[0], right, near_recv.at[8]),
        start(in_near.at[1, :, 0:64], hop2.at[1], left, near_recv.at[9]),
    )
    send_near(2)
    own_level((2,))
    own_level((3,))

    for n, ref in enumerate((ra, rb, rc, rd, re)):
        pltpu.make_async_copy(ref, ref, recv.at[n]).wait()
    wrap = jnp.where(s == 1, jnp.where(x == 0, 1.0, 0.0), jnp.where(x == NX - 1, 1.0, 0.0))
    wrap_d = jnp.where(s == 1, jnp.where(x == NX - 1, 1.0, 0.0), jnp.where(x == 0, 1.0, 0.0))
    a, b, c_, d_, e_ = ra[...], rb[...], rc[...], rd[...], re[...]

    def flat(y):
        return y.reshape(y.shape[0] * y.shape[1], E)

    kv_c = jnp.concatenate([flat(c_[:, 0:32]), flat(c_[:, 32:64])], axis=1)
    kv_d = jnp.concatenate([flat(d_[:, 0:16]), flat(d_[:, 16:32])], axis=1)
    k4 = jnp.concatenate([flat(a[:, 16:48]), kv_c[:, 0:E]], axis=0)
    v4 = jnp.concatenate([flat(a[:, 48:80]), kv_c[:, E:]], axis=0)
    q4, q5 = flat(b), flat(a[:, 0:16])
    pooled_c = dot(pool_matrix(((64, 1, 0, 1), (32, 2, 0, 1)), 128), kv_c).astype(BF)
    pooled_d = dot(pool_matrix(((32, 1, 0, 1),), 64), kv_d).astype(BF)
    q_oth = dot(pool_matrix(((128, 1, 0, 2), (128, 2, 0, 4)), 128), q4).astype(BF)
    q6 = dot(pool_matrix(((64, 1, 0, 2),), 64), q5).astype(BF)
    qh = iota((128, 256), 0) // 64
    col = iota((128, 256), 1)
    kh = (col % 128) // 64
    sign = 2 * s - 1
    lead = (kh - qh) * sign
    mask4 = jnp.where(
        col < 128, jnp.where(lead >= 0, 16.0, 0.0), jnp.where(lead <= 0, 16.0 - 16.0 * wrap, 0.0)
    )
    k5 = jnp.concatenate([pooled_c[0:64, 0:E], kv_d[:, 0:E]], axis=0)
    v5 = jnp.concatenate([pooled_c[0:64, E:], kv_d[:, E:]], axis=0)
    far = e_.astype(F32)
    k6 = jnp.concatenate(
        [jnp.concatenate([far[i, 0:8] for i in range(4)], axis=0).astype(BF), pooled_c[64:96, 0:E], pooled_d[:, 0:E]], axis=0
    )
    v6 = jnp.concatenate(
        [jnp.concatenate([far[i, 8:16] for i in range(4)], axis=0).astype(BF), pooled_c[64:96, E:], pooled_d[:, E:]], axis=0
    )
    col6 = iota((128, 96), 1)
    mask6 = 64.0 * jnp.where(col6 < 32, 1.0, jnp.where(col6 < 64, wrap, wrap_d))
    mask5 = 32.0 * jnp.where(iota((64, 128), 1) < 64, 1.0 - wrap, 1.0 - wrap_d)
    outs = attn_all([
        (q4, k4, v4, mask4),
        (q5, k5, v5, mask5),
        (q6, k6, v6, mask6[0:64]),
        (q_oth[0:128], kv_d[:, 0:E], kv_d[:, E:], None),
        (q_oth[128:256], k6, v6, mask6),
    ])
    out_own = outs[1] + outs[2]
    out_oth = outs[0] + 32.0 * (1.0 - wrap_d) * outs[3] + outs[4]

    lane = iota((16, E), 1)

    def den_tile(pieces):
        tile = jnp.zeros((16, E), F32)
        for n, piece in enumerate(pieces):
            hi, lo = split(piece)
            tile = jnp.where((lane >= 32 * n) & (lane < 32 * n + 16), hi, tile)
            tile = jnp.where((lane >= 32 * n + 16) & (lane < 32 * n + 32), lo, tile)
        return tile.astype(BF)

    for i in range(4):
        mine = out_own[i * 16 : i * 16 + 16]
        u_own[i, 0:16] = mine[:, 0:E].astype(BF)
        u_own[i, 16:32] = den_tile([mine[:, E:]])
        other = out_oth[i * 32 : i * 32 + 32]
        u_oth[i, 0:32] = other[:, 0:E].astype(BF)
        u_oth[i, 32:48] = den_tile([other[0:16, E:], other[16:32, E:]])
    own_return = pltpu.make_async_copy(u_own.at[r], w_own.at[r], recv.at[7])
    own_return.start()
    for j in range(1, 4):
        i = (r + j) % 4
        start(u_own.at[i], w_own.at[r], at(x, 4 * s + i), recv.at[7])
    for i in range(4):
        start(u_oth.at[i], w_oth.at[r], at(x, 4 * (1 - s) + i), recv.at[8])

    before_on = jnp.where(d >= 1, 1.0, 0.0)
    after_on = jnp.where(d <= NSEQ - 2, 1.0, 0.0)
    pair_before_on = jnp.where(g >= 1, 1.0, 0.0)
    pair_after_on = jnp.where(g <= NSEQ // 2 - 2, 1.0, 0.0)
    wait_both(second)
    third = start(hop2.at[par], hop3, 2 * g + 1 - par, near_recv.at[10])
    send_near(3)

    def rows_of(side, t, n, chunk, rows):
        return in_near[side, t, 64 * n + rows * chunk : 64 * n + rows * chunk + rows, :].astype(F32)

    wait_both(near[1])
    for side in range(2):
        for t in range(2):
            for chunk in range(4):
                coarse = rebuild(rows_of(side, t, 0, chunk, 16), rows_of(side, t, 1, chunk, 16))
                at_row = 256 * side + 32 * chunk
                kv2[t, at_row : at_row + 32, :] = coarse.astype(BF)

    def pair_rows(kv, t, first, second, c):
        return jnp.concatenate([kv[t, first : first + 128, c], kv[t, second : second + 128, c]], axis=0)

    mask2 = 4.0 * half_mask(128, before_on, after_on)
    outs = attn_all([
        (q2[:, c], pair_rows(kv2, 0, 0, 256, c), pair_rows(kv2, 1, 0, 256, c), mask2) for c in lanes_of
    ])
    for h, out in enumerate(outs):
        put(acc2, h * 128, out)

    def middle(side, t, n):
        chunk = n + (2 if side == 0 else 0)
        coarse = rebuild(rows_of(side, t, 0, chunk, 16), rows_of(side, t, 1, chunk, 16))
        return rebuild(coarse, rows_of(side, t, 2, n, 32))

    wait_both(near[2])
    for side in range(2):
        for t in range(2):
            for n in range(2):
                at_row = 384 * side + 64 * n
                kv1[t, at_row : at_row + 64, :] = middle(side, t, n).astype(BF)

    masks1 = (2.0 * half_mask(128, before_on, 1.0), 2.0 * half_mask(128, 1.0, after_on))
    for b, mask1 in enumerate(masks1):
        lo, hi = b * 128, 256 + b * 128
        outs = attn_all([
            (q1[lo : lo + 128, c], pair_rows(kv1, 0, lo, hi, c), pair_rows(kv1, 1, lo, hi, c), mask1) for c in lanes_of
        ])
        for h, out in enumerate(outs):
            put(acc1, h * 256 + b * 128, out)

    third.wait_recv()
    col192 = iota((64, 192), 1)
    last_on = jnp.where(par == 0, pair_after_on, pair_before_on)
    mask3 = 8.0 * jnp.where(col192 < 64, pair_before_on, jnp.where(col192 < 128, pair_after_on, last_on))

    outs = attn_all([
        (q3[:, c],)
        + tuple(jnp.concatenate([hop2[0, n, :, c], hop2[1, n, :, c], hop3[n, :, c]], axis=0) for n in range(2))
        + (mask3,)
        for c in lanes_of
    ])
    for h, out in enumerate(outs):
        put(acc3, h * 64, out)

    pltpu.make_async_copy(w_own, w_own, recv.at[7]).wait()
    pltpu.make_async_copy(w_oth, w_oth, recv.at[8]).wait()

    def den_of(tile, lo, hi, rows):
        return jnp.broadcast_to(tile[:, lo : lo + 1] + tile[:, hi : hi + 1], (rows, E))

    for h in range(HD):
        own, oth = w_own[h].astype(F32), w_oth[h].astype(F32)
        acc4[0, h * 32 : h * 32 + 32, :] = oth[0:32]
        acc4[1, h * 32 : h * 32 + 16, :] = den_of(oth[32:48], 0, 16, 16)
        acc4[1, h * 32 + 16 : h * 32 + 32, :] = den_of(oth[32:48], 32, 48, 16)
        spread(acc4, (own[0:16], den_of(own[16:32], 0, 16, 16)), h, 16)
        for acc, finer, n in ((acc4, acc3, 32), (acc3, acc2, 64), (acc2, acc1, 128), (acc1, acc0, 256)):
            spread(finer, tuple(acc[t, h * n : h * n + n, :] for t in range(2)), h, n)

    power = []

    def share_power(part, starts):
        for n, first in enumerate(starts):
            squares = jnp.zeros((128, E), F32)
            for h in range(HD):
                rows = slice(h * ROWS + first, h * ROWS + first + 128)
                scaled = acc0[0, rows, :] / acc0[1, rows, :] * scale_ref[h]
                acc0[0, rows, :] = scaled
                squares = squares + scaled * scaled
            pw[part, me, :, n * 128 : n * 128 + 128] = jnp.sum(squares.T, axis=0, keepdims=True)
        for j in (4, 3, 5, 2, 6, 1, 7):
            copy = pltpu.make_async_remote_copy(
                src_ref=pw.at[part, me], dst_ref=pw.at[part, me],
                send_sem=pw_send.at[part, j], recv_sem=pw_recv.at[part, me],
                device_id=(d, (me + j) % NHEAD), device_id_type=MESH,
            )
            copy.start()
            power.append(copy)

    def write_out(part, starts):
        for j in range(1, 8):
            peer = (me + j) % NHEAD
            pltpu.make_async_remote_copy(
                src_ref=pw.at[part, peer], dst_ref=pw.at[part, peer],
                send_sem=pw_send.at[part, j], recv_sem=pw_recv.at[part, peer],
                device_id=(d, peer), device_id_type=MESH,
            ).wait_recv()
        total = jnp.sum(pw[part], axis=0)
        factor = lax.rsqrt(total / (NHEAD * WIDTH) + EPSILON)
        for n, first in enumerate(starts):
            column = jnp.broadcast_to(factor[:, n * 128 : n * 128 + 128], (128, 128)).T
            for h, c in enumerate(lanes_of):
                scaled = acc0[0, h * ROWS + first : h * ROWS + first + 128, :]
                o_ref[first : first + 128, c] = (scaled * column).astype(BF)

    share_power(0, (128, 256))

    wait_both(near[3])
    for side in range(2):
        for t in range(2):
            fine = rebuild(middle(side, t, 1 - side), in_near[side, t, 192:256, :].astype(F32))
            kv0[t, 640 * side : 640 * side + 128, :] = fine.astype(BF)

    ends = ((0, 0, before_on), (384, 640, after_on))
    outs = attn_all([
        (qu[first : first + 128, c], kv0[0, key : key + 128, c], kv0[1, key : key + 128, c], None)
        for c in lanes_of
        for first, key, on in ends
    ])
    for n, out in enumerate(outs):
        first, key, on = ends[n % 2]
        for t in range(2):
            acc0[t, pl.ds(n // 2 * ROWS + first, 128), :] += on * out[:, t * E : (t + 1) * E]
    share_power(1, (0, 384))
    write_out(0, (128, 256))
    write_out(1, (0, 384))
    for copy in started:
        copy.wait_send()
    for copy in power:
        copy.wait_send()


def on_device(queries, key_inputs, value_inputs, head_scale, out_gain):
    vmem = pl.BlockSpec(memory_space=pltpu.VMEM)
    hbm = pl.BlockSpec(memory_space=pltpu.HBM)
    normed = pl.pallas_call(
        kernel,
        out_shape=jax.ShapeDtypeStruct((ROWS, WIDTH), BF),
        in_specs=[hbm] * 4,
        out_specs=vmem,
        scratch_shapes=[
            pltpu.VMEM((512, WIDTH), BF),
            pltpu.VMEM((512, WIDTH), BF),
            pltpu.SMEM((HD,), F32),
            pltpu.VMEM((512, WIDTH), BF),
            pltpu.VMEM((2, 768, WIDTH), BF),
            pltpu.VMEM((256, WIDTH), BF),
            pltpu.VMEM((2, 512, WIDTH), BF),
            pltpu.VMEM((128, WIDTH), BF),
            pltpu.VMEM((2, 384, WIDTH), BF),
            pltpu.VMEM((64, WIDTH), BF),
            pltpu.VMEM((2, 384, WIDTH), BF),
            pltpu.VMEM((2, 2, 256, WIDTH), BF),
            pltpu.VMEM((2, 2, 64, WIDTH), BF),
            pltpu.VMEM((2, 64, WIDTH), BF),
            pltpu.VMEM((4, 160, E), BF),
            pltpu.VMEM((4, 80, E), BF),
            pltpu.VMEM((4, 32, E), BF),
            pltpu.VMEM((4, 64, E), BF),
            pltpu.VMEM((4, 32, E), BF),
            pltpu.VMEM((4, 16, E), BF),
            pltpu.VMEM((4, 32, E), BF),
            pltpu.VMEM((4, 48, E), BF),
            pltpu.VMEM((4, 32, E), BF),
            pltpu.VMEM((4, 48, E), BF),
            pltpu.VMEM((2, HD * 512, E), F32),
            pltpu.VMEM((2, HD * 256, E), F32),
            pltpu.VMEM((2, HD * 128, E), F32),
            pltpu.VMEM((2, HD * 64, E), F32),
            pltpu.VMEM((2, HD * 32, E), F32),
            pltpu.VMEM((2, NHEAD, 1, ROWS // 2), F32),
            pltpu.SemaphoreType.DMA((40,)),
            pltpu.SemaphoreType.DMA((10,)),
            pltpu.SemaphoreType.DMA((11,)),
            pltpu.SemaphoreType.DMA((2, 8)),
            pltpu.SemaphoreType.DMA((2, 8)),
            pltpu.SemaphoreType.DMA((5,)),
        ],
        compiler_params=pltpu.CompilerParams(
            collective_id=0, has_side_effects=True, vmem_limit_bytes=int(53.25 * 2**20)
        ),
    )(queries, key_inputs, value_inputs, head_scale)
    return (normed.astype(F32) * out_gain[None, :]).astype(BF)


def solution(mesh):
    placed = (P("seq", "head"), P("seq", "head"), P("seq", "head"), P("head"), P("head"))
    return jax.shard_map(
        on_device, mesh=mesh, in_specs=placed, out_specs=P("seq", "head"), check_vma=False
    )
```
